32 devices in a mesh: clip: 8 (over z, x), frame: 4 (over y, core).
Axes of the slice: x: 2, y: 2, z: 4, core: 2. Of those that a mesh axis runs over, the one named last changes fastest.
Arguments:
- media: bfloat16 [16, 4, 256, 1536], P('clip', 'frame'), may hold values from -6 to 6
- frame_order: int32 [16, 4], P('clip'), may hold values from 0 to 3, each once within a row
- clip_counts: int32 [4], replicated, may hold values from 1 to 4, as said below
- latents: float32 [16, 64, 1536], P('clip'), may hold values from -6 to 6
- time_embed: float32 [4, 1536], replicated, may hold values from -6 to 6
- media_gain: float32 [2, 1536], replicated, may hold values from 0.25 to 1.75
- latent_gain: float32 [2, 1536], replicated, may hold values from 0.25 to 1.75
- ffn_gain: float32 [2, 1536], replicated, may hold values from 0.25 to 1.75
- query_weight: bfloat16 [2, 1536, 1536], P(None, None, 'frame'), may hold values from -0.15625 to 0.15625
- key_weight: bfloat16 [2, 1536, 1536], P(None, None, 'frame'), may hold values from -0.15625 to 0.15625
- value_weight: bfloat16 [2, 1536, 1536], P(None, None, 'frame'), may hold values from -0.15625 to 0.15625
- out_weight: bfloat16 [2, 1536, 1536], P(None, 'frame'), may hold values from -2.5 to 2.5
- up_weight: bfloat16 [2, 1536, 6144], P(None, None, 'frame'), may hold values from -0.15625 to 0.15625
- down_weight: bfloat16 [2, 6144, 1536], P(None, 'frame'), may hold values from -0.078125 to 0.078125
- cotangent: float32 [16, 64, 1536], P('clip'), may hold values from -6 to 6
Outputs:
- latents_out: float32 [16, 64, 1536], P('clip')
- media_grad: float32 [16, 4, 256, 1536], P('clip', 'frame')
- latents_grad: float32 [16, 64, 1536], P('clip')
- time_grad: float32 [4, 1536], P(None, ('clip', 'frame'))
- media_gain_grad: float32 [2, 1536], P(None, ('clip', 'frame'))
- latent_gain_grad: float32 [2, 1536], P(None, 'clip')
- ffn_gain_grad: float32 [2, 1536], P(None, 'clip')
- query_weight_grad: float32 [2, 1536, 1536], P(None, 'clip', 'frame')
- key_weight_grad: float32 [2, 1536, 1536], P(None, 'clip', 'frame')
- value_weight_grad: float32 [2, 1536, 1536], P(None, 'clip', 'frame')
- out_weight_grad: float32 [2, 1536, 1536], P(None, 'frame', 'clip')
- up_weight_grad: float32 [2, 1536, 6144], P(None, 'clip', 'frame')
- down_weight_grad: float32 [2, 6144, 1536], P(None, 'frame', 'clip')
The draws below stay inside these ranges and needn't reach their ends.
Inputs may be any that keep to these rules, and one draw needn't show every extreme that they name: `clip_counts`: every sequence has at least one live clip, and some sequence fills all 4 slots. `frame_order`: each clip's row is a permutation of the 4 time positions.
All inputs are finite; a program needn't handle non-finite values.
Results may differ from the reference program's by a relative error of at most 0.028.
Values may be sent and summed in bfloat16 or wider, within the bound.
No kernel may reach another device: no remote copies, remote signals or barrier semaphores. Data moves between devices by JAX's collectives and lax.ppermute only.
A program may use at most 256 MiB of HBM per device.

```python
import jax
import jax.numpy as jnp
from jax import lax

D = 1536
HEADS = 16
HEAD_DIM = 96
FF = 6144
LATENTS = 64
PATCHES = 256
LAYERS = 2
SLOTS = 4
FRAMES = 4
CLIPS = 16
SEQS = 4


def draw_clip_counts(key, part):
    key = jax.random.fold_in(key, 7)
    first_key, second_key = jax.random.split(key)
    counts_drawn = jax.random.randint(first_key, (SEQS,), 1, SLOTS + 1)
    full_seq = jax.random.randint(second_key, (), 0, SEQS)
    return jnp.where(jnp.arange(SEQS) == full_seq, SLOTS, counts_drawn).astype(jnp.int32)


def level_of(own_key, dims, pieces, smallest, largest):
    gain = 1.0
    for dim, blocks in pieces:
        heights = jax.random.uniform(jax.random.fold_in(jax.random.fold_in(own_key, 6), dim), (blocks,), jnp.float32, smallest / len(pieces), largest / len(pieces))
        gain = gain * jnp.repeat(jnp.exp(heights), dims[dim] // blocks).reshape((-1,) + (1,) * (len(dims) - 1 - dim))
    return gain


def bell_draw(key, shape, width, most, cuts=(), kind=jnp.bfloat16):
    entries = width * jax.random.normal(key, shape, jnp.float32)
    if cuts:
        entries = entries * level_of(key, shape, cuts, -0.22, 0.18)
    return jnp.clip(entries, -most, most).astype(kind)


def setup_inputs(seed: int = 0) -> dict:
    arg_keys = jax.random.split(jax.random.key(seed), 16)
    return {
        "media": bell_draw(arg_keys[0], (CLIPS, FRAMES, PATCHES, D), 1.0, 6.0, ((0, 8), (1, 4))),
        "frame_order": jax.vmap(lambda own: jax.random.permutation(own, FRAMES))(jax.random.split(arg_keys[1], CLIPS)).reshape((CLIPS, FRAMES)).astype(jnp.int32),
        "clip_counts": draw_clip_counts(jax.random.fold_in(arg_keys[15], 71), 0),
        "latents": bell_draw(arg_keys[3], (CLIPS, LATENTS, D), 1.0, 6.0, ((0, 8),), jnp.float32),
        "time_embed": bell_draw(arg_keys[4], (FRAMES, D), 1.0, 6.0, (), jnp.float32),
        "media_gain": jnp.clip(1.0 + 0.15 * jax.random.normal(arg_keys[5], (LAYERS, D), jnp.float32), 0.25, 1.75),
        "latent_gain": jnp.clip(1.0 + 0.15 * jax.random.normal(arg_keys[6], (LAYERS, D), jnp.float32), 0.25, 1.75),
        "ffn_gain": jnp.clip(1.0 + 0.15 * jax.random.normal(arg_keys[7], (LAYERS, D), jnp.float32), 0.25, 1.75),
        "query_weight": bell_draw(arg_keys[8], (LAYERS, D, D), D ** -0.5, 0.15625, ((2, 4),)),
        "key_weight": bell_draw(arg_keys[9], (LAYERS, D, D), D ** -0.5, 0.15625, ((2, 4),)),
        "value_weight": bell_draw(arg_keys[10], (LAYERS, D, D), D ** -0.5, 0.15625, ((2, 4),)),
        "out_weight": bell_draw(arg_keys[11], (LAYERS, D, D), (max(1, 4 * D // (FRAMES * PATCHES))) ** -0.5, 2.5, ((1, 4),)),
        "up_weight": bell_draw(arg_keys[12], (LAYERS, D, FF), D ** -0.5, 0.15625, ((2, 4),)),
        "down_weight": bell_draw(arg_keys[13], (LAYERS, FF, D), FF ** -0.5, 0.078125, ((1, 4),)),
        "cotangent": bell_draw(arg_keys[14], (CLIPS, LATENTS, D), 1.0, 6.0, ((0, 8),), jnp.float32),
    }


EPSILON = 1e-05
HIGHEST = lax.Precision.HIGHEST

@jax.custom_vjp
def low(v):
    return lax.optimization_barrier(v.astype(jnp.bfloat16)).astype(jnp.float32)

@jax.custom_vjp
def low_back(v):
    return v

def low_keep(v):
    return (low(v), None)

def low_pass(kept, grad):
    return (grad,)

def back_keep(v):
    return (v, None)

def back_low(kept, grad):
    return (low(grad),)
low.defvjp(low_keep, low_pass)
low_back.defvjp(back_keep, back_low)

def norm_rows(values_in, gain_row):
    row_mean = lax.optimization_barrier(jnp.mean(values_in, axis=-1, keepdims=True))
    centred = values_in - row_mean
    variance = lax.optimization_barrier(jnp.mean(centred * centred, axis=-1, keepdims=True))
    return centred * lax.rsqrt(variance + EPSILON) * gain_row

def both_ways(values_in):
    return low_back(low(values_in))

def resampler_clip(weights, gains, time_embed, media_clip, latent_rows, order_row, living):
    query_w, key_w, value_w, out_w, up_w, down_w = weights
    media_g, latent_g, ffn_g = gains
    onehot = (order_row[:, None] == jnp.arange(FRAMES)[None, :]).astype(jnp.float32)
    stamped = media_clip + jnp.dot(onehot, time_embed, precision=HIGHEST)[:, None, :]
    stamped = stamped.reshape(FRAMES * PATCHES, D)
    scaling = HEAD_DIM ** (-0.5)
    current = latent_rows
    for layer_no in range(LAYERS):
        media_n = low(norm_rows(stamped, media_g[layer_no]))
        latent_n = low(norm_rows(current, latent_g[layer_no]))
        sources = jnp.concatenate([media_n, latent_n], axis=0)
        queries = both_ways(jnp.dot(latent_n, query_w[layer_no], precision=HIGHEST)).reshape(LATENTS, HEADS, HEAD_DIM)
        keys_all = both_ways(jnp.dot(sources, key_w[layer_no], precision=HIGHEST)).reshape(-1, HEADS, HEAD_DIM)
        values_all = both_ways(jnp.dot(sources, value_w[layer_no], precision=HIGHEST)).reshape(-1, HEADS, HEAD_DIM)
        scores = low_back(jnp.einsum('qhd,khd->hqk', queries, keys_all, precision=HIGHEST) * scaling)
        soft_weights = low(jax.nn.softmax(scores, axis=-1))
        attended = jnp.einsum('hqk,khd->qhd', soft_weights, values_all, precision=HIGHEST).reshape(LATENTS, D)
        attended = both_ways(attended)
        middle = current + low_back(jnp.dot(attended, out_w[layer_no], precision=HIGHEST))
        ffn_in = low(norm_rows(middle, ffn_g[layer_no]))
        pre_act = low_back(jnp.dot(ffn_in, up_w[layer_no], precision=HIGHEST))
        hidden = low(jax.nn.gelu(pre_act, approximate=False))
        current = middle + low_back(jnp.dot(hidden, down_w[layer_no], precision=HIGHEST))
    return current * living

def reference(media, frame_order, clip_counts, latents, time_embed, media_gain, latent_gain, ffn_gain, query_weight, key_weight, value_weight, out_weight, up_weight, down_weight, cotangent):
    weights = (query_weight.astype(jnp.float32), key_weight.astype(jnp.float32), value_weight.astype(jnp.float32), out_weight.astype(jnp.float32), up_weight.astype(jnp.float32), down_weight.astype(jnp.float32))
    gains = (media_gain, latent_gain, ffn_gain)
    clip_index = jnp.arange(CLIPS)
    owner_count = jnp.take(clip_counts, clip_index // SLOTS)
    living_all = (clip_index % SLOTS < owner_count).astype(jnp.float32)

    def one_clip(totals, inputs):
        media_clip, order_row, latent_rows, cot_rows, living = inputs

        def forward(weights_f, gains_f, time_f, media_f, latent_f):
            return resampler_clip(weights_f, gains_f, time_f, media_f, latent_f, order_row, living)
        result, pullback = jax.vjp(forward, weights, gains, time_embed, media_clip.astype(jnp.float32), latent_rows)
        grad_w, grad_g, grad_t, grad_m, grad_l = pullback(cot_rows)
        totals = jax.tree.map(lambda left_sum, right_sum: left_sum + right_sum, totals, (grad_w, grad_g, grad_t))
        return (totals, (result, grad_m, grad_l))
    zero_init = jax.tree.map(jnp.zeros_like, (weights, gains, time_embed))
    totals, outputs = lax.scan(one_clip, zero_init, (media, frame_order, latents, cotangent, living_all))
    latents_out, media_grad, latents_grad = outputs
    grad_w, grad_g, grad_t = totals
    return (latents_out, media_grad, latents_grad, grad_t, grad_g[0], grad_g[1], grad_g[2], grad_w[0], grad_w[1], grad_w[2], grad_w[3], grad_w[4], grad_w[5])
```

```python
import jax
import jax.numpy as jnp
from jax import lax
from jax.sharding import PartitionSpec as P

HEAD_DIM = 96
SLOTS = 4
LAYERS = 2
EPSILON = 1e-05
SCALING = HEAD_DIM ** (-0.5)
f32 = jnp.float32
bf16 = jnp.bfloat16


def norm_plain(v):
    mean = jnp.mean(v, axis=-1, keepdims=True)
    centred = v - mean
    inverse = lax.rsqrt(jnp.mean(centred * centred, axis=-1, keepdims=True) + EPSILON)
    return centred * inverse, inverse


def norm_back(u, normed, inverse):
    return inverse * (
        u
        - jnp.mean(u, axis=-1, keepdims=True)
        - normed * jnp.mean(u * normed, axis=-1, keepdims=True)
    )


def dot(a, b):
    return jnp.dot(a, b, preferred_element_type=f32)


def dot_nt(a, b):
    return lax.dot_general(a, b, (((1,), (1,)), ((), ())), preferred_element_type=f32)


def dot_tn(a, b):
    return lax.dot_general(a, b, (((0,), (0,)), ((), ())), preferred_element_type=f32)


def swap(v, axis, bit):
    size = lax.axis_size(axis)
    return lax.ppermute(v, axis, [(i, i ^ bit) for i in range(size)])


def bits_of(size):
    out, bit = [], 1
    while bit < size:
        out.append(bit)
        bit *= 2
    return out


def frame_sum(part, core):
    keep = lax.dynamic_index_in_dim(part, core, 0, keepdims=False)
    send = lax.dynamic_index_in_dim(part, 1 - core, 0, keepdims=False).astype(bf16)
    total = keep.astype(bf16).astype(f32) + swap(send, "frame", 1).astype(f32)
    for bit in bits_of(lax.axis_size("frame"))[1:]:
        mine = total.astype(bf16)
        total = mine.astype(f32) + swap(mine, "frame", bit).astype(f32)
    mine = total.astype(bf16)
    other = swap(mine, "frame", 1)
    first = jnp.where(core == 0, mine, other)
    second = jnp.where(core == 0, other, mine)
    return jnp.concatenate([first, second], axis=0).astype(f32)


def gather_rows(rows, frame_here):
    count = rows.shape[0] // lax.axis_size("frame")
    have = lax.dynamic_slice_in_dim(rows, frame_here * count, count, 0)
    for bit in bits_of(lax.axis_size("clip")):
        have = jnp.concatenate([have, swap(have, "clip", bit)], axis=0)
    for bit in bits_of(lax.axis_size("frame"))[::-1]:
        have = jnp.concatenate([have, swap(have, "frame", bit)], axis=0)
    return have


def scatter_rows(part, clip_here):
    total = part
    for bit in bits_of(lax.axis_size("clip")):
        mine = (clip_here // bit) % 2
        rows, width = total.shape
        blocks = lax.axis_size("clip") // bit
        halves = total.reshape(blocks // 2, 2, rows // blocks, width)
        keep = lax.dynamic_index_in_dim(halves, mine, 1, keepdims=False)
        send = lax.dynamic_index_in_dim(halves, 1 - mine, 1, keepdims=False).astype(bf16)
        total = keep.astype(f32) + swap(send, "clip", bit).astype(f32)
        total = total.reshape(rows // 2, width)
    return total


def gelu_parts(x):
    half = 0.5 * (1.0 + lax.erf(x * (0.5**0.5)))
    return x * half, half + x * jnp.exp(-0.5 * x * x) * (0.5 / jnp.pi) ** 0.5


def on_device(
    media, frame_order, clip_counts, latents, time_embed, media_gain, latent_gain, ffn_gain,
    query_weight, key_weight, value_weight, out_weight, up_weight, down_weight, cotangent,
):
    clips, _, patches, width = media.shape
    lat_rows = latents.shape[1]
    nf = lax.axis_size("frame")
    nc = lax.axis_size("clip")
    frame_here = lax.axis_index("frame")
    clip_here = lax.axis_index("clip")
    core = frame_here % 2
    own = query_weight.shape[2]
    heads = own // HEAD_DIM
    rows = clips * lat_rows

    clip_ids = clip_here * clips + jnp.arange(clips, dtype=jnp.int32)
    owner_match = (clip_ids // SLOTS)[:, None] == jnp.arange(clip_counts.shape[0], dtype=jnp.int32)[None, :]
    owner_count = jnp.sum(jnp.where(owner_match, clip_counts[None, :], 0), axis=1)
    living = (clip_ids % SLOTS < owner_count).astype(f32)
    living = jnp.repeat(living, lat_rows)[:, None]

    frames = [media[:, 0]]
    for bit in bits_of(nf)[::-1]:
        got = [swap(m, "frame", bit) for m in frames]
        frames = frames + got
    rel = [0]
    for bit in bits_of(nf)[::-1]:
        rel = rel + [r ^ bit for r in rel]
    frames = [frames[rel.index(r)] for r in range(nf)]

    times = jnp.arange(nf, dtype=jnp.int32)
    plain_b, plain0, inv0, onehot0 = [], None, None, None
    for r in range(nf):
        order = lax.dynamic_index_in_dim(frame_order, frame_here ^ r, 1, keepdims=False)
        onehot = (order[:, None] == times[None, :]).astype(f32)
        stamp = jnp.dot(onehot, time_embed, precision=lax.Precision.HIGHEST)
        plain, inv = norm_plain(frames[r].astype(f32) + stamp[:, None, :])
        if r == 0:
            plain0, inv0, onehot0 = plain, inv, onehot
        plain_b.append(plain.astype(bf16).reshape(clips * patches, width))

    wide = jnp.concatenate(
        [
            (media_gain[l][:, None] * w[l].astype(f32)).astype(bf16)
            for l in range(LAYERS)
            for w in (key_weight, value_weight)
        ],
        axis=1,
    )
    kv_media = [dot(p, wide).astype(bf16).reshape(clips, patches, -1) for p in plain_b]

    head_of = jnp.arange(own, dtype=jnp.int32) // HEAD_DIM
    mask = (head_of[None, :] == jnp.arange(heads, dtype=jnp.int32)[:, None]).astype(bf16)

    def spread(v):
        return (v[:, None] * mask[None, :, None, :]).reshape(clips, heads * lat_rows, own)

    def gathered(v):
        v = v.reshape(clips, heads, lat_rows, own) * mask[None, :, None, :].astype(f32)
        return jnp.sum(v, axis=1)

    stored = []
    current = latents.reshape(rows, width)
    for l in range(LAYERS):
        lat_plain, lat_inv = norm_plain(current)
        lat_n = (lat_plain * latent_gain[l]).astype(bf16)
        q = dot(lat_n, query_weight[l]).astype(bf16)
        kl = dot(lat_n, key_weight[l]).astype(bf16).reshape(clips, lat_rows, own)
        vl = dot(lat_n, value_weight[l]).astype(bf16).reshape(clips, lat_rows, own)
        keys = jnp.concatenate([kv[:, :, 2 * l * own : (2 * l + 1) * own] for kv in kv_media] + [kl], axis=1)
        values = jnp.concatenate([kv[:, :, (2 * l + 1) * own : (2 * l + 2) * own] for kv in kv_media] + [vl], axis=1)
        qs = spread(q.reshape(clips, lat_rows, own))
        scores = jnp.einsum("cqd,ckd->cqk", qs, keys, preferred_element_type=f32) * SCALING
        top = jnp.max(scores, axis=-1, keepdims=True)
        ex = jnp.exp(scores - top)
        soft = (ex / jnp.sum(ex, axis=-1, keepdims=True)).astype(bf16)
        att = gathered(jnp.einsum("cqk,ckd->cqd", soft, values, preferred_element_type=f32))
        att = att.reshape(rows, own).astype(bf16)
        middle = current + frame_sum(dot(att, out_weight[l]).reshape(2, rows // 2, width), core)
        ffn_plain, ffn_inv = norm_plain(middle)
        ffn_in = (ffn_plain * ffn_gain[l]).astype(bf16)
        hidden, slope = gelu_parts(dot(ffn_in, up_weight[l]))
        current = middle + frame_sum(
            dot(hidden.astype(bf16), down_weight[l]).reshape(2, rows // 2, width), core
        )
        stored.append((lat_plain, lat_inv, lat_n, qs, keys, values, soft, att, ffn_plain, ffn_inv, ffn_in, slope))
    latents_out = current * living

    grad = cotangent.reshape(rows, width) * living
    proj_grads, up_grads, down_grads = [None] * LAYERS, [None] * LAYERS, [None] * LAYERS
    lat_gain_grads, ffn_gain_grads, media_gain_grads = [None] * LAYERS, [None] * LAYERS, [None] * LAYERS
    gkv = [None] * LAYERS
    for l in reversed(range(LAYERS)):
        lat_plain, lat_inv, lat_n, qs, keys, values, soft, att, ffn_plain, ffn_inv, ffn_in, slope = stored[l]
        gy = grad.astype(bf16)
        gpre = (slope * dot_nt(gy, down_weight[l])).astype(bf16)
        gffn = frame_sum(dot_nt(gpre, up_weight[l]).reshape(2, rows // 2, width), core)
        ffn_gain_grads[l] = jnp.sum(gffn * ffn_plain, axis=0)
        gmid = grad + norm_back(gffn * ffn_gain[l], ffn_plain, ffn_inv)
        gupd = gmid.astype(bf16)
        gatt = dot_nt(gupd, out_weight[l]).astype(bf16).reshape(clips, lat_rows, own)
        gatts = spread(gatt)
        gsoft = jnp.einsum("cqd,ckd->cqk", gatts, values, preferred_element_type=f32)
        soft32 = soft.astype(f32)
        delta = jnp.sum(soft32 * gsoft, axis=-1, keepdims=True)
        gscore = (soft32 * (gsoft - delta)).astype(bf16)
        gq = (gathered(jnp.einsum("cqk,ckd->cqd", gscore, keys, preferred_element_type=f32)) * SCALING).astype(bf16).reshape(rows, own)
        gk = (jnp.einsum("cqk,cqd->ckd", gscore, qs, preferred_element_type=f32) * SCALING).astype(bf16)
        gv = jnp.einsum("cqk,cqd->ckd", soft, gatts, preferred_element_type=f32).astype(bf16)
        gkl = gk[:, nf * patches :].reshape(rows, own)
        gvl = gv[:, nf * patches :].reshape(rows, own)
        glat = frame_sum(
            (dot_nt(gq, query_weight[l]) + dot_nt(gkl, key_weight[l]) + dot_nt(gvl, value_weight[l])).reshape(2, rows // 2, width), core
        )
        lat_gain_grads[l] = jnp.sum(glat * lat_plain, axis=0)
        grad = gmid + norm_back(glat * latent_gain[l], lat_plain, lat_inv)

        fa = gather_rows(ffn_in, frame_here)
        ga = gather_rows(gy, frame_here)
        hid_a, slope_a = gelu_parts(dot(fa, up_weight[l]))
        gpre_a = (slope_a * dot_nt(ga, down_weight[l])).astype(bf16)
        cols = width // nc
        fs = lax.dynamic_slice_in_dim(fa, clip_here * cols, cols, 1)
        gs = lax.dynamic_slice_in_dim(ga, clip_here * cols, cols, 1)
        up_grads[l] = dot_tn(fs, gpre_a)
        down_grads[l] = dot_tn(hid_a.astype(bf16), gs)

        gkm = [gk[:, r * patches : (r + 1) * patches].reshape(clips * patches, own) for r in range(nf)]
        gvm = [gv[:, r * patches : (r + 1) * patches].reshape(clips * patches, own) for r in range(nf)]
        kraw = sum(dot_tn(plain_b[r], gkm[r]) for r in range(nf))
        vraw = sum(dot_tn(plain_b[r], gvm[r]) for r in range(nf))
        media_gain_grads[l] = jnp.sum(kraw * key_weight[l].astype(f32) + vraw * value_weight[l].astype(f32), axis=1)
        kg = kraw * media_gain[l][:, None] + dot_tn(lat_n, gkl)
        vg = vraw * media_gain[l][:, None] + dot_tn(lat_n, gvl)
        qg = dot_tn(lat_n, gq)
        og = dot_tn(gupd, att)
        proj_grads[l] = scatter_rows(jnp.concatenate([qg, kg, vg, og], axis=1), clip_here)
        gkv[l] = (gkm, gvm)

    u = [
        dot_nt(jnp.concatenate([g for l in range(LAYERS) for g in (gkv[l][0][r], gkv[l][1][r])], axis=1), wide)
        for r in range(nf)
    ]
    for bit in bits_of(nf):
        step = [r for r in range(nf) if u[r] is not None and r & bit]
        for r in step:
            u[r ^ bit] = u[r ^ bit] + swap(u[r].astype(bf16), "frame", bit).astype(f32)
            u[r] = None
    media_grad = norm_back(u[0].reshape(clips, patches, width), plain0, inv0)
    time_part = jnp.dot(onehot0.T, jnp.sum(media_grad, axis=1), precision=lax.Precision.HIGHEST)

    n_all = nc * nf
    narrow = jnp.concatenate([time_part, jnp.stack(media_gain_grads)], axis=0)
    narrow = narrow.reshape(nf + 2, n_all, width // n_all).transpose(1, 0, 2).reshape(n_all, -1)
    broad = jnp.concatenate([jnp.stack(lat_gain_grads), jnp.stack(ffn_gain_grads)], axis=0)
    broad = broad.reshape(4, nc, width // nc).transpose(1, 0, 2).reshape(nc, 1, -1)
    broad = broad * (jnp.arange(nf) == frame_here).astype(f32)[None, :, None]
    packed = jnp.concatenate([narrow, broad.reshape(n_all, -1)], axis=1)
    packed = jnp.sum(lax.all_to_all(packed, ("clip", "frame"), 0, 0, tiled=True), axis=0)
    cut = (nf + 2) * (width // n_all)
    narrow = packed[:cut].reshape(nf + 2, -1)
    broad = packed[cut:].reshape(4, -1)

    proj = jnp.stack(proj_grads)
    return (
        latents_out.reshape(latents.shape),
        media_grad[:, None],
        grad.reshape(latents.shape),
        narrow[:nf],
        narrow[nf:],
        broad[:2],
        broad[2:],
        proj[:, :, :own],
        proj[:, :, own : 2 * own],
        proj[:, :, 2 * own : 3 * own],
        jnp.swapaxes(proj[:, :, 3 * own :], 1, 2),
        jnp.stack(up_grads),
        jnp.stack(down_grads),
    )


def solution(mesh):
    return jax.shard_map(
        on_device,
        mesh=mesh,
        in_specs=(
            P("clip", "frame", None, None),
            P("clip", None),
            P(),
            P("clip", None, None),
            P(),
            P(),
            P(),
            P(),
            P(None, None, "frame"),
            P(None, None, "frame"),
            P(None, None, "frame"),
            P(None, "frame", None),
            P(None, None, "frame"),
            P(None, "frame", None),
            P("clip", None, None),
        ),
        out_specs=(
            P("clip", None, None),
            P("clip", "frame", None, None),
            P("clip", None, None),
            P(None, ("clip", "frame")),
            P(None, ("clip", "frame")),
            P(None, "clip"),
            P(None, "clip"),
            P(None, "clip", "frame"),
            P(None, "clip", "frame"),
            P(None, "clip", "frame"),
            P(None, "frame", "clip"),
            P(None, "clip", "frame"),
            P(None, "frame", "clip"),
        ),
        check_vma=False,
    )
```

```python
import functools

import jax
import jax.numpy as jnp
from jax import lax
from jax.experimental import pallas as pl
from jax.experimental.pallas import tpu as pltpu
from jax.sharding import PartitionSpec as P

HEAD_DIM = 96
SLOTS = 4
LAYERS = 2
EPSILON = 1e-05
SCALING = HEAD_DIM ** (-0.5)
MIB = 1 << 20
f32 = jnp.float32
bf16 = jnp.bfloat16
VMEM = pl.BlockSpec(memory_space=pltpu.VMEM)
ANY = pl.BlockSpec(memory_space=pl.ANY)
HBM = pl.BlockSpec(memory_space=pltpu.HBM)


def norm_plain(v):
    mean = jnp.mean(v, axis=-1, keepdims=True)
    centred = v - mean
    inverse = lax.rsqrt(jnp.mean(centred * centred, axis=-1, keepdims=True) + EPSILON)
    return centred * inverse, inverse


def norm_back(u, normed, inverse):
    return inverse * (
        u
        - jnp.mean(u, axis=-1, keepdims=True)
        - normed * jnp.mean(u * normed, axis=-1, keepdims=True)
    )


def dot(a, b):
    return jnp.dot(a, b, preferred_element_type=f32)


def dot_nt(a, b):
    return lax.dot_general(a, b, (((1,), (1,)), ((), ())), preferred_element_type=f32)


def dot_tn(a, b):
    return lax.dot_general(a, b, (((0,), (0,)), ((), ())), preferred_element_type=f32)


def gelu_parts(x):
    half = 0.5 + 0.5 * lax.erf(x * (0.5**0.5))
    return x * half, half + x * jnp.exp(-0.5 * x * x) * (0.5 / jnp.pi) ** 0.5


def shape(dims, kind=bf16):
    return jax.ShapeDtypeStruct(tuple(dims), kind)


def far(dims, kind=bf16):
    return pltpu.HBM(tuple(dims), kind)


def settings(mib, micros):
    return dict(
        compiler_params=pltpu.CompilerParams(vmem_limit_bytes=mib * MIB),
        cost_estimate=pl.CostEstimate(flops=int(micros * 1.15e9), bytes_accessed=1000, transcendentals=0),
    )


def hbm(v):
    return pltpu.with_memory_space_constraint(v, pltpu.HBM)


def fixed(dims, maps=None):
    return pl.BlockSpec(tuple(dims), maps or (lambda *i: (0,) * len(dims)), pipeline_mode=pl.Buffered(1))


def spread(v, heads):
    head = lax.broadcasted_iota(jnp.int32, v.shape, 1) // HEAD_DIM
    return jnp.concatenate([jnp.where(head == h, v, jnp.zeros_like(v)) for h in range(heads)], axis=0)


def gathered(v, heads):
    rows = v.shape[0] // heads
    head = lax.broadcasted_iota(jnp.int32, (rows, v.shape[1]), 1) // HEAD_DIM
    total = v[:rows]
    for h in range(1, heads):
        total = jnp.where(head == h, v[h * rows : (h + 1) * rows], total)
    return total


def on_core(run):
    core = lax.rem(lax.axis_index("frame"), 2)
    for value in (0, 1):
        pl.when(core == value)(functools.partial(run, value))


def put_halves(part, keep, send):
    half = part.shape[0] // 2
    halves = (part[:half].astype(bf16), part[half:].astype(bf16))

    def run(core):
        keep[...] = halves[core]
        send[...] = halves[1 - core]

    on_core(run)


def take_halves(dest, base, mine, other):
    half = mine.shape[0]

    def run(core):
        ordered = (mine, other) if core == 0 else (other, mine)
        for n in range(2):
            rows = slice(n * half, (n + 1) * half)
            dest[rows] = base[rows] + ordered[n][...].astype(f32) if base is not None else ordered[n][...].astype(f32)

    on_core(run)


def tie(v, after):
    return pl.pallas_call(
        lambda *refs: None,
        in_specs=[ANY] * (1 + len(after)),
        out_specs=ANY,
        out_shape=shape(v.shape, v.dtype),
        input_output_aliases={0: 0},
        **settings(1, 1),
    )(v, *after)


class Fetch:
    def __init__(self, sems):
        self.sems, self.used = sems, 0

    def __call__(self, src, dst):
        copy = pltpu.make_async_copy(src, dst, self.sems.at[self.used])
        self.used += 1
        copy.start()
        return copy


def media_kernel(frame, stamp, wide_k, wide_v, plain_out, *outs):
    plain, _ = norm_plain(frame[...].astype(f32) + stamp[0])
    plain = plain.astype(bf16)
    plain_out[...] = plain
    for l in range(LAYERS):
        outs[2 * l][...] = dot(plain, wide_k[l]).astype(bf16)
        outs[2 * l + 1][...] = dot(plain, wide_v[l]).astype(bf16)


def media_stage(frame, stamp, wide_k, wide_v, clips):
    rows, width = frame.shape
    own = wide_k.shape[2]
    patches = rows // clips
    piece = lambda w: pl.BlockSpec((patches, w), lambda i: (i, 0))
    return pl.pallas_call(
        media_kernel,
        grid=(clips,),
        in_specs=[piece(width), pl.BlockSpec((1, 1, width), lambda i: (i, 0, 0)), VMEM, VMEM],
        out_specs=[piece(width)] + [piece(own)] * 4,
        out_shape=[far((rows, width))] + [far((rows, own))] * 4,
        **settings(14, 5),
    )(frame, stamp, wide_k, wide_v)


def fetch_keys(fetch, groups, ks, clips):
    copies = [[] for _ in range(clips)]
    at = 0
    for ref in groups:
        patches = ref.shape[0] // clips
        for c in range(clips):
            copies[c].append(fetch(ref.at[pl.ds(c * patches, patches)], ks.at[c, pl.ds(at, patches)]))
        at += patches
    return copies, at


def attn_kernel(l, clips, nf, first, *refs):
    if first:
        base, gain, wq, wk, wv, wo = refs[:6]
        refs = refs[6:]
    else:
        base, mine, other, gain, wq, wk, wv, wo = refs[:8]
        refs = refs[8:]
    frame_keys, frame_values = refs[:nf], refs[nf : 2 * nf]
    keep, send, lat_n_out, heads_out, soft_out = refs[2 * nf : 2 * nf + 5]
    wqs, wks, wvs, wos, ks, vs, soft_s, lat_n_s, heads_s, sems = refs[-10:]
    fetch = Fetch(sems)
    waits = [fetch(wq.at[l], wqs), fetch(wk.at[l], wks), fetch(wv.at[l], wvs)]
    key_copies, media_keys = fetch_keys(fetch, frame_keys, ks, clips)
    value_copies, _ = fetch_keys(fetch, frame_values, vs, clips)
    wo_copy = fetch(wo.at[l], wos)
    stores = []
    if first:
        lat = base
    else:
        lat, lat_out = refs[2 * nf + 5 : 2 * nf + 7]
        take_halves(lat, base, mine, other)
        stores.append(fetch(lat, lat_out))
    plain, _ = norm_plain(lat[...])
    lat_n = (plain * gain[l : l + 1, :]).astype(bf16)
    lat_n_s[...] = lat_n
    stores.append(fetch(lat_n_s, lat_n_out))
    heads = wqs.shape[1] // HEAD_DIM
    rows = lat_n.shape[0] // clips
    for copy in waits:
        copy.wait()
    q = dot(lat_n, wqs[...]).astype(bf16)
    kl = dot(lat_n, wks[...]).astype(bf16)
    vl = dot(lat_n, wvs[...]).astype(bf16)
    heads_s[0] = q
    heads_s[1] = kl
    heads_s[2] = vl
    atts = []
    for c in range(clips):
        part = slice(c * rows, (c + 1) * rows)
        ks[c, media_keys:] = kl[part]
        vs[c, media_keys:] = vl[part]
        for copy in key_copies[c]:
            copy.wait()
        scores = dot_nt(spread(q[part], heads), ks[c]) * SCALING
        ex = jnp.exp(scores - jnp.max(scores, axis=-1, keepdims=True))
        soft = (ex / jnp.sum(ex, axis=-1, keepdims=True)).astype(bf16)
        soft_s[c] = soft
        stores.append(fetch(soft_s.at[c], soft_out.at[c]))
        for copy in value_copies[c]:
            copy.wait()
        atts.append(gathered(dot(soft, vs[c]), heads).astype(bf16))
    att = jnp.concatenate(atts, axis=0)
    heads_s[3] = att
    stores.append(fetch(heads_s, heads_out))
    wo_copy.wait()
    put_halves(dot(att, wos[...]), keep, send)
    for copy in stores:
        copy.wait()


def attn_stage(l, clips, base, halves, gain, wq, wk, wv, wo, keys, values):
    rows, width = base.shape
    own = wq.shape[2]
    heads = own // HEAD_DIM
    nkeys = sum(k.shape[0] // clips for k in keys) + rows // clips
    soft = (clips, heads * rows // clips, nkeys)
    first = halves is None
    smalls = [base] + ([] if first else list(halves)) + [gain]
    outs = [shape((rows // 2, width)), shape((rows // 2, width)), far((rows, width)), far((4, rows, own)), far(soft)]
    specs = [VMEM] * 2 + [HBM] * 3
    if not first:
        outs += [shape((rows, width), f32), far((rows, width), f32)]
        specs += [VMEM, HBM]
    return pl.pallas_call(
        functools.partial(attn_kernel, l, clips, len(keys), first),
        in_specs=[VMEM] * len(smalls) + [HBM] * (4 + 2 * len(keys)),
        out_specs=specs,
        out_shape=outs,
        scratch_shapes=[pltpu.VMEM((width, own), bf16)] * 3
        + [pltpu.VMEM((own, width), bf16)]
        + [pltpu.VMEM((clips, nkeys, own), bf16)] * 2
        + [pltpu.VMEM(soft, bf16), pltpu.VMEM((rows, width), bf16), pltpu.VMEM((4, rows, own), bf16)]
        + [pltpu.SemaphoreType.DMA((7 + clips + 2 * clips * len(keys),))],
        **settings(20, 9),
    )(*smalls, wq, wk, wv, wo, *keys, *values)


def quarter(dest, src):
    count = dest.shape[0]
    at = lax.rem(lax.axis_index("frame"), src.shape[0] // count)
    dest[...] = src[pl.ds(pl.multiple_of(at * count, count), count), :]


def ffn_kernel(
    l, step, base, mine, other, gain, up, down, keep, send, middle, rows_out, middle_out, slope_out,
    ups, downs, slope_s, ffn_s, sems,
):
    fetch = Fetch(sems)
    hidden_all = ups.shape[1]
    blocks = [pl.ds(n * step, step) for n in range(hidden_all // step)]
    up_copies = [fetch(up.at[l, :, b], ups.at[:, b]) for b in blocks]
    down_copies = [fetch(down.at[l, b], downs.at[b]) for b in blocks]
    take_halves(middle, base, mine, other)
    stores = [fetch(middle, middle_out)]
    plain, _ = norm_plain(middle[...])
    ffn_in = (plain * gain[l : l + 1, :]).astype(bf16)
    ffn_s[...] = ffn_in
    quarter(rows_out, ffn_s)
    hiddens = []
    for n, b in enumerate(blocks):
        up_copies[n].wait()
        hidden, slope = gelu_parts(dot(ffn_in, ups[:, b]))
        slope_s[:, b] = slope.astype(bf16)
        hiddens.append(hidden.astype(bf16))
    stores.append(fetch(slope_s, slope_out))
    total = None
    for n, b in enumerate(blocks):
        down_copies[n].wait()
        part = dot(hiddens[n], downs[b, :])
        total = part if total is None else total + part
    put_halves(total, keep, send)
    for copy in stores:
        copy.wait()


def ffn_stage(l, shares, base, halves, gain, up, down):
    rows, width = base.shape
    hidden = up.shape[2]
    step = 256
    return pl.pallas_call(
        functools.partial(ffn_kernel, l, step),
        in_specs=[VMEM] * 4 + [HBM] * 2,
        out_specs=[VMEM] * 4 + [HBM] * 2,
        out_shape=[
            shape((rows // 2, width)),
            shape((rows // 2, width)),
            shape((rows, width), f32),
            shape((rows // shares, width)),
            far((rows, width), f32),
            far((rows, hidden)),
        ],
        scratch_shapes=[
            pltpu.VMEM((width, hidden), bf16),
            pltpu.VMEM((hidden, width), bf16),
            pltpu.VMEM((rows, hidden), bf16),
            pltpu.VMEM((rows, width), bf16),
            pltpu.SemaphoreType.DMA((2 * hidden // step + 2,)),
        ],
        **settings(15, 5),
    )(base, *halves, gain, up, down)


def ffn_back_kernel(l, step, top, *refs):
    if top:
        base, living, slope_in, up, down = refs[:5]
        keep, send, grad, rows_out = refs[5:9]
        ups, downs, slope_s, gy_s, sems = refs[9:]
    else:
        base, mine, other, gain, lat_in, slope_in, up, down = refs[:8]
        keep, send, grad, rows_out, gain_grad = refs[8:13]
        ups, downs, slope_s, gy_s, sems, work, lat = refs[13:]
    fetch = Fetch(sems)
    blocks = [pl.ds(n * step, step) for n in range(ups.shape[1] // step)]
    lat_copy = None if top else fetch(lat_in, lat)
    down_copies = [fetch(down.at[l, b], downs.at[b]) for b in blocks]
    slope_copy = fetch(slope_in, slope_s)
    up_copies = [fetch(up.at[l, :, b], ups.at[:, b]) for b in blocks]
    if top:
        now = base[...] * living[...]
    else:
        take_halves(work, None, mine, other)
        lat_copy.wait()
        now = latent_back(base, work, lat, gain, l + 1, gain_grad)
    grad[...] = now
    gy = now.astype(bf16)
    gy_s[...] = gy
    quarter(rows_out, gy_s)
    slope_copy.wait()
    gpres = []
    for n, b in enumerate(blocks):
        down_copies[n].wait()
        gpres.append((slope_s[:, b].astype(f32) * dot_nt(gy, downs[b, :])).astype(bf16))
    total = None
    for n, b in enumerate(blocks):
        up_copies[n].wait()
        part = dot_nt(gpres[n], ups[:, b])
        total = part if total is None else total + part
    put_halves(total, keep, send)


def latent_back(base, work, lat, gain, l, gain_grad):
    plain, inverse = norm_plain(lat[...])
    arrived = work[...]
    gain_grad[...] = jnp.sum(arrived * plain, axis=0, keepdims=True)
    return base[...] + norm_back(arrived * gain[l : l + 1, :], plain, inverse)


def ffn_back_stage(l, shares, base, above, slope, up, down):
    rows, width = base.shape
    hidden = up.shape[2]
    step = 256
    top = len(above) == 1
    outs = [
        shape((rows // 2, width)),
        shape((rows // 2, width)),
        shape((rows, width), f32),
        shape((rows // shares, width)),
    ] + ([] if top else [shape((1, width), f32)])
    return pl.pallas_call(
        functools.partial(ffn_back_kernel, l, step, top),
        in_specs=([VMEM] * 2 if top else [VMEM] * 4 + [HBM]) + [HBM] * 3,
        out_specs=[VMEM] * len(outs),
        out_shape=outs,
        scratch_shapes=[
            pltpu.VMEM((width, hidden), bf16),
            pltpu.VMEM((hidden, width), bf16),
            pltpu.VMEM((rows, hidden), bf16),
            pltpu.VMEM((rows, width), bf16),
            pltpu.SemaphoreType.DMA((2 * hidden // step + 2,)),
        ]
        + ([] if top else [pltpu.VMEM((rows, width), f32)] * 2),
        **settings(16, 6),
    )(base, *above, slope, up, down)


def attn_back_kernel(l, clips, nf, base, mine, other, gain, middle_in, heads_in, soft_in, wo, wq, wk, wv, *refs):
    frame_keys, frame_values = refs[:nf], refs[nf : 2 * nf]
    keep, send, gmid_out, gain_grad, gupd_out, grads_out, gscore_out = refs[2 * nf : 2 * nf + 7]
    wqs, wks, wvs, wos, ks, vs, work, middle, heads_s, grads_s, gupd_s, soft_s, score_s, sems = refs[2 * nf + 7 :]
    fetch = Fetch(sems)
    middle_copy = fetch(middle_in, middle)
    wo_copy = fetch(wo.at[l], wos)
    heads_copy = fetch(heads_in, heads_s)
    value_copies, media_keys = fetch_keys(fetch, frame_values, vs, clips)
    soft_copies = [fetch(soft_in.at[c], soft_s.at[c]) for c in range(clips)]
    key_copies, _ = fetch_keys(fetch, frame_keys, ks, clips)
    waits = [fetch(wq.at[l], wqs), fetch(wk.at[l], wks), fetch(wv.at[l], wvs)]
    take_halves(work, None, mine, other)
    middle_copy.wait()
    gmid = latent_back(base, work, middle, gain, l, gain_grad)
    gmid_out[...] = gmid
    gupd = gmid.astype(bf16)
    gupd_s[...] = gupd
    stores = [fetch(gupd_s, gupd_out)]
    heads = wqs.shape[1] // HEAD_DIM
    rows = gupd.shape[0] // clips
    wo_copy.wait()
    gatt = dot_nt(gupd, wos[...]).astype(bf16)
    heads_copy.wait()
    gqs, gkls, gvls = [], [], []
    for c in range(clips):
        part = slice(c * rows, (c + 1) * rows)
        ks[c, media_keys:] = heads_s[1, part]
        vs[c, media_keys:] = heads_s[2, part]
        qs = spread(heads_s[0, part], heads)
        gs = spread(gatt[part], heads)
        for copy in value_copies[c]:
            copy.wait()
        gsoft = dot_nt(gs, vs[c])
        soft_copies[c].wait()
        soft = soft_s[c]
        soft32 = soft.astype(f32)
        delta = jnp.sum(soft32 * gsoft, axis=-1, keepdims=True)
        gscore = (soft32 * (gsoft - delta)).astype(bf16)
        score_s[c] = gscore
        stores.append(fetch(score_s.at[c], gscore_out.at[c]))
        for copy in key_copies[c]:
            copy.wait()
        gqs.append(gathered(dot(gscore, ks[c]), heads) * SCALING)
        gkls.append(dot_tn(gscore[:, media_keys:], qs) * SCALING)
        gvls.append(dot_tn(soft[:, media_keys:], gs))
    gq = jnp.concatenate(gqs, axis=0).astype(bf16)
    gkl = jnp.concatenate(gkls, axis=0).astype(bf16)
    gvl = jnp.concatenate(gvls, axis=0).astype(bf16)
    grads_s[0] = gatt
    grads_s[1] = gq
    grads_s[2] = gkl
    grads_s[3] = gvl
    stores.append(fetch(grads_s, grads_out))
    for copy in waits:
        copy.wait()
    put_halves(dot_nt(gq, wqs[...]) + dot_nt(gkl, wks[...]) + dot_nt(gvl, wvs[...]), keep, send)
    for copy in stores:
        copy.wait()


def attn_back_stage(l, clips, base, halves, gain, middle, heads_all, soft, wo, wq, wk, wv, keys, values):
    rows, width = base.shape
    own = wq.shape[2]
    outs = [
        shape((rows // 2, width)),
        shape((rows // 2, width)),
        shape((rows, width), f32),
        shape((1, width), f32),
        far((rows, width)),
        far((4, rows, own)),
        far(soft.shape),
    ]
    nkeys = soft.shape[2]
    return pl.pallas_call(
        functools.partial(attn_back_kernel, l, clips, len(keys)),
        in_specs=[VMEM] * 4 + [HBM] * (7 + 2 * len(keys)),
        out_specs=[VMEM] * 4 + [HBM] * 3,
        out_shape=outs,
        scratch_shapes=[pltpu.VMEM((width, own), bf16)] * 3
        + [pltpu.VMEM((own, width), bf16)]
        + [pltpu.VMEM((clips, nkeys, own), bf16)] * 2
        + [pltpu.VMEM((rows, width), f32)] * 2
        + [pltpu.VMEM((4, rows, own), bf16)] * 2
        + [pltpu.VMEM((rows, width), bf16)]
        + [pltpu.VMEM(soft.shape, bf16)] * 2
        + [pltpu.SemaphoreType.DMA((8 + 2 * clips + 2 * clips * len(keys),))],
        **settings(24, 10),
    )(base, *halves, gain, middle, heads_all, soft, wo, wq, wk, wv, *keys, *values)


def last_kernel(l, base, mine, other, lat, gain, *refs):
    grad, gain_grad, work = refs[-3:]
    take_halves(work, None, mine, other)
    grad[...] = latent_back(base, work, lat, gain, l, gain_grad)


def last_stage(base, halves, lat, gain, after):
    rows, width = base.shape
    return pl.pallas_call(
        functools.partial(last_kernel, 0),
        in_specs=[VMEM] * 5 + [ANY] * len(after),
        out_specs=[VMEM] * 2,
        out_shape=[shape((rows, width), f32), shape((1, width), f32)],
        scratch_shapes=[pltpu.VMEM((rows, width), f32)],
        **settings(12, 2),
    )(base, *halves, lat, gain, *after)


def proj_kernel(clips, cut, nf, *refs):
    plains = refs[:nf]
    lat_n, gupd, wk, wv, gain, gscore, soft, heads_all, grads = refs[nf : nf + 9]
    out, out_last, media_gain, qs, gs = refs[-5:]
    _, total, own = heads_all.shape
    heads = own // HEAD_DIM
    rows = total // clips
    wide = heads * rows

    @pl.when(pl.program_id(0) == 0)
    def _():
        for c in range(clips):
            part = slice(c * rows, (c + 1) * rows)
            qs[c * wide : (c + 1) * wide] = (spread(heads_all[0, part], heads).astype(f32) * SCALING).astype(bf16)
            gs[c * wide : (c + 1) * wide] = spread(grads[0, part], heads)

    scale = gain[...]
    zs, ys = [], []
    for c in range(clips):
        z = y = None
        at = 0
        for plain in plains:
            patches = plain.shape[0] // clips
            block = plain[c * patches : (c + 1) * patches]
            part_z = dot(gscore[c, :, at : at + patches], block)
            part_y = dot(soft[c, :, at : at + patches], block)
            z = part_z if z is None else z + part_z
            y = part_y if y is None else y + part_y
            at += patches
        zs.append((z * scale).astype(bf16))
        ys.append((y * scale).astype(bf16))
    kg = dot_tn(jnp.concatenate(zs, axis=0), qs[...])
    vg = dot_tn(jnp.concatenate(ys, axis=0), gs[...])
    along = kg * wk[0].astype(f32) + vg * wv[0].astype(f32)
    ones = jnp.ones((8, own), f32)
    media_gain[...] = lax.dot_general(
        ones, along, (((1,), (1,)), ((), ())), precision=lax.Precision.HIGHEST, preferred_element_type=f32
    ) / scale
    lat_b = lat_n[...]
    kg = (kg + dot_tn(lat_b, grads[2])).astype(bf16)
    vg = (vg + dot_tn(lat_b, grads[3])).astype(bf16)
    qg = dot_tn(lat_b, grads[1]).astype(bf16)
    og = dot_tn(gupd[...], heads_all[3]).astype(bf16)
    for b in range(kg.shape[0] // cut):
        for n, grad in enumerate((kg, vg, qg, og)):
            dest = (out, n) if n < 3 else (out_last, 0)
            dest[0][b, dest[1]] = grad[b * cut : (b + 1) * cut]


def proj_stage(l, clips, nc, plains, lat_n, gupd, wk, wv, gain, gscore, soft, heads_all, grads, after):
    width = lat_n.shape[1]
    _, rows, own = heads_all.shape
    cut = width // nc
    block = 384
    per = block // cut
    heads = own // HEAD_DIM
    wide = heads * rows
    full = lambda v: fixed(v.shape)
    columns = lambda v: pl.BlockSpec(v.shape[:-1] + (block,), lambda i: (0,) * (v.ndim - 1) + (i,))
    weight = pl.BlockSpec((1, block, own), lambda i: (l, i, 0))
    return pl.pallas_call(
        functools.partial(proj_kernel, clips, cut, len(plains)),
        grid=(width // block,),
        in_specs=[columns(v) for v in plains]
        + [columns(lat_n), columns(gupd), weight, weight, columns(gain)]
        + [full(v) for v in (gscore, soft, heads_all, grads)]
        + [ANY] * len(after),
        out_specs=[
            pl.BlockSpec((per, 3, cut, own), lambda i: (i, 0, 0, 0)),
            pl.BlockSpec((per, 1, cut, own), lambda i: (i, 0, 0, 0)),
            pl.BlockSpec((8, block), lambda i: (0, i)),
        ],
        out_shape=[shape((nc, 3, cut, own)), shape((nc, 1, cut, own)), shape((8, width), f32)],
        scratch_shapes=[pltpu.VMEM((wide, own), bf16)] * 2,
        **settings(22, 12),
    )(*plains, lat_n, gupd, wk, wv, gain, gscore, soft, heads_all, grads, *after)


def media_back_kernel(clips, *refs):
    count = 2 * LAYERS
    tables, firsts, weights = refs[:count], refs[count : 2 * count], refs[2 * count : 2 * count + 2]
    out, stack = refs[-2:]

    @pl.when(pl.program_id(1) == 0)
    def _():
        own = weights[0].shape[2]
        heads = own // HEAD_DIM
        for n in range(count):
            l = n // 2
            v = firsts[n][0]
            if n % 2 == 0:
                v = (v.astype(f32) * SCALING).astype(bf16)
            across = dot_nt(spread(v, heads), weights[n % 2][l])
            rows = across.shape[0]
            stack[n * rows : (n + 1) * rows] = across.astype(bf16)

    left = jnp.concatenate([t[0] for t in tables], axis=0)
    out[0] = dot_tn(left, stack[...]).astype(bf16)


def media_back_stage(first_frame, frames, clips, patches, tables, firsts, wk, wv, after):
    width = wk.shape[1]
    table = pl.BlockSpec((1, tables[0].shape[1], patches), lambda c, r: (c, 0, first_frame + r))
    _, rows, own = firsts[0].shape
    piece = pl.BlockSpec((1, rows // clips, own), lambda c, r: (0, c, 0))
    full = lambda v: fixed(v.shape)
    return pl.pallas_call(
        functools.partial(media_back_kernel, clips),
        grid=(clips, frames),
        in_specs=[table] * 4 + [piece] * 4 + [full(wk), full(wv)] + [ANY] * len(after),
        out_specs=pl.BlockSpec((1, patches, width), lambda c, r: (r, c, 0)),
        out_shape=shape((frames, clips * patches, width)),
        scratch_shapes=[pltpu.VMEM((4 * tables[0].shape[1], width), bf16)],
        **settings(24, 8),
    )(*tables, *firsts, wk, wv, *after)


def media_last_kernel(count, per, media, stamp, *refs):
    parts, out, sums = refs[:count], refs[count], refs[count + 1]
    plain, inverse = norm_plain(media[...].astype(f32) + stamp[0])
    u = parts[0][...].astype(f32)
    for part in parts[1:]:
        u = u + part[...].astype(f32)
    grad = norm_back(u, plain, inverse)
    out[...] = grad

    @pl.when(pl.program_id(0) % per == 0)
    def _():
        sums[...] = jnp.zeros_like(sums)

    sums[0] += jnp.sum(grad, axis=0, keepdims=True)


def media_last_stage(media, stamp, parts, clips):
    rows, width = media.shape
    step = 128
    per = rows // clips // step
    piece = pl.BlockSpec((step, width), lambda i: (i, 0))
    clip = pl.BlockSpec((1, 1, width), lambda i: (i // per, 0, 0))
    return pl.pallas_call(
        functools.partial(media_last_kernel, len(parts), per),
        grid=(rows // step,),
        in_specs=[piece, clip] + [piece] * len(parts),
        out_specs=[piece, clip],
        out_shape=[shape((rows, width), f32), shape((clips, 1, width), f32)],
        **settings(20, 5),
    )(media, stamp, *parts)


def ffn_grad_kernel(pieces, *refs):
    up, down = refs[4 * pieces : 4 * pieces + 2]
    up_grad, down_grad = refs[-2:]
    flat = lambda ref: ref[...].reshape(-1, ref.shape[2])
    up_part = down_part = None
    for n in range(pieces):
        rows_all, grads_all, rows_own, grads_own = refs[4 * n : 4 * n + 4]
        hidden, slope = gelu_parts(dot(flat(rows_all), up[0]))
        gpre = (slope * dot_nt(flat(grads_all), down[0])).astype(bf16)
        up_more = dot_tn(flat(rows_own), gpre)
        down_more = dot_tn(hidden.astype(bf16), flat(grads_own))
        up_part = up_more if up_part is None else up_part + up_more
        down_part = down_more if down_part is None else down_part + down_more
    chunk = pl.program_id(1)

    @pl.when(chunk == 0)
    def _():
        up_grad[0] = up_part
        down_grad[0] = down_part

    @pl.when(chunk > 0)
    def _():
        up_grad[0] += up_part
        down_grad[0] += down_part


def ffn_grad_stage(l, count, pieces, up, down, earlier, after):
    devices, _, width = pieces[0][0].shape
    cut = pieces[0][2].shape[2]
    hidden = up.shape[2]
    step = 256
    chunk = min(devices, 1024 // (len(pieces) * count))
    outs = [shape((LAYERS, cut, hidden), f32), shape((LAYERS, hidden, cut), f32)]
    piece = lambda w, at: pl.BlockSpec((chunk, count, w), lambda j, i: (i, at, 0))
    specs, arrays = [], []
    for rows, grads, rows_own, grads_own, at_rows, at_grads in pieces:
        arrays += [hbm(rows), hbm(grads), rows_own, grads_own]
        specs += [piece(width, at_rows), piece(width, at_grads), piece(cut, at_rows), piece(cut, at_grads)]
    known = len(arrays) + 2
    return pl.pallas_call(
        functools.partial(ffn_grad_kernel, len(pieces)),
        grid=(hidden // step, devices // chunk),
        in_specs=specs
        + [
            pl.BlockSpec((1, width, step), lambda j, i: (l, 0, j)),
            pl.BlockSpec((1, step, width), lambda j, i: (l, j, 0)),
        ]
        + [ANY] * (len(earlier) + len(after)),
        out_specs=[
            pl.BlockSpec((1, cut, step), lambda j, i: (l, 0, j)),
            pl.BlockSpec((1, step, cut), lambda j, i: (l, j, 0)),
        ],
        out_shape=outs,
        input_output_aliases={known: 0, known + 1: 1} if earlier else {},
        **settings(36, 16),
    )(*arrays, up, down, *earlier, *after)


def swap(v, axis, bit):
    size = lax.axis_size(axis)
    return lax.ppermute(v, axis, [(i, i ^ bit) for i in range(size)])


def bits_of(size):
    out, bit = [], 1
    while bit < size:
        out.append(bit)
        bit *= 2
    return out


def add_kernel(mine, arrived, *refs):
    refs[-1][...] = (mine[...].astype(f32) + arrived[...].astype(f32)).astype(bf16)


def add_after(mine, arrived, after):
    return pl.pallas_call(
        add_kernel,
        in_specs=[VMEM] * 2 + [ANY] * len(after),
        out_specs=VMEM,
        out_shape=shape(mine.shape),
        **settings(4, 1),
    )(mine, arrived, *after)


def frame_sum(keep, send, fill=None):
    mine = (keep.astype(f32) + swap(send, "frame", 1).astype(f32)).astype(bf16)
    made = None
    for bit in bits_of(lax.axis_size("frame"))[1:]:
        arrived = swap(mine, "frame", bit)
        if fill is not None and made is None:
            made = fill((mine,))
            mine = add_after(mine, arrived, made)
        else:
            mine = (mine.astype(f32) + arrived.astype(f32)).astype(bf16)
    return (mine, swap(mine, "frame", 1)) if fill is None else ((mine, swap(mine, "frame", 1)), made)


def gather_rows(shares):
    return lax.all_gather(jnp.concatenate(shares, axis=0), ("clip", "frame"), axis=0)


class Scatter:
    def __init__(self, parts, bits, clip_here):
        self.total = parts.reshape((2,) * len(bits) + parts.shape[1:])
        self.bits, self.left, self.clip_here = list(bits), sorted(bits, reverse=True), clip_here

    def send(self):
        bit = self.bits.pop(0)
        axis = self.left.index(bit)
        self.left.remove(bit)
        mine = (self.clip_here // bit) % 2
        self.kept = lax.dynamic_index_in_dim(self.total, mine, axis, keepdims=False)
        sent = lax.dynamic_index_in_dim(self.total, 1 - mine, axis, keepdims=False).astype(bf16)
        self.arriving = swap(sent, "clip", bit)
        return self

    def step(self, after):
        if self.arriving is None:
            return
        arrived = tie(self.arriving, after) if after else self.arriving
        self.total = self.kept.astype(f32) + arrived.astype(f32)
        self.arriving = None
        if self.bits:
            self.send()


def exchange_rows(share, nc):
    mine = lax.all_to_all(jnp.broadcast_to(share, (nc,) + share.shape), "clip", 0, 0, tiled=True)
    return mine, swap(mine, "frame", 1)


def on_device(
    media, frame_order, clip_counts, latents, time_embed, media_gain, latent_gain, ffn_gain,
    query_weight, key_weight, value_weight, out_weight, up_weight, down_weight, cotangent,
):
    clips, _, patches, width = media.shape
    lat_rows = latents.shape[1]
    nf = lax.axis_size("frame")
    nc = lax.axis_size("clip")
    frame_here = lax.axis_index("frame")
    clip_here = lax.axis_index("clip")
    rows = clips * lat_rows

    key_plain, value_plain = key_weight, value_weight
    query_weight, key_weight, value_weight, out_weight, up_weight, down_weight = (
        pltpu.with_memory_space_constraint(w, pltpu.HBM)
        for w in (query_weight, key_weight, value_weight, out_weight, up_weight, down_weight)
    )
    clip_ids = clip_here * clips + jnp.arange(clips, dtype=jnp.int32)
    owner_match = (clip_ids // SLOTS)[:, None] == jnp.arange(clip_counts.shape[0], dtype=jnp.int32)[None, :]
    owner_count = jnp.sum(jnp.where(owner_match, clip_counts[None, :], 0), axis=1)
    living = (clip_ids % SLOTS < owner_count).astype(f32)
    living = jnp.repeat(living, lat_rows)[:, None]

    flat = media.reshape(clips * patches, width)
    top = nf // 2
    frames = {0: flat}
    if top > 1:
        frames[top] = swap(flat, "frame", top)
    for bit in bits_of(top)[::-1]:
        for r in [r for r in frames if r < top]:
            frames[r | bit] = swap(frames[r], "frame", bit)
    times = jnp.arange(nf, dtype=jnp.int32)
    order = jnp.stack(
        [lax.dynamic_index_in_dim(frame_order, frame_here ^ r, 1, keepdims=False) for r in range(nf)]
    )
    onehot = (order[:, :, None] == times).astype(f32)
    stamps = jnp.sum(onehot[..., None] * time_embed, axis=2)[:, :, None, :]
    wide_k = (media_gain[:, :, None] * key_plain.astype(f32)).astype(bf16)
    wide_v = (media_gain[:, :, None] * value_plain.astype(f32)).astype(bf16)
    ready = [media_stage(frames[r], stamps[r], wide_k, wide_v, clips) for r in range(top)]
    frames[top] = tie(frames[top], [made[0] for made in ready])
    for bit in bits_of(top)[::-1]:
        for r in [r for r in frames if r >= top]:
            frames[r | bit] = swap(frames[r], "frame", bit)
    ready += [media_stage(frames[r], stamps[r], wide_k, wide_v, clips) for r in range(top, nf)]
    plains = [hbm(g[0]) for g in ready]

    stored = []
    current, halves = latents.reshape(rows, width), None
    for l in range(LAYERS):
        keys = [hbm(g[1 + 2 * l]) for g in ready]
        values = [hbm(g[2 + 2 * l]) for g in ready]
        out = attn_stage(
            l, clips, current, halves, latent_gain, query_weight, key_weight, value_weight, out_weight, keys, values
        )
        keep, send, lat_n, heads_all, soft = out[:5]
        lat, lat_far = (current, None) if halves is None else (out[5], hbm(out[6]))
        halves = frame_sum(keep, send)
        keep, send, current, ffn_rows, middle, slope = ffn_stage(l, nf if l else 2, lat, halves, ffn_gain, up_weight, down_weight)
        halves = frame_sum(keep, send)
        if not l:
            lower_rows = exchange_rows(ffn_rows, nc)
        stored.append((keys, values, lat_far, hbm(lat_n), hbm(heads_all), hbm(soft), hbm(middle), ffn_rows, hbm(slope)))
    core = frame_here % 2
    first = jnp.where(core == 0, halves[0], halves[1])
    second = jnp.where(core == 0, halves[1], halves[0])
    latents_out = (current + jnp.concatenate([first, second], axis=0).astype(f32)) * living

    cut = width // nc
    count = rows // nf
    own_columns = lambda v: lax.dynamic_slice_in_dim(v, clip_here * cut, cut, 2)
    lat_gain_grads, ffn_gain_grads, media_gain_grads = [None] * LAYERS, [None] * LAYERS, [None] * LAYERS
    projs, tables, firsts = [None] * LAYERS, [None] * LAYERS, [None] * LAYERS

    def back(l, base, above, fill):
        keys, values, lat_far, lat_n, heads_all, soft, middle, _, slope = stored[l]
        out = ffn_back_stage(l, nf if l else 2, base, above, slope, up_weight, down_weight)
        keep, send, grad, share = out[:4]
        if l < LAYERS - 1:
            lat_gain_grads[l + 1] = out[4]
        halves, made = frame_sum(keep, send, fill) if fill else (frame_sum(keep, send), None)
        keep, send, gmid, ffn_gain_grads[l], gupd, grads, gscore = attn_back_stage(
            l, clips, grad, halves, ffn_gain, middle, heads_all, soft, out_weight, query_weight, key_weight,
            value_weight, keys, values,
        )
        gupd, grads, gscore = hbm(gupd), hbm(grads), hbm(gscore)
        tables[l], firsts[l] = (gscore, soft), (heads_all, grads)

        def projections(after):
            return proj_stage(
                l, clips, nc, plains, lat_n, gupd, key_weight, value_weight, media_gain[l : l + 1], gscore, soft,
                heads_all, grads, after,
            )

        halves, (*projs[l], along) = frame_sum(keep, send, projections)
        media_gain_grads[l] = along[:1]
        return share, made, gmid, halves, lat_far

    def scattered(l):
        bits = bits_of(nc)
        return [
            Scatter(projs[l][0], bits, clip_here).send(),
            Scatter(projs[l][1], bits[1:] + bits[:1], clip_here).send(),
        ]

    share, _, gmid, halves, lat_far = back(1, cotangent.reshape(rows, width), (living,), None)
    early = gather_rows([stored[1][7], share])
    upper = scattered(1)
    share, _, gmid, halves, _ = back(0, gmid, (*halves, latent_gain, lat_far), None)
    lower_grads = exchange_rows(share, nc)
    lower = scattered(0)
    gate = (projs[0][0],)
    upper[1].step(gate)

    half = nf // 2
    tables = [t for pair in tables for t in pair]
    firsts = [t for pair in firsts for t in pair]
    u = {}
    part = media_back_stage(half, half, clips, patches, tables, firsts, wide_k, wide_v, gate)
    for r in range(half):
        u[half + r] = [part[r]]
    gate = (part,)
    latents_grad, lat_gain_grads[0] = last_stage(gmid, halves, latents.reshape(rows, width), latent_gain, gate)
    upper[0].step(gate)
    merged = lambda v: v[0] if len(v) == 1 else sum(x.astype(f32) for x in v).astype(bf16)

    def fold(bits, least):
        for bit in bits:
            for r in [r for r in u if r & bit and r >= least]:
                u[r ^ bit].append(swap(merged(u.pop(r)), "frame", bit))

    fold(bits_of(half), half)
    sent = merged(u.pop(half))
    arrived = swap(sent, "frame", half)
    part = media_back_stage(0, half, clips, patches, tables, firsts, wide_k, wide_v, (sent, latents_grad))
    for r in range(half):
        u[r] = [part[r]]
    fold(bits_of(half), 0)
    gate = (part,)
    upper[1].step(gate)
    lower[1].step(gate)
    early_own = own_columns(early)
    ffn_parts = ffn_grad_stage(
        1, count, [(early, early, early_own, early_own, 0, 1)], up_weight, down_weight, (), gate
    )
    gate = (ffn_parts[0],)
    upper[0].step(gate)
    upper[1].step(gate)
    lower[0].step(gate)
    lower[1].step(gate)
    up_grad, down_grad = ffn_grad_stage(
        0,
        rows // 2,
        [(r, g, own_columns(r), own_columns(g), 0, 0) for r, g in zip(lower_rows, lower_grads)],
        up_weight,
        down_weight,
        ffn_parts,
        (),
    )
    gate = (up_grad,)
    upper[0].step(gate)
    lower[0].step(gate)
    lower[1].step(gate)
    media_grad, patch_sums = media_last_stage(flat, stamps[0], u[0] + [tie(arrived, gate)], clips)
    lower[0].step((patch_sums,))
    for scatter in upper + lower:
        while scatter.arriving is not None:
            scatter.step(())
    time_part = jnp.dot(onehot[0].T, patch_sums[:, 0], precision=lax.Precision.HIGHEST)

    n_all = nc * nf
    narrow = jnp.concatenate([time_part] + media_gain_grads, axis=0)
    narrow = narrow.reshape(nf + 2, n_all, width // n_all).transpose(1, 0, 2).reshape(n_all, -1)
    broad = jnp.concatenate(lat_gain_grads + ffn_gain_grads, axis=0)
    broad = broad.reshape(4, nc, width // nc).transpose(1, 0, 2).reshape(nc, 1, -1)
    broad = broad * (jnp.arange(nf) == frame_here).astype(f32)[None, :, None]
    packed = jnp.concatenate([narrow, broad.reshape(n_all, -1)], axis=1)
    packed = jnp.sum(lax.all_to_all(packed, ("clip", "frame"), 0, 0, tiled=True), axis=0)
    edge = (nf + 2) * (width // n_all)
    narrow = packed[:edge].reshape(nf + 2, -1)
    broad = packed[edge:].reshape(4, -1)

    pick = lambda part, n: jnp.stack([pair[part].total[n] for pair in (lower, upper)])
    return (
        latents_out.reshape(latents.shape),
        media_grad.reshape(media.shape),
        latents_grad.reshape(latents.shape),
        narrow[:nf],
        narrow[nf:],
        broad[:2],
        broad[2:],
        pick(0, 2),
        pick(0, 0),
        pick(0, 1),
        jnp.swapaxes(pick(1, 0), 1, 2),
        up_grad,
        down_grad,
    )


def solution(mesh):
    return jax.shard_map(
        on_device,
        mesh=mesh,
        in_specs=(
            P("clip", "frame", None, None),
            P("clip", None),
            P(),
            P("clip", None, None),
            P(),
            P(),
            P(),
            P(),
            P(None, None, "frame"),
            P(None, None, "frame"),
            P(None, None, "frame"),
            P(None, "frame", None),
            P(None, None, "frame"),
            P(None, "frame", None),
            P("clip", None, None),
        ),
        out_specs=(
            P("clip", None, None),
            P("clip", "frame", None, None),
            P("clip", None, None),
            P(None, ("clip", "frame")),
            P(None, ("clip", "frame")),
            P(None, "clip"),
            P(None, "clip"),
            P(None, "clip", "frame"),
            P(None, "clip", "frame"),
            P(None, "clip", "frame"),
            P(None, "frame", "clip"),
            P(None, "clip", "frame"),
            P(None, "frame", "clip"),
        ),
        check_vma=False,
    )
```

```python
import functools

import jax
import jax.numpy as jnp
from jax import lax
from jax.experimental import pallas as pl
from jax.experimental.pallas import tpu as pltpu
from jax.sharding import PartitionSpec as P

HEAD_DIM = 96
SLOTS = 4
LAYERS = 2
EPSILON = 1e-05
SCALING = HEAD_DIM ** (-0.5)
MIB = 1 << 20
f32 = jnp.float32
bf16 = jnp.bfloat16
VMEM = pl.BlockSpec(memory_space=pltpu.VMEM)
ANY = pl.BlockSpec(memory_space=pl.ANY)
HBM = pl.BlockSpec(memory_space=pltpu.HBM)


def norm_plain(v):
    mean = jnp.mean(v, axis=-1, keepdims=True)
    centred = v - mean
    inverse = lax.rsqrt(jnp.mean(centred * centred, axis=-1, keepdims=True) + EPSILON)
    return centred * inverse, inverse


def norm_back(u, normed, inverse):
    return inverse * (
        u
        - jnp.mean(u, axis=-1, keepdims=True)
        - normed * jnp.mean(u * normed, axis=-1, keepdims=True)
    )


def dot(a, b):
    return jnp.dot(a, b, preferred_element_type=f32)


def dot_nt(a, b):
    return lax.dot_general(a, b, (((1,), (1,)), ((), ())), preferred_element_type=f32)


def dot_tn(a, b):
    return lax.dot_general(a, b, (((0,), (0,)), ((), ())), preferred_element_type=f32)


def gelu_parts(x):
    half = 0.5 + 0.5 * lax.erf(x * (0.5**0.5))
    return x * half, half + x * jnp.exp(-0.5 * x * x) * (0.5 / jnp.pi) ** 0.5


def skip(kernel, inputs, extra):
    return lambda *refs: kernel(*refs[:inputs], *refs[inputs + extra :])


def shape(dims, kind=bf16):
    return jax.ShapeDtypeStruct(tuple(dims), kind)


def far(dims, kind=bf16):
    return pltpu.HBM(tuple(dims), kind)


def settings(mib, micros):
    return dict(
        compiler_params=pltpu.CompilerParams(vmem_limit_bytes=mib * MIB),
        cost_estimate=pl.CostEstimate(flops=int(micros * 1.15e9), bytes_accessed=1000, transcendentals=0),
    )


def hbm(v):
    return pltpu.with_memory_space_constraint(v, pltpu.HBM)


def fixed(dims, maps=None):
    return pl.BlockSpec(tuple(dims), maps or (lambda *i: (0,) * len(dims)), pipeline_mode=pl.Buffered(1))


def spread(v, heads):
    head = lax.broadcasted_iota(jnp.int32, v.shape, 1) // HEAD_DIM
    return jnp.concatenate([jnp.where(head == h, v, jnp.zeros_like(v)) for h in range(heads)], axis=0)


def gathered(v, heads):
    rows = v.shape[0] // heads
    head = lax.broadcasted_iota(jnp.int32, (rows, v.shape[1]), 1) // HEAD_DIM
    total = v[:rows]
    for h in range(1, heads):
        total = jnp.where(head == h, v[h * rows : (h + 1) * rows], total)
    return total


def on_core(run):
    core = lax.rem(lax.axis_index("frame"), 2)
    for value in (0, 1):
        pl.when(core == value)(functools.partial(run, value))


def put_halves(part, keep, send):
    half = part.shape[0] // 2
    halves = (part[:half].astype(bf16), part[half:].astype(bf16))

    def run(core):
        keep[...] = halves[core]
        send[...] = halves[1 - core]

    on_core(run)


def take_halves(dest, base, mine, other):
    half = mine.shape[0]

    def run(core):
        ordered = (mine, other) if core == 0 else (other, mine)
        for n in range(2):
            rows = slice(n * half, (n + 1) * half)
            dest[rows] = base[rows] + ordered[n][...].astype(f32) if base is not None else ordered[n][...].astype(f32)

    on_core(run)


def tie(v, after):
    return pl.pallas_call(
        lambda *refs: None,
        in_specs=[ANY] * (1 + len(after)),
        out_specs=ANY,
        out_shape=shape(v.shape, v.dtype),
        input_output_aliases={0: 0},
        **settings(1, 1),
    )(v, *after)


class Fetch:
    def __init__(self, sems):
        self.sems, self.used = sems, 0

    def __call__(self, src, dst):
        copy = pltpu.make_async_copy(src, dst, self.sems.at[self.used])
        self.used += 1
        copy.start()
        return copy


def media_kernel(frame, stamp, wide_k, wide_v, plain_out, inverse_out, *outs):
    plain, inverse = norm_plain(frame[...].astype(f32) + stamp[0])
    inverse_out[...] = jnp.broadcast_to(inverse, inverse_out.shape)
    plain = plain.astype(bf16)
    plain_out[...] = plain
    for l in range(LAYERS):
        outs[2 * l][...] = dot(plain, wide_k[l]).astype(bf16)
        outs[2 * l + 1][...] = dot(plain, wide_v[l]).astype(bf16)


def media_stage(frame, stamp, wide_k, wide_v, clips):
    rows, width = frame.shape
    own = wide_k.shape[2]
    patches = rows // clips
    piece = lambda w: pl.BlockSpec((patches, w), lambda i: (i, 0))
    return pl.pallas_call(
        media_kernel,
        grid=(clips,),
        in_specs=[piece(width), pl.BlockSpec((1, 1, width), lambda i: (i, 0, 0)), VMEM, VMEM],
        out_specs=[piece(width), piece(128)] + [piece(own)] * 4,
        out_shape=[far((rows, width)), far((rows, 128), f32)] + [far((rows, own))] * 4,
        **settings(14, 5),
    )(frame, stamp, wide_k, wide_v)


def fetch_keys(fetch, groups, ks, clips):
    copies = [[] for _ in range(clips)]
    at = 0
    for ref in groups:
        patches = ref.shape[0] // clips
        for c in range(clips):
            copies[c].append(fetch(ref.at[pl.ds(c * patches, patches)], ks.at[c, pl.ds(at, patches)]))
        at += patches
    return copies, at


def attn_kernel(l, clips, nf, first, *refs):
    if first:
        base, gain, wq, wk, wv, wo = refs[:6]
        refs = refs[6:]
    else:
        base, mine, other, gain, wq, wk, wv, wo = refs[:8]
        refs = refs[8:]
    frame_keys, frame_values = refs[:nf], refs[nf : 2 * nf]
    keep, send, lat_n_out, heads_out, soft_out = refs[2 * nf : 2 * nf + 5]
    wqs, wks, wvs, wos, ks, vs, soft_s, lat_n_s, heads_s, sems = refs[-10:]
    fetch = Fetch(sems)
    waits = [fetch(wq.at[l], wqs), fetch(wk.at[l], wks), fetch(wv.at[l], wvs)]
    key_copies, media_keys = fetch_keys(fetch, frame_keys, ks, clips)
    value_copies, _ = fetch_keys(fetch, frame_values, vs, clips)
    wo_copy = fetch(wo.at[l], wos)
    stores = []
    if first:
        lat = base
    else:
        lat, lat_out = refs[2 * nf + 5 : 2 * nf + 7]
        take_halves(lat, base, mine, other)
        stores.append(fetch(lat, lat_out))
    plain, _ = norm_plain(lat[...])
    lat_n = (plain * gain[l : l + 1, :]).astype(bf16)
    lat_n_s[...] = lat_n
    stores.append(fetch(lat_n_s, lat_n_out))
    heads = wqs.shape[1] // HEAD_DIM
    rows = lat_n.shape[0] // clips
    for copy in waits:
        copy.wait()
    q = dot(lat_n, wqs[...]).astype(bf16)
    kl = dot(lat_n, wks[...]).astype(bf16)
    vl = dot(lat_n, wvs[...]).astype(bf16)
    heads_s[0] = q
    heads_s[1] = kl
    heads_s[2] = vl
    atts = []
    for c in range(clips):
        part = slice(c * rows, (c + 1) * rows)
        ks[c, media_keys:] = kl[part]
        vs[c, media_keys:] = vl[part]
        for copy in key_copies[c]:
            copy.wait()
        scores = dot_nt(spread(q[part], heads), ks[c]) * SCALING
        ex = jnp.exp(scores - jnp.max(scores, axis=-1, keepdims=True))
        soft = (ex / jnp.sum(ex, axis=-1, keepdims=True)).astype(bf16)
        soft_s[c] = soft
        stores.append(fetch(soft_s.at[c], soft_out.at[c]))
        for copy in value_copies[c]:
            copy.wait()
        atts.append(gathered(dot(soft, vs[c]), heads).astype(bf16))
    att = jnp.concatenate(atts, axis=0)
    heads_s[3] = att
    stores.append(fetch(heads_s, heads_out))
    wo_copy.wait()
    put_halves(dot(att, wos[...]), keep, send)
    for copy in stores:
        copy.wait()


def attn_stage(l, clips, base, halves, gain, wq, wk, wv, wo, keys, values, after):
    rows, width = base.shape
    own = wq.shape[2]
    heads = own // HEAD_DIM
    nkeys = sum(k.shape[0] // clips for k in keys) + rows // clips
    soft = (clips, heads * rows // clips, nkeys)
    first = halves is None
    smalls = [base] + ([] if first else list(halves)) + [gain]
    outs = [shape((rows // 2, width)), shape((rows // 2, width)), far((rows, width)), far((4, rows, own)), far(soft)]
    specs = [VMEM] * 2 + [HBM] * 3
    if not first:
        outs += [shape((rows, width), f32), far((rows, width), f32)]
        specs += [VMEM, HBM]
    return pl.pallas_call(
        skip(functools.partial(attn_kernel, l, clips, len(keys), first), len(smalls) + 4 + 2 * len(keys), len(after)),
        in_specs=[VMEM] * len(smalls) + [HBM] * (4 + 2 * len(keys)) + [ANY] * len(after),
        out_specs=specs,
        out_shape=outs,
        scratch_shapes=[pltpu.VMEM((width, own), bf16)] * 3
        + [pltpu.VMEM((own, width), bf16)]
        + [pltpu.VMEM((clips, nkeys, own), bf16)] * 2
        + [pltpu.VMEM(soft, bf16), pltpu.VMEM((rows, width), bf16), pltpu.VMEM((4, rows, own), bf16)]
        + [pltpu.SemaphoreType.DMA((7 + clips + 2 * clips * len(keys),))],
        **settings(20, 9),
    )(*smalls, wq, wk, wv, wo, *keys, *values, *after)


def quarter(dest, src):
    count = dest.shape[0]
    at = lax.rem(lax.axis_index("frame"), src.shape[0] // count)
    dest[...] = src[pl.ds(pl.multiple_of(at * count, count), count), :]


def ffn_kernel(l, step, top, *refs):
    base, mine, other, gain, up, down = refs[:6]
    if top:
        gh_in, keep, send, middle, rows_out, middle_out, keep_back, send_back = refs[6:14]
        ups, downs, ffn_s, sems, gh_s = refs[14:]
    else:
        keep, send, middle, rows_out, middle_out, slope_out = refs[6:12]
        ups, downs, ffn_s, sems, slope_s = refs[12:]
    fetch = Fetch(sems)
    hidden_all = ups.shape[1]
    blocks = [pl.ds(n * step, step) for n in range(hidden_all // step)]
    up_copies = [fetch(up.at[l, :, b], ups.at[:, b]) for b in blocks]
    gh_copy = fetch(gh_in, gh_s) if top else None
    down_copies = [fetch(down.at[l, b], downs.at[b]) for b in blocks]
    take_halves(middle, base, mine, other)
    stores = [fetch(middle, middle_out)]
    plain, _ = norm_plain(middle[...])
    ffn_in = (plain * gain[l : l + 1, :]).astype(bf16)
    ffn_s[...] = ffn_in
    quarter(rows_out, ffn_s)
    if top:
        gh_copy.wait()
    hiddens, gpres = [], []
    for n, b in enumerate(blocks):
        up_copies[n].wait()
        hidden, slope = gelu_parts(dot(ffn_in, ups[:, b]))
        if top:
            gpres.append((slope * gh_s[:, b]).astype(bf16))
        else:
            slope_s[:, b] = slope.astype(bf16)
        hiddens.append(hidden.astype(bf16))
    if top:
        total = None
        for n, b in enumerate(blocks):
            part = dot_nt(gpres[n], ups[:, b])
            total = part if total is None else total + part
        put_halves(total, keep_back, send_back)
    else:
        stores.append(fetch(slope_s, slope_out))
    total = None
    for n, b in enumerate(blocks):
        down_copies[n].wait()
        part = dot(hiddens[n], downs[b, :])
        total = part if total is None else total + part
    put_halves(total, keep, send)
    for copy in stores:
        copy.wait()


def ffn_stage(l, nf, base, halves, gain, up, down, gh, after):
    rows, width = base.shape
    hidden = up.shape[2]
    step = 256
    top = len(gh) == 1
    half = shape((rows // 2, width))
    return pl.pallas_call(
        skip(functools.partial(ffn_kernel, l, step, top), 6 + len(gh), len(after)),
        in_specs=[VMEM] * 4 + [HBM] * (2 + len(gh)) + [ANY] * len(after),
        out_specs=[VMEM] * 4 + [HBM] + ([VMEM] * 2 if top else [HBM]),
        out_shape=[half, half, shape((rows, width), f32), shape((rows // nf, width)), far((rows, width), f32)]
        + ([half, half] if top else [far((rows, hidden))]),
        scratch_shapes=[
            pltpu.VMEM((width, hidden), bf16),
            pltpu.VMEM((hidden, width), bf16),
            pltpu.VMEM((rows, width), bf16),
            pltpu.SemaphoreType.DMA((2 * hidden // step + 2,)),
            pltpu.VMEM((rows, hidden), f32 if top else bf16),
        ],
        **settings(16, 6),
    )(base, *halves, gain, up, down, *gh, *after)


def top_kernel(l, step, base, living, down, grad, rows_out, gh, downs, gy_s, sems):
    fetch = Fetch(sems)
    blocks = [pl.ds(n * step, step) for n in range(downs.shape[0] // step)]
    down_copies = [fetch(down.at[l, b], downs.at[b]) for b in blocks]
    now = base[...] * living[...]
    grad[...] = now
    gy = now.astype(bf16)
    gy_s[...] = gy
    quarter(rows_out, gy_s)
    for n, b in enumerate(blocks):
        down_copies[n].wait()
        gh[:, b] = dot_nt(gy, downs[b, :])


def top_stage(nf, base, living, down):
    rows, width = base.shape
    hidden = down.shape[1]
    step = 256
    return pl.pallas_call(
        functools.partial(top_kernel, LAYERS - 1, step),
        in_specs=[VMEM] * 2 + [HBM],
        out_specs=[VMEM] * 3,
        out_shape=[shape((rows, width), f32), shape((rows // nf, width)), shape((rows, hidden), f32)],
        scratch_shapes=[
            pltpu.VMEM((hidden, width), bf16),
            pltpu.VMEM((rows, width), bf16),
            pltpu.SemaphoreType.DMA((hidden // step,)),
        ],
        **settings(12, 4),
    )(base, living, down)


def ffn_back_kernel(
    l, step, base, mine, other, gain, lat_in, slope_in, up, down, keep, send, rows_out, gain_grad, grad_out,
    ups, downs, slope_s, gy_s, sems, work, lat, grad_s,
):
    fetch = Fetch(sems)
    blocks = [pl.ds(n * step, step) for n in range(ups.shape[1] // step)]
    lat_copy = fetch(lat_in, lat)
    down_copies = [fetch(down.at[l, b], downs.at[b]) for b in blocks]
    slope_copy = fetch(slope_in, slope_s)
    up_copies = [fetch(up.at[l, :, b], ups.at[:, b]) for b in blocks]
    take_halves(work, None, mine, other)
    lat_copy.wait()
    now = latent_back(base, work, lat, gain, l + 1, gain_grad)
    grad_s[...] = now
    grad_copy = fetch(grad_s, grad_out)
    gy = now.astype(bf16)
    gy_s[...] = gy
    quarter(rows_out, gy_s)
    slope_copy.wait()
    gpres = []
    for n, b in enumerate(blocks):
        down_copies[n].wait()
        gpres.append((slope_s[:, b].astype(f32) * dot_nt(gy, downs[b, :])).astype(bf16))
    total = None
    for n, b in enumerate(blocks):
        up_copies[n].wait()
        part = dot_nt(gpres[n], ups[:, b])
        total = part if total is None else total + part
    put_halves(total, keep, send)
    grad_copy.wait()


def latent_back(base, work, lat, gain, l, gain_grad):
    plain, inverse = norm_plain(lat[...])
    arrived = work[...]
    gain_grad[...] = jnp.sum(arrived * plain, axis=0, keepdims=True)
    return base[...] + norm_back(arrived * gain[l : l + 1, :], plain, inverse)


def ffn_back_stage(l, nf, base, halves, gain, lat, slope, up, down, after):
    rows, width = base.shape
    hidden = up.shape[2]
    step = 256
    half = shape((rows // 2, width))
    return pl.pallas_call(
        skip(functools.partial(ffn_back_kernel, l, step), 8, len(after)),
        in_specs=[VMEM] * 4 + [HBM] * 4 + [ANY] * len(after),
        out_specs=[VMEM] * 4 + [HBM],
        out_shape=[half, half, shape((rows // nf, width)), shape((1, width), f32), far((rows, width), f32)],
        scratch_shapes=[
            pltpu.VMEM((width, hidden), bf16),
            pltpu.VMEM((hidden, width), bf16),
            pltpu.VMEM((rows, hidden), bf16),
            pltpu.VMEM((rows, width), bf16),
            pltpu.SemaphoreType.DMA((2 * hidden // step + 3,)),
        ]
        + [pltpu.VMEM((rows, width), f32)] * 3,
        **settings(16, 6),
    )(base, *halves, gain, lat, slope, up, down, *after)


def attn_back_kernel(l, clips, nf, mine, other, gain, base_in, middle_in, heads_in, soft_in, wo, wq, wk, wv, *refs):
    frame_keys, frame_values = refs[:nf], refs[nf : 2 * nf]
    keep, send, gmid_out, gain_grad, gupd_out, grads_out, gscore_out = refs[2 * nf : 2 * nf + 7]
    wqs, wks, wvs, wos, ks, vs, work, middle, base, heads_s, grads_s, gupd_s, soft_s, score_s, sems = refs[2 * nf + 7 :]
    fetch = Fetch(sems)
    middle_copy, base_copy = fetch(middle_in, middle), fetch(base_in, base)
    wo_copy = fetch(wo.at[l], wos)
    heads_copy = fetch(heads_in, heads_s)
    value_copies, media_keys = fetch_keys(fetch, frame_values, vs, clips)
    soft_copies = [fetch(soft_in.at[c], soft_s.at[c]) for c in range(clips)]
    key_copies, _ = fetch_keys(fetch, frame_keys, ks, clips)
    waits = [fetch(wq.at[l], wqs), fetch(wk.at[l], wks), fetch(wv.at[l], wvs)]
    take_halves(work, None, mine, other)
    middle_copy.wait()
    base_copy.wait()
    gmid = latent_back(base, work, middle, gain, l, gain_grad)
    gmid_out[...] = gmid
    gupd = gmid.astype(bf16)
    gupd_s[...] = gupd
    stores = [fetch(gupd_s, gupd_out)]
    heads = wqs.shape[1] // HEAD_DIM
    rows = gupd.shape[0] // clips
    wo_copy.wait()
    gatt = dot_nt(gupd, wos[...]).astype(bf16)
    heads_copy.wait()
    gqs, gkls, gvls = [], [], []
    for c in range(clips):
        part = slice(c * rows, (c + 1) * rows)
        ks[c, media_keys:] = heads_s[1, part]
        vs[c, media_keys:] = heads_s[2, part]
        qs = spread(heads_s[0, part], heads)
        gs = spread(gatt[part], heads)
        for copy in value_copies[c]:
            copy.wait()
        gsoft = dot_nt(gs, vs[c])
        soft_copies[c].wait()
        soft = soft_s[c]
        soft32 = soft.astype(f32)
        delta = jnp.sum(soft32 * gsoft, axis=-1, keepdims=True)
        gscore = (soft32 * (gsoft - delta)).astype(bf16)
        score_s[c] = gscore
        stores.append(fetch(score_s.at[c], gscore_out.at[c]))
        for copy in key_copies[c]:
            copy.wait()
        gqs.append(gathered(dot(gscore, ks[c]), heads) * SCALING)
        gkls.append(dot_tn(gscore[:, media_keys:], qs) * SCALING)
        gvls.append(dot_tn(soft[:, media_keys:], gs))
    gq = jnp.concatenate(gqs, axis=0).astype(bf16)
    gkl = jnp.concatenate(gkls, axis=0).astype(bf16)
    gvl = jnp.concatenate(gvls, axis=0).astype(bf16)
    grads_s[0] = gatt
    grads_s[1] = gq
    grads_s[2] = gkl
    grads_s[3] = gvl
    stores.append(fetch(grads_s, grads_out))
    for copy in waits:
        copy.wait()
    put_halves(dot_nt(gq, wqs[...]) + dot_nt(gkl, wks[...]) + dot_nt(gvl, wvs[...]), keep, send)
    for copy in stores:
        copy.wait()


def attn_back_stage(l, clips, base, halves, gain, middle, heads_all, soft, wo, wq, wk, wv, keys, values, after):
    rows, width = base.shape
    own = wq.shape[2]
    outs = [
        shape((rows // 2, width)),
        shape((rows // 2, width)),
        shape((rows, width), f32),
        shape((1, width), f32),
        far((rows, width)),
        far((4, rows, own)),
        far(soft.shape),
    ]
    nkeys = soft.shape[2]
    return pl.pallas_call(
        skip(functools.partial(attn_back_kernel, l, clips, len(keys)), 11 + 2 * len(keys), len(after)),
        in_specs=[VMEM] * 3 + [HBM] * (8 + 2 * len(keys)) + [ANY] * len(after),
        out_specs=[VMEM] * 4 + [HBM] * 3,
        out_shape=outs,
        scratch_shapes=[pltpu.VMEM((width, own), bf16)] * 3
        + [pltpu.VMEM((own, width), bf16)]
        + [pltpu.VMEM((clips, nkeys, own), bf16)] * 2
        + [pltpu.VMEM((rows, width), f32)] * 3
        + [pltpu.VMEM((4, rows, own), bf16)] * 2
        + [pltpu.VMEM((rows, width), bf16)]
        + [pltpu.VMEM(soft.shape, bf16)] * 2
        + [pltpu.SemaphoreType.DMA((9 + 2 * clips + 2 * clips * len(keys),))],
        **settings(25, 7),
    )(*halves, gain, base, middle, heads_all, soft, wo, wq, wk, wv, *keys, *values, *after)


def last_kernel(l, base, mine, other, lat, gain, *refs):
    grad, gain_grad, work = refs[-3:]
    take_halves(work, None, mine, other)
    grad[...] = latent_back(base, work, lat, gain, l, gain_grad)


def last_stage(base, halves, lat, gain, after):
    rows, width = base.shape
    return pl.pallas_call(
        functools.partial(last_kernel, 0),
        in_specs=[VMEM] * 5 + [ANY] * len(after),
        out_specs=[VMEM] * 2,
        out_shape=[shape((rows, width), f32), shape((1, width), f32)],
        scratch_shapes=[pltpu.VMEM((rows, width), f32)],
        **settings(12, 2),
    )(base, *halves, lat, gain, *after)


def proj_kernel(clips, cut, nf, lead, *refs):
    plains = refs[:nf]
    lat_n, gupd, wk, wv, gain, gscore, soft, heads_all, grads = refs[nf : nf + 9]
    media_gain, qs, gs = refs[-3:]
    outs = refs[nf + 9 : -3] if lead == 4 else refs[-5:-3]
    out, out_last = outs[-1] if lead == 4 else outs[0], outs[-1]
    _, total, own = heads_all.shape
    heads = own // HEAD_DIM
    rows = total // clips
    wide = heads * rows

    @pl.when(pl.program_id(0) == 0)
    def _():
        for c in range(clips):
            part = slice(c * rows, (c + 1) * rows)
            qs[c * wide : (c + 1) * wide] = (spread(heads_all[0, part], heads).astype(f32) * SCALING).astype(bf16)
            gs[c * wide : (c + 1) * wide] = spread(grads[0, part], heads)

    scale = gain[...]
    zs, ys = [], []
    for c in range(clips):
        z = y = None
        at = 0
        for plain in plains:
            patches = plain.shape[0] // clips
            block = plain[c * patches : (c + 1) * patches]
            part_z = dot(gscore[c, :, at : at + patches], block)
            part_y = dot(soft[c, :, at : at + patches], block)
            z = part_z if z is None else z + part_z
            y = part_y if y is None else y + part_y
            at += patches
        zs.append((z * scale).astype(bf16))
        ys.append((y * scale).astype(bf16))
    kg = dot_tn(jnp.concatenate(zs, axis=0), qs[...])
    vg = dot_tn(jnp.concatenate(ys, axis=0), gs[...])
    along = kg * wk[0].astype(f32) + vg * wv[0].astype(f32)
    along = jnp.broadcast_to(jnp.sum(along, axis=1, keepdims=True), (along.shape[0], 128))
    media_gain[...] = jnp.transpose(along)[:8] / scale
    lat_b = lat_n[...]
    kg = (kg + dot_tn(lat_b, grads[2])).astype(bf16)
    vg = (vg + dot_tn(lat_b, grads[3])).astype(bf16)
    qg = dot_tn(lat_b, grads[1]).astype(bf16)
    og = dot_tn(gupd[...], heads_all[3]).astype(bf16)
    for b in range(kg.shape[0] // cut):
        for n, grad in enumerate((kg, vg, qg, og)):
            dest = (out, n) if n < lead else (out_last, n - lead)
            dest[0][b, dest[1]] = grad[b * cut : (b + 1) * cut]


def proj_stage(l, lead, clips, nc, plains, lat_n, gupd, wk, wv, gain, gscore, soft, heads_all, grads, after):
    width = lat_n.shape[1]
    _, rows, own = heads_all.shape
    cut = width // nc
    block = 384
    per = block // cut
    heads = own // HEAD_DIM
    wide = heads * rows
    full = lambda v: fixed(v.shape)
    columns = lambda v: pl.BlockSpec(v.shape[:-1] + (block,), lambda i: (0,) * (v.ndim - 1) + (i,))
    weight = pl.BlockSpec((1, block, own), lambda i: (l, i, 0))
    return pl.pallas_call(
        functools.partial(proj_kernel, clips, cut, len(plains), lead),
        grid=(width // block,),
        in_specs=[columns(v) for v in plains]
        + [columns(lat_n), columns(gupd), weight, weight, columns(gain)]
        + [full(v) for v in (gscore, soft, heads_all, grads)]
        + [ANY] * len(after),
        out_specs=[pl.BlockSpec((per, n, cut, own), lambda i: (i, 0, 0, 0)) for n in (lead, 4 - lead) if n]
        + [pl.BlockSpec((8, block), lambda i: (0, i))],
        out_shape=[shape((nc, n, cut, own)) for n in (lead, 4 - lead) if n] + [shape((8, width), f32)],
        scratch_shapes=[pltpu.VMEM((wide, own), bf16)] * 2,
        **settings(22, 12),
    )(*plains, lat_n, gupd, wk, wv, gain, gscore, soft, heads_all, grads, *after)


def media_back_kernel(frames, *refs):
    count = 2 * LAYERS
    tables, firsts, weights = refs[:count], refs[count : 2 * count], refs[2 * count : 2 * count + 2]
    out, sums, stack = refs[-3:]
    norms = refs[2 * count + 2 : 2 * count + 2 + 2 * frames]

    @pl.when(pl.program_id(1) == 0)
    def _():
        own = weights[0].shape[2]
        heads = own // HEAD_DIM
        for n in range(count):
            l = n // 2
            v = firsts[n][0]
            if n % 2 == 0:
                v = (v.astype(f32) * SCALING).astype(bf16)
            across = dot_nt(spread(v, heads), weights[n % 2][l])
            rows = across.shape[0]
            stack[n * rows : (n + 1) * rows] = across.astype(bf16)

    left = jnp.concatenate([t[0] for t in tables], axis=0)
    u = dot_tn(left, stack[...])
    out[0] = u.astype(bf16)
    mean = jnp.mean(u, axis=-1, keepdims=True)
    for n in range(frames):

        @pl.when(pl.program_id(1) == n)
        def _():
            plain, inverse = norms[2 * n][...].astype(f32), norms[2 * n + 1][:, :1]
            along = jnp.mean(u * plain, axis=-1, keepdims=True)
            sums[0, 0] = jnp.sum(inverse * (u - mean - plain * along), axis=0, keepdims=True)


def media_back_stage(first_frame, frames, clips, patches, tables, firsts, wk, wv, ready, after):
    width = wk.shape[1]
    table = pl.BlockSpec((1, tables[0].shape[1], patches), lambda c, r: (c, 0, first_frame + r))
    _, rows, own = firsts[0].shape
    piece = pl.BlockSpec((1, rows // clips, own), lambda c, r: (0, c, 0))
    full = lambda v: fixed(v.shape)
    norms = [hbm(v) for made in ready for v in made[:2]]
    norm_piece = lambda v: pl.BlockSpec((patches, v.shape[1]), lambda c, r: (c, 0))
    return pl.pallas_call(
        functools.partial(media_back_kernel, frames),
        grid=(clips, frames),
        in_specs=[table] * 4 + [piece] * 4 + [full(wk), full(wv)] + [norm_piece(v) for v in norms] + [ANY] * len(after),
        out_specs=[
            pl.BlockSpec((1, patches, width), lambda c, r: (r, c, 0)),
            pl.BlockSpec((1, 1, 1, width), lambda c, r: (r, c, 0, 0)),
        ],
        out_shape=[shape((frames, clips * patches, width)), shape((frames, clips, 1, width), f32)],
        scratch_shapes=[pltpu.VMEM((4 * tables[0].shape[1], width), bf16)],
        **settings(28, 9),
    )(*tables, *firsts, wk, wv, *norms, *after)


def media_last_kernel(count, media, stamp, *refs):
    parts, out = refs[:count], refs[-1]
    plain, inverse = norm_plain(media[...].astype(f32) + stamp[0])
    u = parts[0][...].astype(f32)
    for part in parts[1:]:
        u = u + part[...].astype(f32)
    out[...] = norm_back(u, plain, inverse)


def media_last_stage(media, stamp, parts, clips, after):
    rows, width = media.shape
    step = 128
    per = rows // clips // step
    piece = pl.BlockSpec((step, width), lambda i: (i, 0))
    clip = pl.BlockSpec((1, 1, width), lambda i: (i // per, 0, 0))
    return pl.pallas_call(
        functools.partial(media_last_kernel, len(parts)),
        grid=(rows // step,),
        in_specs=[piece, clip] + [piece] * len(parts) + [ANY] * len(after),
        out_specs=piece,
        out_shape=shape((rows, width), f32),
        **settings(20, 5),
    )(media, stamp, *parts, *after)


def own_columns(dest, src, nc):
    cut = dest.shape[1]
    block = 384
    at = lax.axis_index("clip") * cut
    wide = src[:, :, pl.ds(pl.multiple_of(at // block * block, block), block)].reshape(-1, block)
    for n in range(block // cut):

        @pl.when(lax.rem(at, block) == n * cut)
        def _():
            dest[...] = wide[:, n * cut : (n + 1) * cut]


def fetch_rows(fetch, refs, at, dest, chunk):
    each, rows, _ = dest.shape
    copies = []
    if len(refs) > 1:
        count = rows // len(refs)
        for r, ref in enumerate(refs):
            place = pl.ds(pl.multiple_of((lax.axis_index("frame") ^ r) * count, count), count)
            copies.append(fetch(ref.at[pl.ds(chunk * each, each)], dest.at[:, place]))
    else:
        nf = lax.axis_size("frame")
        count = rows // nf
        for c in range(each):
            for f in range(nf):
                source = refs[0].at[(chunk * each + c) * nf + f, pl.ds(at * count, count)]
                copies.append(fetch(source, dest.at[c, pl.ds(f * count, count)]))
    return copies


def ffn_grad_kernel(counts, shares, nc, *refs):
    rows_refs, grads_refs = refs[: counts[0]], refs[counts[0] : sum(counts)]
    up, down = refs[sum(counts) : sum(counts) + 2]
    up_grad, down_grad, rows_all, grads_all, rows_own, grads_own, sems = refs[-7:]
    chunk = pl.program_id(1)
    flat = lambda ref: ref[...].reshape(-1, ref.shape[2])

    @pl.when(jnp.logical_or(pl.program_id(0) == 0, pl.num_programs(1) > 1))
    def _():
        fetch = Fetch(sems)
        copies = fetch_rows(fetch, rows_refs, shares[0], rows_all, chunk)
        copies += fetch_rows(fetch, grads_refs, shares[1], grads_all, chunk)
        for copy in copies:
            copy.wait()
        own_columns(rows_own, rows_all, nc)
        own_columns(grads_own, grads_all, nc)

    step = up.shape[2]
    width = min(step, 256)
    halves = [slice(n, n + width) for n in range(0, step, width)]
    pres = [dot(flat(rows_all), up[0, :, b]) for b in halves]
    ghs = [dot_nt(flat(grads_all), down[0, b, :]) for b in halves]
    for n, b in enumerate(halves):
        hidden, slope = gelu_parts(pres[n])
        gpre = (slope * ghs[n]).astype(bf16)
        up_part = dot_tn(rows_own[...], gpre)
        down_part = dot_tn(grads_own[...], hidden.astype(bf16))

        @pl.when(chunk == 0)
        def _():
            up_grad[0, :, b] = up_part
            down_grad[0, :, b] = down_part

        @pl.when(chunk > 0)
        def _():
            up_grad[0, :, b] += up_part
            down_grad[0, :, b] += down_part


def ffn_grad_stage(l, nc, count, rows, grads, shares, up, down, earlier, after):
    width = rows[0].shape[2]
    cut = width // nc
    hidden = up.shape[2]
    step = 512 if hidden % 512 == 0 else 256
    each = min(nc, 1024 // count)
    outs = [shape((LAYERS, cut, hidden), f32)] * 2
    arrays = [hbm(v) for v in list(rows) + list(grads)]
    known = len(arrays) + 2
    return pl.pallas_call(
        functools.partial(ffn_grad_kernel, (len(rows), len(grads)), shares, nc),
        grid=(hidden // step, nc // each),
        in_specs=[HBM] * len(arrays)
        + [
            pl.BlockSpec((1, width, step), lambda j, i: (l, 0, j)),
            pl.BlockSpec((1, step, width), lambda j, i: (l, j, 0)),
        ]
        + [ANY] * (len(earlier) + len(after)),
        out_specs=[
            pl.BlockSpec((1, cut, step), lambda j, i: (l, 0, j)),
            pl.BlockSpec((1, cut, step), lambda j, i: (l, 0, j)),
        ],
        out_shape=outs,
        input_output_aliases={known: 0, known + 1: 1} if earlier else {},
        scratch_shapes=[pltpu.VMEM((each, count, width), bf16)] * 2
        + [pltpu.VMEM((each * count, cut), bf16)] * 2
        + [pltpu.SemaphoreType.DMA((2 * each * lax.axis_size("frame"),))],
        **settings(40, 14),
    )(*arrays, up, down, *earlier, *after)


def swap(v, axis, bit):
    size = lax.axis_size(axis)
    return lax.ppermute(v, axis, [(i, i ^ bit) for i in range(size)])


def bits_of(size):
    out, bit = [], 1
    while bit < size:
        out.append(bit)
        bit *= 2
    return out


def add_kernel(mine, arrived, *refs):
    refs[-1][...] = (mine[...].astype(f32) + arrived[...].astype(f32)).astype(bf16)


def add_after(mine, arrived, after):
    return pl.pallas_call(
        add_kernel,
        in_specs=[VMEM] * 2 + [ANY] * len(after),
        out_specs=VMEM,
        out_shape=shape(mine.shape),
        **settings(4, 1),
    )(mine, arrived, *after)


def frame_sum(keep, send, fill=None):
    mine = (keep.astype(f32) + swap(send, "frame", 1).astype(f32)).astype(bf16)
    made = None
    for bit in bits_of(lax.axis_size("frame"))[1:]:
        arrived = swap(mine, "frame", bit)
        if fill is not None and made is None:
            made = fill((mine,))
            mine = add_after(mine, arrived, made)
        else:
            mine = (mine.astype(f32) + arrived.astype(f32)).astype(bf16)
    return (mine, swap(mine, "frame", 1)) if fill is None else ((mine, swap(mine, "frame", 1)), made)


class Scatter:
    def __init__(self, parts, bits, clip_here):
        self.pieces = [parts.reshape((2,) * len(bits) + parts.shape[1:])]
        self.bits, self.left, self.clip_here = list(bits), sorted(bits, reverse=True), clip_here

    def send(self):
        bit = self.bits.pop(0)
        axis = self.left.index(bit)
        self.left.remove(bit)
        mine = (self.clip_here // bit) % 2
        pick = lambda v, n: lax.dynamic_index_in_dim(v, n, axis, keepdims=False)
        self.sent = sum(pick(v, 1 - mine).astype(f32) for v in self.pieces).astype(bf16)
        self.pieces = [pick(v, mine) for v in self.pieces]
        self.arriving = swap(self.sent, "clip", bit)
        return self

    def step(self, after):
        if self.arriving is None:
            return
        self.pieces.append(tie(self.arriving, after) if after else self.arriving)
        self.arriving = None
        if self.bits:
            self.send()

    @property
    def total(self):
        return sum(v.astype(f32) for v in self.pieces)


def gather_rows(shares):
    return lax.all_gather(jnp.concatenate(shares, axis=0), ("clip", "frame"), axis=0)


def exchange_rows(share, nc):
    return lax.all_to_all(jnp.broadcast_to(share, (nc,) + share.shape), "clip", 0, 0, tiled=True)


def spread_rows(mine, first_gate, second_gate):
    pieces = {0: tie(mine, first_gate)}
    for bit in bits_of(lax.axis_size("frame"))[::-1]:
        for r in list(pieces):
            arrived = swap(pieces[r], "frame", bit)
            pieces[r | bit] = tie(arrived, second_gate) if bit > 1 else arrived
    return [pieces[r] for r in range(len(pieces))]


def on_device(
    media, frame_order, clip_counts, latents, time_embed, media_gain, latent_gain, ffn_gain,
    query_weight, key_weight, value_weight, out_weight, up_weight, down_weight, cotangent,
):
    clips, _, patches, width = media.shape
    lat_rows = latents.shape[1]
    nf = lax.axis_size("frame")
    nc = lax.axis_size("clip")
    frame_here = lax.axis_index("frame")
    clip_here = lax.axis_index("clip")
    rows = clips * lat_rows

    key_plain, value_plain = key_weight, value_weight
    query_weight, key_weight, value_weight, out_weight, up_weight, down_weight = (
        pltpu.with_memory_space_constraint(w, pltpu.HBM)
        for w in (query_weight, key_weight, value_weight, out_weight, up_weight, down_weight)
    )
    clip_ids = clip_here * clips + jnp.arange(clips, dtype=jnp.int32)
    owner_match = (clip_ids // SLOTS)[:, None] == jnp.arange(clip_counts.shape[0], dtype=jnp.int32)[None, :]
    owner_count = jnp.sum(jnp.where(owner_match, clip_counts[None, :], 0), axis=1)
    living = (clip_ids % SLOTS < owner_count).astype(f32)
    living = jnp.repeat(living, lat_rows)[:, None]

    flat = media.reshape(clips * patches, width)
    top = nf // 2
    frames = {0: flat}
    if top > 1:
        frames[top] = swap(flat, "frame", top)
    for bit in bits_of(top)[::-1]:
        for r in [r for r in frames if r < top]:
            frames[r | bit] = swap(frames[r], "frame", bit)
    times = jnp.arange(nf, dtype=jnp.int32)
    order = jnp.stack(
        [lax.dynamic_index_in_dim(frame_order, frame_here ^ r, 1, keepdims=False) for r in range(nf)]
    )
    onehot = (order[:, :, None] == times).astype(f32)
    stamps = jnp.sum(onehot[..., None] * time_embed, axis=2)[:, :, None, :]
    wide_k = (media_gain[:, :, None] * key_plain.astype(f32)).astype(bf16)
    wide_v = (media_gain[:, :, None] * value_plain.astype(f32)).astype(bf16)
    ready = [media_stage(frames[r], stamps[r], wide_k, wide_v, clips) for r in range(top)]
    last = LAYERS - 1
    grad, top_share, gh = top_stage(nf, cotangent.reshape(rows, width), living, down_weight)
    frames[top] = tie(frames[top], [made[0] for made in ready] + [gh])
    for bit in bits_of(top)[::-1]:
        for r in [r for r in frames if r >= top]:
            frames[r | bit] = swap(frames[r], "frame", bit)
    ready += [media_stage(frames[r], stamps[r], wide_k, wide_v, clips) for r in range(top, nf)]
    plains = [hbm(g[0]) for g in ready]

    stored, ffn_shares = [], []
    current, halves = latents.reshape(rows, width), None
    for l in range(LAYERS):
        keys = [hbm(g[2 + 2 * l]) for g in ready]
        values = [hbm(g[3 + 2 * l]) for g in ready]
        out = attn_stage(
            l, clips, current, halves, latent_gain, query_weight, key_weight, value_weight, out_weight, keys, values, ()
        )
        keep, send, lat_n, heads_all, soft = out[:5]
        lat, lat_far = (current, None) if halves is None else (out[5], hbm(out[6]))
        halves = frame_sum(keep, send)
        gh_here = (hbm(gh),) if l == last else ()
        out = ffn_stage(l, nf, lat, halves, ffn_gain, up_weight, down_weight, gh_here, ())
        keep, send, current, share, middle = out[:5]
        ffn_shares.append(share)
        if l < last:
            slope = out[5]
        else:
            slope, (keep_back, send_back) = middle, out[5:]
            early = gather_rows(ffn_shares + [top_share])
        halves = frame_sum(keep, send) if l < last else None
        stored.append((keys, values, lat_far, hbm(lat_n), hbm(heads_all), hbm(soft), hbm(middle), hbm(slope)))
    forward_keep, forward_send = keep, send
    lat_gain_grads, ffn_gain_grads, media_gain_grads = [None] * LAYERS, [None] * LAYERS, [None] * LAYERS
    projs, tables, firsts = [None] * LAYERS, [None] * LAYERS, [None] * LAYERS

    def attend_back(l, grad, halves, lead, before, between):
        keys, values, _, lat_n, heads_all, soft, middle, _ = stored[l]
        keep, send, gmid, ffn_gain_grads[l], gupd, grads, gscore = attn_back_stage(
            l, clips, hbm(grad), halves, ffn_gain, middle, heads_all, soft, out_weight, query_weight, key_weight,
            value_weight, keys, values, before,
        )
        gupd, grads, gscore = hbm(gupd), hbm(grads), hbm(gscore)
        tables[l], firsts[l] = (gscore, soft), (heads_all, grads)

        def projections(after):
            return proj_stage(
                l, lead, clips, nc, plains, lat_n, gupd, key_weight, value_weight, media_gain[l : l + 1], gscore, soft,
                heads_all, grads, after + between,
            )

        halves, (*projs[l], along) = frame_sum(keep, send, projections)
        media_gain_grads[l] = along[:1]
        return gmid, halves

    def scattered(l):
        bits = bits_of(nc)
        orders = (bits, bits[1:] + bits[:1])
        return [Scatter(v, order, clip_here).send() for v, order in zip(projs[l], orders)]

    back_halves = frame_sum(keep_back, send_back)
    gmid, halves = attend_back(1, grad, back_halves, 3, (), ())
    upper = scattered(1)
    keep, send, share, lat_gain_grads[1], grad = ffn_back_stage(
        0, nf, gmid, halves, latent_gain, stored[1][2], stored[0][7], up_weight, down_weight, (),
    )
    lower_grads = exchange_rows(share, nc)
    halves = frame_sum(keep, send)
    gmid, halves = attend_back(0, grad, halves, 3, (), ())
    lower = scattered(0)
    forward = frame_sum(tie(forward_keep, (gmid,)), tie(forward_send, (gmid,)))
    core = frame_here % 2
    first = jnp.where(core == 0, forward[0], forward[1])
    second = jnp.where(core == 0, forward[1], forward[0])
    latents_out = (current + jnp.concatenate([first, second], axis=0).astype(f32)) * living


    half = nf // 2
    tables = [t for pair in tables for t in pair]
    firsts = [t for pair in firsts for t in pair]
    u = {}
    part, far_sums = media_back_stage(
        half, half, clips, patches, tables, firsts, wide_k, wide_v, ready[half:], (lower[0].sent, lower[1].sent)
    )
    for r in range(half):
        u[half + r] = [part[r]]
    for part_sum in upper:
        part_sum.step((part,))
    gate = tuple(part_sum.sent for part_sum in upper)
    latents_grad, lat_gain_grads[0] = last_stage(gmid, halves, latents.reshape(rows, width), latent_gain, gate)
    merged = lambda v: v[0] if len(v) == 1 else sum(x.astype(f32) for x in v).astype(bf16)

    def fold(bits, least):
        for bit in bits:
            for r in [r for r in u if r & bit and r >= least]:
                u[r ^ bit].append(swap(merged(u.pop(r)), "frame", bit))

    fold(bits_of(half), half)
    sent = merged(u.pop(half))
    lower_mine = tie(lower_grads, (far_sums,))
    arrived = swap(sent, "frame", half)
    part, near_sums = media_back_stage(
        0, half, clips, patches, tables, firsts, wide_k, wide_v, ready[:half], (sent, latents_grad, lower_mine)
    )
    for r in range(half):
        u[r] = [part[r]]
    fold(bits_of(half), 0)
    gate = (part,)
    ffn_parts = ffn_grad_stage(1, nc, rows, (early,), (early,), (1, 2), up_weight, down_weight, (), gate)
    gate = (ffn_parts[0],)
    for part_sum in upper + lower:
        part_sum.step(gate)
    lower_grads = spread_rows(lower_mine, (near_sums,), (ffn_parts[0],))
    up_grad, down_grad = ffn_grad_stage(
        0, nc, rows, (early,), lower_grads, (0, 0), up_weight, down_weight, ffn_parts,
        (lower[0].sent, lower[1].sent, upper[0].sent, upper[1].sent),
    )
    gate = (up_grad,)
    for part_sum in lower + upper:
        part_sum.step(gate)
    media_grad = media_last_stage(
        flat, stamps[0], u[0] + [tie(arrived, gate)], clips,
        (lower[0].sent, lower[1].sent, upper[0].pieces[-1], upper[1].pieces[-1]),
    )
    for part_sum in upper + lower:
        part_sum.step((media_grad,))
    for scatter in upper + lower:
        while scatter.arriving is not None:
            scatter.step(())
    sums = jnp.concatenate([near_sums, far_sums], axis=0)
    time_part = jnp.einsum("rct,rcd->td", onehot, sums[:, :, 0], precision=lax.Precision.HIGHEST)

    n_all = nc * nf
    narrow = jnp.concatenate([time_part] + media_gain_grads, axis=0)
    narrow = narrow.reshape(nf + 2, n_all, width // n_all).transpose(1, 0, 2).reshape(n_all, -1)
    broad = jnp.concatenate(lat_gain_grads + ffn_gain_grads, axis=0)
    broad = broad.reshape(4, nc, width // nc).transpose(1, 0, 2).reshape(nc, 1, -1)
    broad = broad * (jnp.arange(nf) == frame_here).astype(f32)[None, :, None]
    packed = tie(jnp.concatenate([narrow, broad.reshape(n_all, -1)], axis=1), (ffn_parts[0],))
    packed = jnp.sum(lax.all_to_all(packed, ("clip", "frame"), 0, 0, tiled=True), axis=0)
    edge = (nf + 2) * (width // n_all)
    narrow = packed[:edge].reshape(nf + 2, -1)
    broad = packed[edge:].reshape(4, -1)

    totals = [jnp.concatenate([part.total for part in pair], axis=0) for pair in (lower, upper)]
    pick = lambda n: jnp.stack([total[n] for total in totals])
    return (
        latents_out.reshape(latents.shape),
        media_grad.reshape(media.shape),
        latents_grad.reshape(latents.shape),
        narrow[:nf],
        narrow[nf:],
        broad[:2],
        broad[2:],
        pick(2),
        pick(0),
        pick(1),
        jnp.swapaxes(pick(3), 1, 2),
        up_grad,
        jnp.swapaxes(down_grad, 1, 2),
    )


def solution(mesh):
    return jax.shard_map(
        on_device,
        mesh=mesh,
        in_specs=(
            P("clip", "frame", None, None),
            P("clip", None),
            P(),
            P("clip", None, None),
            P(),
            P(),
            P(),
            P(),
            P(None, None, "frame"),
            P(None, None, "frame"),
            P(None, None, "frame"),
            P(None, "frame", None),
            P(None, None, "frame"),
            P(None, "frame", None),
            P("clip", None, None),
        ),
        out_specs=(
            P("clip", None, None),
            P("clip", "frame", None, None),
            P("clip", None, None),
            P(None, ("clip", "frame")),
            P(None, ("clip", "frame")),
            P(None, "clip"),
            P(None, "clip"),
            P(None, "clip", "frame"),
            P(None, "clip", "frame"),
            P(None, "clip", "frame"),
            P(None, "frame", "clip"),
            P(None, "clip", "frame"),
            P(None, "frame", "clip"),
        ),
        check_vma=False,
    )
```

```python
import functools

import jax
import jax.numpy as jnp
from jax import lax
from jax.experimental import pallas as pl
from jax.experimental.pallas import tpu as pltpu
from jax.sharding import PartitionSpec as P

HEAD_DIM = 96
SLOTS = 4
LAYERS = 2
EPSILON = 1e-05
SCALING = HEAD_DIM ** (-0.5)
MIB = 1 << 20
f32 = jnp.float32
bf16 = jnp.bfloat16
VMEM = pl.BlockSpec(memory_space=pltpu.VMEM)
ANY = pl.BlockSpec(memory_space=pl.ANY)
HBM = pl.BlockSpec(memory_space=pltpu.HBM)


def norm_plain(v):
    mean = jnp.mean(v, axis=-1, keepdims=True)
    centred = v - mean
    inverse = lax.rsqrt(jnp.mean(centred * centred, axis=-1, keepdims=True) + EPSILON)
    return centred * inverse, inverse


def norm_back(u, normed, inverse):
    return inverse * (
        u
        - jnp.mean(u, axis=-1, keepdims=True)
        - normed * jnp.mean(u * normed, axis=-1, keepdims=True)
    )


def dot(a, b):
    return jnp.dot(a, b, preferred_element_type=f32)


def dot_nt(a, b):
    return lax.dot_general(a, b, (((1,), (1,)), ((), ())), preferred_element_type=f32)


def dot_tn(a, b):
    return lax.dot_general(a, b, (((0,), (0,)), ((), ())), preferred_element_type=f32)


def gelu_parts(x):
    half = 0.5 + 0.5 * lax.erf(x * (0.5**0.5))
    return x * half, half + x * jnp.exp(-0.5 * x * x) * (0.5 / jnp.pi) ** 0.5


def skip(kernel, inputs, extra):
    return lambda *refs: kernel(*refs[:inputs], *refs[inputs + extra :])


def shape(dims, kind=bf16):
    return jax.ShapeDtypeStruct(tuple(dims), kind)


def far(dims, kind=bf16):
    return pltpu.HBM(tuple(dims), kind)


def settings(mib, micros):
    return dict(
        compiler_params=pltpu.CompilerParams(vmem_limit_bytes=mib * MIB),
        cost_estimate=pl.CostEstimate(flops=int(micros * 1.15e9), bytes_accessed=1000, transcendentals=0),
    )


def hbm(v):
    return pltpu.with_memory_space_constraint(v, pltpu.HBM)


def fixed(dims, maps=None):
    return pl.BlockSpec(tuple(dims), maps or (lambda *i: (0,) * len(dims)), pipeline_mode=pl.Buffered(1))


def spread(v, heads):
    head = lax.broadcasted_iota(jnp.int32, v.shape, 1) // HEAD_DIM
    return jnp.concatenate([jnp.where(head == h, v, jnp.zeros_like(v)) for h in range(heads)], axis=0)


def gathered(v, heads):
    rows = v.shape[0] // heads
    head = lax.broadcasted_iota(jnp.int32, (rows, v.shape[1]), 1) // HEAD_DIM
    total = v[:rows]
    for h in range(1, heads):
        total = jnp.where(head == h, v[h * rows : (h + 1) * rows], total)
    return total


def on_core(run):
    core = lax.rem(lax.axis_index("frame"), 2)
    for value in (0, 1):
        pl.when(core == value)(functools.partial(run, value))


def put_halves(part, keep, send):
    half = part.shape[0] // 2
    halves = (part[:half].astype(bf16), part[half:].astype(bf16))

    def run(core):
        keep[...] = halves[core]
        send[...] = halves[1 - core]

    on_core(run)


def take_halves(dest, base, mine, other):
    half = mine.shape[0]

    def run(core):
        ordered = (mine, other) if core == 0 else (other, mine)
        for n in range(2):
            rows = slice(n * half, (n + 1) * half)
            dest[rows] = base[rows] + ordered[n][...].astype(f32) if base is not None else ordered[n][...].astype(f32)

    on_core(run)


def tie(v, after):
    return pl.pallas_call(
        lambda *refs: None,
        in_specs=[ANY] * (1 + len(after)),
        out_specs=ANY,
        out_shape=shape(v.shape, v.dtype),
        input_output_aliases={0: 0},
        **settings(1, 1),
    )(v, *after)


class Fetch:
    def __init__(self, sems):
        self.sems, self.used = sems, 0

    def __call__(self, src, dst):
        copy = pltpu.make_async_copy(src, dst, self.sems.at[self.used])
        self.used += 1
        copy.start()
        return copy


def media_kernel(frame, stamp, wide_k, wide_v, plain_out, inverse_out, *outs):
    plain, inverse = norm_plain(frame[...].astype(f32) + stamp[0])
    inverse_out[...] = jnp.broadcast_to(inverse, inverse_out.shape)
    plain = plain.astype(bf16)
    plain_out[...] = plain
    for l in range(LAYERS):
        outs[2 * l][...] = dot(plain, wide_k[l]).astype(bf16)
        outs[2 * l + 1][...] = dot(plain, wide_v[l]).astype(bf16)


def media_stage(frame, stamp, wide_k, wide_v, clips):
    rows, width = frame.shape
    own = wide_k.shape[2]
    patches = rows // clips
    piece = lambda w: pl.BlockSpec((patches, w), lambda i: (i, 0))
    return pl.pallas_call(
        media_kernel,
        grid=(clips,),
        in_specs=[piece(width), pl.BlockSpec((1, 1, width), lambda i: (i, 0, 0)), VMEM, VMEM],
        out_specs=[piece(width), piece(128)] + [piece(own)] * 4,
        out_shape=[far((rows, width)), far((rows, 128), f32)] + [far((rows, own))] * 4,
        **settings(14, 5),
    )(frame, stamp, wide_k, wide_v)


def fetch_keys(fetch, groups, ks, clips):
    copies = [[] for _ in range(clips)]
    at = 0
    for ref in groups:
        patches = ref.shape[0] // clips
        for c in range(clips):
            copies[c].append(fetch(ref.at[pl.ds(c * patches, patches)], ks.at[c, pl.ds(at, patches)]))
        at += patches
    return copies, at


def attn_kernel(l, clips, nf, first, *refs):
    if first:
        base, gain, wq, wk, wv, wo = refs[:6]
        refs = refs[6:]
    else:
        base, mine, other, gain, wq, wk, wv, wo = refs[:8]
        refs = refs[8:]
    frame_keys, frame_values = refs[:nf], refs[nf : 2 * nf]
    keep, send, lat_n_out, heads_out, soft_out = refs[2 * nf : 2 * nf + 5]
    wqs, wks, wvs, wos, ks, vs, soft_s, lat_n_s, heads_s, sems = refs[-10:]
    fetch = Fetch(sems)
    waits = [fetch(wq.at[l], wqs), fetch(wk.at[l], wks), fetch(wv.at[l], wvs)]
    key_copies, media_keys = fetch_keys(fetch, frame_keys, ks, clips)
    value_copies, _ = fetch_keys(fetch, frame_values, vs, clips)
    wo_copy = fetch(wo.at[l], wos)
    stores = []
    if first:
        lat = base
    else:
        lat, lat_out = refs[2 * nf + 5 : 2 * nf + 7]
        take_halves(lat, base, mine, other)
        stores.append(fetch(lat, lat_out))
    plain, _ = norm_plain(lat[...])
    lat_n = (plain * gain[l : l + 1, :]).astype(bf16)
    lat_n_s[...] = lat_n
    stores.append(fetch(lat_n_s, lat_n_out))
    heads = wqs.shape[1] // HEAD_DIM
    rows = lat_n.shape[0] // clips
    for copy in waits:
        copy.wait()
    q = dot(lat_n, wqs[...]).astype(bf16)
    kl = dot(lat_n, wks[...]).astype(bf16)
    vl = dot(lat_n, wvs[...]).astype(bf16)
    heads_s[0] = q
    heads_s[1] = kl
    heads_s[2] = vl
    atts = []
    for c in range(clips):
        part = slice(c * rows, (c + 1) * rows)
        ks[c, media_keys:] = kl[part]
        vs[c, media_keys:] = vl[part]
        for copy in key_copies[c]:
            copy.wait()
        scores = dot_nt(spread(q[part], heads), ks[c]) * SCALING
        ex = jnp.exp(scores - jnp.max(scores, axis=-1, keepdims=True))
        soft = (ex / jnp.sum(ex, axis=-1, keepdims=True)).astype(bf16)
        soft_s[c] = soft
        stores.append(fetch(soft_s.at[c], soft_out.at[c]))
        for copy in value_copies[c]:
            copy.wait()
        atts.append(gathered(dot(soft, vs[c]), heads).astype(bf16))
    att = jnp.concatenate(atts, axis=0)
    heads_s[3] = att
    stores.append(fetch(heads_s, heads_out))
    wo_copy.wait()
    put_halves(dot(att, wos[...]), keep, send)
    for copy in stores:
        copy.wait()


def attn_stage(l, clips, base, halves, gain, wq, wk, wv, wo, keys, values, after):
    rows, width = base.shape
    own = wq.shape[2]
    heads = own // HEAD_DIM
    nkeys = sum(k.shape[0] // clips for k in keys) + rows // clips
    soft = (clips, heads * rows // clips, nkeys)
    first = halves is None
    smalls = [base] + ([] if first else list(halves)) + [gain]
    outs = [shape((rows // 2, width)), shape((rows // 2, width)), far((rows, width)), far((4, rows, own)), far(soft)]
    specs = [VMEM] * 2 + [HBM] * 3
    if not first:
        outs += [shape((rows, width), f32), far((rows, width), f32)]
        specs += [VMEM, HBM]
    return pl.pallas_call(
        skip(functools.partial(attn_kernel, l, clips, len(keys), first), len(smalls) + 4 + 2 * len(keys), len(after)),
        in_specs=[VMEM] * len(smalls) + [HBM] * (4 + 2 * len(keys)) + [ANY] * len(after),
        out_specs=specs,
        out_shape=outs,
        scratch_shapes=[pltpu.VMEM((width, own), bf16)] * 3
        + [pltpu.VMEM((own, width), bf16)]
        + [pltpu.VMEM((clips, nkeys, own), bf16)] * 2
        + [pltpu.VMEM(soft, bf16), pltpu.VMEM((rows, width), bf16), pltpu.VMEM((4, rows, own), bf16)]
        + [pltpu.SemaphoreType.DMA((7 + clips + 2 * clips * len(keys),))],
        **settings(20, 9),
    )(*smalls, wq, wk, wv, wo, *keys, *values, *after)


def quarter(dest, src):
    count = dest.shape[0]
    at = lax.rem(lax.axis_index("frame"), src.shape[0] // count)
    dest[...] = src[pl.ds(pl.multiple_of(at * count, count), count), :]


def ffn_kernel(l, step, top, *refs):
    base, mine, other, gain, up, down = refs[:6]
    if top:
        gh_in, keep, send, middle, rows_out, middle_out, keep_back, send_back = refs[6:14]
        ups, downs, ffn_s, sems, gh_s = refs[14:]
    else:
        keep, send, middle, rows_out, middle_out, slope_out = refs[6:12]
        ups, downs, ffn_s, sems, slope_s = refs[12:]
    fetch = Fetch(sems)
    hidden_all = ups.shape[1]
    blocks = [pl.ds(n * step, step) for n in range(hidden_all // step)]
    up_copies = [fetch(up.at[l, :, b], ups.at[:, b]) for b in blocks]
    gh_copy = fetch(gh_in, gh_s) if top else None
    down_copies = [fetch(down.at[l, b], downs.at[b]) for b in blocks]
    take_halves(middle, base, mine, other)
    stores = [fetch(middle, middle_out)]
    plain, _ = norm_plain(middle[...])
    ffn_in = (plain * gain[l : l + 1, :]).astype(bf16)
    ffn_s[...] = ffn_in
    quarter(rows_out, ffn_s)
    if top:
        gh_copy.wait()
    hiddens, gpres = [], []
    for n, b in enumerate(blocks):
        up_copies[n].wait()
        hidden, slope = gelu_parts(dot(ffn_in, ups[:, b]))
        if top:
            gpres.append((slope * gh_s[:, b]).astype(bf16))
        else:
            slope_s[:, b] = slope.astype(bf16)
        hiddens.append(hidden.astype(bf16))
    if top:
        total = None
        for n, b in enumerate(blocks):
            part = dot_nt(gpres[n], ups[:, b])
            total = part if total is None else total + part
        put_halves(total, keep_back, send_back)
    else:
        stores.append(fetch(slope_s, slope_out))
    total = None
    for n, b in enumerate(blocks):
        down_copies[n].wait()
        part = dot(hiddens[n], downs[b, :])
        total = part if total is None else total + part
    put_halves(total, keep, send)
    for copy in stores:
        copy.wait()


def ffn_stage(l, nf, base, halves, gain, up, down, gh, after):
    rows, width = base.shape
    hidden = up.shape[2]
    step = 256
    top = len(gh) == 1
    half = shape((rows // 2, width))
    return pl.pallas_call(
        skip(functools.partial(ffn_kernel, l, step, top), 6 + len(gh), len(after)),
        in_specs=[VMEM] * 4 + [HBM] * (2 + len(gh)) + [ANY] * len(after),
        out_specs=[VMEM] * 4 + [HBM] + ([VMEM] * 2 if top else [HBM]),
        out_shape=[half, half, shape((rows, width), f32), shape((rows // nf, width)), far((rows, width), f32)]
        + ([half, half] if top else [far((rows, hidden))]),
        scratch_shapes=[
            pltpu.VMEM((width, hidden), bf16),
            pltpu.VMEM((hidden, width), bf16),
            pltpu.VMEM((rows, width), bf16),
            pltpu.SemaphoreType.DMA((2 * hidden // step + 2,)),
            pltpu.VMEM((rows, hidden), f32 if top else bf16),
        ],
        **settings(16, 6),
    )(base, *halves, gain, up, down, *gh, *after)


def top_kernel(l, step, base, living, down, grad, rows_out, gh, downs, gy_s, sems):
    fetch = Fetch(sems)
    blocks = [pl.ds(n * step, step) for n in range(downs.shape[0] // step)]
    down_copies = [fetch(down.at[l, b], downs.at[b]) for b in blocks]
    now = base[...] * living[...]
    grad[...] = now
    gy = now.astype(bf16)
    gy_s[...] = gy
    quarter(rows_out, gy_s)
    for n, b in enumerate(blocks):
        down_copies[n].wait()
        gh[:, b] = dot_nt(gy, downs[b, :])


def top_stage(nf, base, living, down):
    rows, width = base.shape
    hidden = down.shape[1]
    step = 256
    return pl.pallas_call(
        functools.partial(top_kernel, LAYERS - 1, step),
        in_specs=[VMEM] * 2 + [HBM],
        out_specs=[VMEM] * 3,
        out_shape=[shape((rows, width), f32), shape((rows // nf, width)), shape((rows, hidden), f32)],
        scratch_shapes=[
            pltpu.VMEM((hidden, width), bf16),
            pltpu.VMEM((rows, width), bf16),
            pltpu.SemaphoreType.DMA((hidden // step,)),
        ],
        **settings(12, 4),
    )(base, living, down)


def ffn_back_kernel(
    l, step, base, mine, other, gain, lat_in, slope_in, up, down, keep, send, rows_out, gain_grad, grad_out,
    ups, downs, slope_s, gy_s, sems, work, lat, grad_s,
):
    fetch = Fetch(sems)
    blocks = [pl.ds(n * step, step) for n in range(ups.shape[1] // step)]
    lat_copy = fetch(lat_in, lat)
    down_copies = [fetch(down.at[l, b], downs.at[b]) for b in blocks]
    slope_copy = fetch(slope_in, slope_s)
    up_copies = [fetch(up.at[l, :, b], ups.at[:, b]) for b in blocks]
    take_halves(work, None, mine, other)
    lat_copy.wait()
    now = latent_back(base, work, lat, gain, l + 1, gain_grad)
    grad_s[...] = now
    grad_copy = fetch(grad_s, grad_out)
    gy = now.astype(bf16)
    gy_s[...] = gy
    quarter(rows_out, gy_s)
    slope_copy.wait()
    gpres = []
    for n, b in enumerate(blocks):
        down_copies[n].wait()
        gpres.append((slope_s[:, b].astype(f32) * dot_nt(gy, downs[b, :])).astype(bf16))
    total = None
    for n, b in enumerate(blocks):
        up_copies[n].wait()
        part = dot_nt(gpres[n], ups[:, b])
        total = part if total is None else total + part
    put_halves(total, keep, send)
    grad_copy.wait()


def latent_back(base, work, lat, gain, l, gain_grad):
    plain, inverse = norm_plain(lat[...])
    arrived = work[...]
    gain_grad[...] = jnp.sum(arrived * plain, axis=0, keepdims=True)
    return base[...] + norm_back(arrived * gain[l : l + 1, :], plain, inverse)


def ffn_back_stage(l, nf, base, halves, gain, lat, slope, up, down, after):
    rows, width = base.shape
    hidden = up.shape[2]
    step = 256
    half = shape((rows // 2, width))
    return pl.pallas_call(
        skip(functools.partial(ffn_back_kernel, l, step), 8, len(after)),
        in_specs=[VMEM] * 4 + [HBM] * 4 + [ANY] * len(after),
        out_specs=[VMEM] * 4 + [HBM],
        out_shape=[half, half, shape((rows // nf, width)), shape((1, width), f32), far((rows, width), f32)],
        scratch_shapes=[
            pltpu.VMEM((width, hidden), bf16),
            pltpu.VMEM((hidden, width), bf16),
            pltpu.VMEM((rows, hidden), bf16),
            pltpu.VMEM((rows, width), bf16),
            pltpu.SemaphoreType.DMA((2 * hidden // step + 3,)),
        ]
        + [pltpu.VMEM((rows, width), f32)] * 3,
        **settings(16, 6),
    )(base, *halves, gain, lat, slope, up, down, *after)


def attn_back_kernel(l, clips, nf, mine, other, gain, base_in, middle_in, heads_in, soft_in, wo, wq, wk, wv, *refs):
    frame_keys, frame_values = refs[:nf], refs[nf : 2 * nf]
    keep, send, gmid_out, gain_grad, gupd_out, grads_out, gscore_out = refs[2 * nf : 2 * nf + 7]
    wqs, wks, wvs, wos, ks, vs, work, middle, base, heads_s, grads_s, gupd_s, soft_s, score_s, sems = refs[2 * nf + 7 :]
    fetch = Fetch(sems)
    middle_copy, base_copy = fetch(middle_in, middle), fetch(base_in, base)
    wo_copy = fetch(wo.at[l], wos)
    heads_copy = fetch(heads_in, heads_s)
    value_copies, media_keys = fetch_keys(fetch, frame_values, vs, clips)
    soft_copies = [fetch(soft_in.at[c], soft_s.at[c]) for c in range(clips)]
    key_copies, _ = fetch_keys(fetch, frame_keys, ks, clips)
    waits = [fetch(wq.at[l], wqs), fetch(wk.at[l], wks), fetch(wv.at[l], wvs)]
    take_halves(work, None, mine, other)
    middle_copy.wait()
    base_copy.wait()
    gmid = latent_back(base, work, middle, gain, l, gain_grad)
    gmid_out[...] = gmid
    gupd = gmid.astype(bf16)
    gupd_s[...] = gupd
    stores = [fetch(gupd_s, gupd_out)]
    heads = wqs.shape[1] // HEAD_DIM
    rows = gupd.shape[0] // clips
    wo_copy.wait()
    gatt = dot_nt(gupd, wos[...]).astype(bf16)
    heads_copy.wait()
    gqs, gkls, gvls = [], [], []
    for c in range(clips):
        part = slice(c * rows, (c + 1) * rows)
        ks[c, media_keys:] = heads_s[1, part]
        vs[c, media_keys:] = heads_s[2, part]
        qs = spread(heads_s[0, part], heads)
        gs = spread(gatt[part], heads)
        for copy in value_copies[c]:
            copy.wait()
        gsoft = dot_nt(gs, vs[c])
        soft_copies[c].wait()
        soft = soft_s[c]
        soft32 = soft.astype(f32)
        delta = jnp.sum(soft32 * gsoft, axis=-1, keepdims=True)
        gscore = (soft32 * (gsoft - delta)).astype(bf16)
        score_s[c] = gscore
        stores.append(fetch(score_s.at[c], gscore_out.at[c]))
        for copy in key_copies[c]:
            copy.wait()
        gqs.append(gathered(dot(gscore, ks[c]), heads) * SCALING)
        gkls.append(dot_tn(gscore[:, media_keys:], qs) * SCALING)
        gvls.append(dot_tn(soft[:, media_keys:], gs))
    gq = jnp.concatenate(gqs, axis=0).astype(bf16)
    gkl = jnp.concatenate(gkls, axis=0).astype(bf16)
    gvl = jnp.concatenate(gvls, axis=0).astype(bf16)
    grads_s[0] = gatt
    grads_s[1] = gq
    grads_s[2] = gkl
    grads_s[3] = gvl
    stores.append(fetch(grads_s, grads_out))
    for copy in waits:
        copy.wait()
    put_halves(dot_nt(gq, wqs[...]) + dot_nt(gkl, wks[...]) + dot_nt(gvl, wvs[...]), keep, send)
    for copy in stores:
        copy.wait()


def attn_back_stage(l, clips, base, halves, gain, middle, heads_all, soft, wo, wq, wk, wv, keys, values, after):
    rows, width = base.shape
    own = wq.shape[2]
    outs = [
        shape((rows // 2, width)),
        shape((rows // 2, width)),
        shape((rows, width), f32),
        shape((1, width), f32),
        far((rows, width)),
        far((4, rows, own)),
        far(soft.shape),
    ]
    nkeys = soft.shape[2]
    return pl.pallas_call(
        skip(functools.partial(attn_back_kernel, l, clips, len(keys)), 11 + 2 * len(keys), len(after)),
        in_specs=[VMEM] * 3 + [HBM] * (8 + 2 * len(keys)) + [ANY] * len(after),
        out_specs=[VMEM] * 4 + [HBM] * 3,
        out_shape=outs,
        scratch_shapes=[pltpu.VMEM((width, own), bf16)] * 3
        + [pltpu.VMEM((own, width), bf16)]
        + [pltpu.VMEM((clips, nkeys, own), bf16)] * 2
        + [pltpu.VMEM((rows, width), f32)] * 3
        + [pltpu.VMEM((4, rows, own), bf16)] * 2
        + [pltpu.VMEM((rows, width), bf16)]
        + [pltpu.VMEM(soft.shape, bf16)] * 2
        + [pltpu.SemaphoreType.DMA((9 + 2 * clips + 2 * clips * len(keys),))],
        **settings(25, 7),
    )(*halves, gain, base, middle, heads_all, soft, wo, wq, wk, wv, *keys, *values, *after)


def last_kernel(l, base, mine, other, lat, gain, *refs):
    grad, gain_grad, work = refs[-3:]
    take_halves(work, None, mine, other)
    grad[...] = latent_back(base, work, lat, gain, l, gain_grad)


def last_stage(base, halves, lat, gain, after):
    rows, width = base.shape
    return pl.pallas_call(
        functools.partial(last_kernel, 0),
        in_specs=[VMEM] * 5 + [ANY] * len(after),
        out_specs=[VMEM] * 2,
        out_shape=[shape((rows, width), f32), shape((1, width), f32)],
        scratch_shapes=[pltpu.VMEM((rows, width), f32)],
        **settings(12, 2),
    )(base, *halves, lat, gain, *after)


def out_kernel(base, mine, other, living, dest):
    take_halves(dest, base, mine, other)
    dest[...] = dest[...] * living[...]


def out_stage(base, halves, living):
    return pl.pallas_call(
        out_kernel,
        in_specs=[VMEM] * 4,
        out_specs=VMEM,
        out_shape=shape(base.shape, f32),
        **settings(8, 1),
    )(base, *halves, living)


def proj_kernel(clips, cut, nf, lead, *refs):
    plains = refs[:nf]
    lat_n, gupd, wk, wv, gain, gscore, soft, heads_all, grads = refs[nf : nf + 9]
    media_gain, qs, gs = refs[-3:]
    outs = refs[nf + 9 : -3] if lead == 4 else refs[-5:-3]
    out, out_last = outs[-1] if lead == 4 else outs[0], outs[-1]
    _, total, own = heads_all.shape
    heads = own // HEAD_DIM
    rows = total // clips
    wide = heads * rows

    @pl.when(pl.program_id(0) == 0)
    def _():
        for c in range(clips):
            part = slice(c * rows, (c + 1) * rows)
            qs[c * wide : (c + 1) * wide] = (spread(heads_all[0, part], heads).astype(f32) * SCALING).astype(bf16)
            gs[c * wide : (c + 1) * wide] = spread(grads[0, part], heads)

    scale = gain[...]
    zs, ys = [], []
    for c in range(clips):
        z = y = None
        at = 0
        for plain in plains:
            patches = plain.shape[0] // clips
            block = plain[c * patches : (c + 1) * patches]
            part_z = dot(gscore[c, :, at : at + patches], block)
            part_y = dot(soft[c, :, at : at + patches], block)
            z = part_z if z is None else z + part_z
            y = part_y if y is None else y + part_y
            at += patches
        zs.append((z * scale).astype(bf16))
        ys.append((y * scale).astype(bf16))
    kg = dot_tn(jnp.concatenate(zs, axis=0), qs[...])
    vg = dot_tn(jnp.concatenate(ys, axis=0), gs[...])
    along = kg * wk[0].astype(f32) + vg * wv[0].astype(f32)
    along = jnp.broadcast_to(jnp.sum(along, axis=1, keepdims=True), (along.shape[0], 128))
    media_gain[...] = jnp.transpose(along)[:1] / scale
    lat_b = lat_n[...]
    kg = (kg + dot_tn(lat_b, grads[2])).astype(bf16)
    vg = (vg + dot_tn(lat_b, grads[3])).astype(bf16)
    qg = dot_tn(lat_b, grads[1]).astype(bf16)
    og = dot_tn(gupd[...], heads_all[3]).astype(bf16)
    for b in range(kg.shape[0] // cut):
        for n, grad in enumerate((kg, vg, qg, og)):
            dest = (out, n) if n < lead else (out_last, n - lead)
            dest[0][b, dest[1]] = grad[b * cut : (b + 1) * cut]


def proj_stage(l, lead, clips, nc, plains, lat_n, gupd, wk, wv, gain, gscore, soft, heads_all, grads, after):
    width = lat_n.shape[1]
    _, rows, own = heads_all.shape
    cut = width // nc
    block = 384
    per = block // cut
    heads = own // HEAD_DIM
    wide = heads * rows
    full = lambda v: fixed(v.shape)
    columns = lambda v: pl.BlockSpec(v.shape[:-1] + (block,), lambda i: (0,) * (v.ndim - 1) + (i,))
    weight = pl.BlockSpec((1, block, own), lambda i: (l, i, 0))
    return pl.pallas_call(
        functools.partial(proj_kernel, clips, cut, len(plains), lead),
        grid=(width // block,),
        in_specs=[columns(v) for v in plains]
        + [columns(lat_n), columns(gupd), weight, weight, columns(gain)]
        + [full(v) for v in (gscore, soft, heads_all, grads)]
        + [ANY] * len(after),
        out_specs=[pl.BlockSpec((per, n, cut, own), lambda i: (i, 0, 0, 0)) for n in (lead, 4 - lead) if n]
        + [pl.BlockSpec((1, block), lambda i: (0, i))],
        out_shape=[shape((nc, n, cut, own)) for n in (lead, 4 - lead) if n] + [shape((1, width), f32)],
        scratch_shapes=[pltpu.VMEM((wide, own), bf16)] * 2,
        **settings(22, 12),
    )(*plains, lat_n, gupd, wk, wv, gain, gscore, soft, heads_all, grads, *after)


def media_back_kernel(frames, *refs):
    count = 2 * LAYERS
    tables, firsts, weights = refs[:count], refs[count : 2 * count], refs[2 * count : 2 * count + 2]
    out, sums, stack = refs[-3:]
    norms = refs[2 * count + 2 : 2 * count + 2 + 2 * frames]

    @pl.when(pl.program_id(1) == 0)
    def _():
        own = weights[0].shape[2]
        heads = own // HEAD_DIM
        for n in range(count):
            l = n // 2
            v = firsts[n][0]
            if n % 2 == 0:
                v = (v.astype(f32) * SCALING).astype(bf16)
            across = dot_nt(spread(v, heads), weights[n % 2][l])
            rows = across.shape[0]
            stack[n * rows : (n + 1) * rows] = across.astype(bf16)

    left = jnp.concatenate([t[0] for t in tables], axis=0)
    u = dot_tn(left, stack[...])
    out[0] = u.astype(bf16)
    mean = jnp.mean(u, axis=-1, keepdims=True)
    for n in range(frames):

        @pl.when(pl.program_id(1) == n)
        def _():
            plain, inverse = norms[2 * n][...].astype(f32), norms[2 * n + 1][:, :1]
            along = jnp.mean(u * plain, axis=-1, keepdims=True)
            sums[0, 0] = jnp.sum(inverse * (u - mean - plain * along), axis=0, keepdims=True)


def media_back_stage(first_frame, frames, clips, patches, tables, firsts, wk, wv, ready, after):
    width = wk.shape[1]
    table = pl.BlockSpec((1, tables[0].shape[1], patches), lambda c, r: (c, 0, first_frame + r))
    _, rows, own = firsts[0].shape
    piece = pl.BlockSpec((1, rows // clips, own), lambda c, r: (0, c, 0))
    full = lambda v: fixed(v.shape)
    norms = [hbm(v) for made in ready for v in made[:2]]
    norm_piece = lambda v: pl.BlockSpec((patches, v.shape[1]), lambda c, r: (c, 0))
    return pl.pallas_call(
        functools.partial(media_back_kernel, frames),
        grid=(clips, frames),
        in_specs=[table] * 4 + [piece] * 4 + [full(wk), full(wv)] + [norm_piece(v) for v in norms] + [ANY] * len(after),
        out_specs=[
            pl.BlockSpec((1, patches, width), lambda c, r: (r, c, 0)),
            pl.BlockSpec((1, 1, 1, width), lambda c, r: (r, c, 0, 0)),
        ],
        out_shape=[shape((frames, clips * patches, width)), shape((frames, clips, 1, width), f32)],
        scratch_shapes=[pltpu.VMEM((4 * tables[0].shape[1], width), bf16)],
        **settings(28, 9),
    )(*tables, *firsts, wk, wv, *norms, *after)


def media_last_kernel(count, media, stamp, *refs):
    parts, out = refs[:count], refs[-1]
    plain, inverse = norm_plain(media[...].astype(f32) + stamp[0])
    u = parts[0][...].astype(f32)
    for part in parts[1:]:
        u = u + part[...].astype(f32)
    out[...] = norm_back(u, plain, inverse)


def media_last_stage(media, stamp, parts, clips, after):
    rows, width = media.shape
    step = 128
    per = rows // clips // step
    piece = pl.BlockSpec((step, width), lambda i: (i, 0))
    clip = pl.BlockSpec((1, 1, width), lambda i: (i // per, 0, 0))
    return pl.pallas_call(
        functools.partial(media_last_kernel, len(parts)),
        grid=(rows // step,),
        in_specs=[piece, clip] + [piece] * len(parts) + [ANY] * len(after),
        out_specs=piece,
        out_shape=shape((rows, width), f32),
        **settings(20, 5),
    )(media, stamp, *parts, *after)


def own_columns(dest, src, nc):
    cut = dest.shape[1]
    block = 384
    at = lax.axis_index("clip") * cut
    wide = src[:, :, pl.ds(pl.multiple_of(at // block * block, block), block)].reshape(-1, block)
    for n in range(block // cut):

        @pl.when(lax.rem(at, block) == n * cut)
        def _():
            dest[...] = wide[:, n * cut : (n + 1) * cut]


def fetch_rows(fetch, refs, at, dest, chunk):
    each, rows, _ = dest.shape
    copies = []
    if len(refs) > 1:
        count = rows // len(refs)
        for r, ref in enumerate(refs):
            place = pl.ds(pl.multiple_of((lax.axis_index("frame") ^ r) * count, count), count)
            copies.append(fetch(ref.at[pl.ds(chunk * each, each)], dest.at[:, place]))
    else:
        nf = lax.axis_size("frame")
        count = rows // nf
        for c in range(each):
            for f in range(nf):
                source = refs[0].at[(chunk * each + c) * nf + f, pl.ds(at * count, count)]
                copies.append(fetch(source, dest.at[c, pl.ds(f * count, count)]))
    return copies


def ffn_grad_kernel(counts, shares, nc, *refs):
    rows_refs, grads_refs = refs[: counts[0]], refs[counts[0] : sum(counts)]
    up, down = refs[sum(counts) : sum(counts) + 2]
    up_grad, down_grad, rows_all, grads_all, rows_own, grads_own, sems = refs[-7:]
    chunk = pl.program_id(1)
    flat = lambda ref: ref[...].reshape(-1, ref.shape[2])

    @pl.when(jnp.logical_or(pl.program_id(0) == 0, pl.num_programs(1) > 1))
    def _():
        fetch = Fetch(sems)
        copies = fetch_rows(fetch, rows_refs, shares[0], rows_all, chunk)
        copies += fetch_rows(fetch, grads_refs, shares[1], grads_all, chunk)
        for copy in copies:
            copy.wait()
        own_columns(rows_own, rows_all, nc)
        own_columns(grads_own, grads_all, nc)

    step = up.shape[2]
    width = min(step, 256)
    halves = [slice(n, n + width) for n in range(0, step, width)]
    pres = [dot(flat(rows_all), up[0, :, b]) for b in halves]
    ghs = [dot_nt(flat(grads_all), down[0, b, :]) for b in halves]
    for n, b in enumerate(halves):
        hidden, slope = gelu_parts(pres[n])
        gpre = (slope * ghs[n]).astype(bf16)
        up_part = dot_tn(rows_own[...], gpre)
        down_part = dot_tn(grads_own[...], hidden.astype(bf16))

        @pl.when(chunk == 0)
        def _():
            up_grad[0, :, b] = up_part
            down_grad[0, :, b] = down_part

        @pl.when(chunk > 0)
        def _():
            up_grad[0, :, b] += up_part
            down_grad[0, :, b] += down_part


def ffn_grad_stage(l, nc, count, rows, grads, shares, up, down, earlier, after):
    width = rows[0].shape[2]
    cut = width // nc
    hidden = up.shape[2]
    step = 512 if hidden % 512 == 0 else 256
    each = min(nc, 1024 // count)
    outs = [shape((LAYERS, cut, hidden), f32)] * 2
    arrays = [hbm(v) for v in list(rows) + list(grads)]
    known = len(arrays) + 2
    return pl.pallas_call(
        functools.partial(ffn_grad_kernel, (len(rows), len(grads)), shares, nc),
        grid=(hidden // step, nc // each),
        in_specs=[HBM] * len(arrays)
        + [
            pl.BlockSpec((1, width, step), lambda j, i: (l, 0, j)),
            pl.BlockSpec((1, step, width), lambda j, i: (l, j, 0)),
        ]
        + [ANY] * (len(earlier) + len(after)),
        out_specs=[
            pl.BlockSpec((1, cut, step), lambda j, i: (l, 0, j)),
            pl.BlockSpec((1, cut, step), lambda j, i: (l, 0, j)),
        ],
        out_shape=outs,
        input_output_aliases={known: 0, known + 1: 1} if earlier else {},
        scratch_shapes=[pltpu.VMEM((each, count, width), bf16)] * 2
        + [pltpu.VMEM((each * count, cut), bf16)] * 2
        + [pltpu.SemaphoreType.DMA((2 * each * lax.axis_size("frame"),))],
        **settings(40, 14),
    )(*arrays, up, down, *earlier, *after)


def swap(v, axis, bit):
    size = lax.axis_size(axis)
    return lax.ppermute(v, axis, [(i, i ^ bit) for i in range(size)])


def bits_of(size):
    out, bit = [], 1
    while bit < size:
        out.append(bit)
        bit *= 2
    return out


def add_kernel(mine, arrived, *refs):
    refs[-1][...] = (mine[...].astype(f32) + arrived[...].astype(f32)).astype(bf16)


def add_after(mine, arrived, after):
    return pl.pallas_call(
        add_kernel,
        in_specs=[VMEM] * 2 + [ANY] * len(after),
        out_specs=VMEM,
        out_shape=shape(mine.shape),
        **settings(4, 1),
    )(mine, arrived, *after)


def frame_sum(keep, send, fill=None):
    mine = (keep.astype(f32) + swap(send, "frame", 1).astype(f32)).astype(bf16)
    made = None
    for bit in bits_of(lax.axis_size("frame"))[1:]:
        arrived = swap(mine, "frame", bit)
        if fill is not None and made is None:
            made = fill((mine,))
            mine = add_after(mine, arrived, made)
        else:
            mine = (mine.astype(f32) + arrived.astype(f32)).astype(bf16)
    return (mine, swap(mine, "frame", 1)) if fill is None else ((mine, swap(mine, "frame", 1)), made)


class Scatter:
    def __init__(self, parts, bits, clip_here):
        self.pieces = [parts.reshape((2,) * len(bits) + parts.shape[1:])]
        self.bits, self.left, self.clip_here = list(bits), sorted(bits, reverse=True), clip_here

    def send(self):
        bit = self.bits.pop(0)
        axis = self.left.index(bit)
        self.left.remove(bit)
        mine = (self.clip_here // bit) % 2
        pick = lambda v, n: lax.dynamic_index_in_dim(v, n, axis, keepdims=False)
        self.sent = sum(pick(v, 1 - mine).astype(f32) for v in self.pieces).astype(bf16)
        self.pieces = [pick(v, mine) for v in self.pieces]
        self.arriving = swap(self.sent, "clip", bit)
        return self

    def step(self, after):
        if self.arriving is None:
            return
        self.pieces.append(tie(self.arriving, after) if after else self.arriving)
        self.arriving = None
        if self.bits:
            self.send()

    @property
    def total(self):
        return sum(v.astype(f32) for v in self.pieces)


def gather_rows(shares):
    return lax.all_gather(jnp.concatenate(shares, axis=0), ("clip", "frame"), axis=0)


def exchange_rows(share, nc):
    return lax.all_to_all(jnp.broadcast_to(share, (nc,) + share.shape), "clip", 0, 0, tiled=True)


def spread_rows(mine, first_gate, second_gate):
    pieces = {0: tie(mine, first_gate)}
    for bit in bits_of(lax.axis_size("frame"))[::-1]:
        for r in list(pieces):
            arrived = swap(pieces[r], "frame", bit)
            pieces[r | bit] = tie(arrived, second_gate) if bit > 1 else arrived
    return [pieces[r] for r in range(len(pieces))]


def on_device(
    media, frame_order, clip_counts, latents, time_embed, media_gain, latent_gain, ffn_gain,
    query_weight, key_weight, value_weight, out_weight, up_weight, down_weight, cotangent,
):
    clips, _, patches, width = media.shape
    lat_rows = latents.shape[1]
    nf = lax.axis_size("frame")
    nc = lax.axis_size("clip")
    frame_here = lax.axis_index("frame")
    clip_here = lax.axis_index("clip")
    rows = clips * lat_rows

    key_plain, value_plain = key_weight, value_weight
    query_weight, key_weight, value_weight, out_weight, up_weight, down_weight = (
        pltpu.with_memory_space_constraint(w, pltpu.HBM)
        for w in (query_weight, key_weight, value_weight, out_weight, up_weight, down_weight)
    )
    clip_ids = clip_here * clips + jnp.arange(clips, dtype=jnp.int32)
    owner_match = (clip_ids // SLOTS)[:, None] == jnp.arange(clip_counts.shape[0], dtype=jnp.int32)[None, :]
    owner_count = jnp.sum(jnp.where(owner_match, clip_counts[None, :], 0), axis=1)
    living = (clip_ids % SLOTS < owner_count).astype(f32)
    living = jnp.repeat(living, lat_rows)[:, None]

    flat = media.reshape(clips * patches, width)
    top = nf // 2
    frames = {0: flat}
    if top > 1:
        frames[top] = swap(flat, "frame", top)
    for bit in bits_of(top)[::-1]:
        for r in [r for r in frames if r < top]:
            frames[r | bit] = swap(frames[r], "frame", bit)
    times = jnp.arange(nf, dtype=jnp.int32)
    order = jnp.stack(
        [lax.dynamic_index_in_dim(frame_order, frame_here ^ r, 1, keepdims=False) for r in range(nf)]
    )
    onehot = (order[:, :, None] == times).astype(f32)
    stamps = jnp.sum(onehot[..., None] * time_embed, axis=2)[:, :, None, :]
    wide_k = (media_gain[:, :, None] * key_plain.astype(f32)).astype(bf16)
    wide_v = (media_gain[:, :, None] * value_plain.astype(f32)).astype(bf16)
    ready = [media_stage(frames[r], stamps[r], wide_k, wide_v, clips) for r in range(top)]
    last = LAYERS - 1
    grad, top_share, gh = top_stage(nf, cotangent.reshape(rows, width), living, down_weight)
    frames[top] = tie(frames[top], [made[0] for made in ready] + [gh])
    for bit in bits_of(top)[::-1]:
        for r in [r for r in frames if r >= top]:
            frames[r | bit] = swap(frames[r], "frame", bit)
    ready += [media_stage(frames[r], stamps[r], wide_k, wide_v, clips) for r in range(top, nf)]
    plains = [hbm(g[0]) for g in ready]

    stored, ffn_shares = [], []
    current, halves = latents.reshape(rows, width), None
    for l in range(LAYERS):
        keys = [hbm(g[2 + 2 * l]) for g in ready]
        values = [hbm(g[3 + 2 * l]) for g in ready]
        out = attn_stage(
            l, clips, current, halves, latent_gain, query_weight, key_weight, value_weight, out_weight, keys, values, ()
        )
        keep, send, lat_n, heads_all, soft = out[:5]
        lat, lat_far = (current, None) if halves is None else (out[5], hbm(out[6]))
        halves = frame_sum(keep, send)
        gh_here = (hbm(gh),) if l == last else ()
        out = ffn_stage(l, nf, lat, halves, ffn_gain, up_weight, down_weight, gh_here, ())
        keep, send, current, share, middle = out[:5]
        ffn_shares.append(share)
        if l < last:
            slope = out[5]
        else:
            slope, (keep_back, send_back) = middle, out[5:]
            early = gather_rows(ffn_shares + [top_share])
        halves = frame_sum(keep, send) if l < last else None
        stored.append((keys, values, lat_far, hbm(lat_n), hbm(heads_all), hbm(soft), hbm(middle), hbm(slope)))
    forward_keep, forward_send = keep, send
    lat_gain_grads, ffn_gain_grads, media_gain_grads = [None] * LAYERS, [None] * LAYERS, [None] * LAYERS
    projs, tables, firsts = [None] * LAYERS, [None] * LAYERS, [None] * LAYERS

    def attend_back(l, grad, halves, lead, before, between):
        keys, values, _, lat_n, heads_all, soft, middle, _ = stored[l]
        keep, send, gmid, ffn_gain_grads[l], gupd, grads, gscore = attn_back_stage(
            l, clips, hbm(grad), halves, ffn_gain, middle, heads_all, soft, out_weight, query_weight, key_weight,
            value_weight, keys, values, before,
        )
        gupd, grads, gscore = hbm(gupd), hbm(grads), hbm(gscore)
        tables[l], firsts[l] = (gscore, soft), (heads_all, grads)

        def projections(after):
            return proj_stage(
                l, lead, clips, nc, plains, lat_n, gupd, key_weight, value_weight, media_gain[l : l + 1], gscore, soft,
                heads_all, grads, after + between,
            )

        halves, (*projs[l], along) = frame_sum(keep, send, projections)
        media_gain_grads[l] = along
        return gmid, halves

    def scattered(l):
        bits = bits_of(nc)
        orders = (bits, bits[1:] + bits[:1])
        return [Scatter(v, order, clip_here).send() for v, order in zip(projs[l], orders)]

    back_halves = frame_sum(keep_back, send_back)
    gmid, halves = attend_back(1, grad, back_halves, 3, (), ())
    upper = scattered(1)
    keep, send, share, lat_gain_grads[1], grad = ffn_back_stage(
        0, nf, gmid, halves, latent_gain, stored[1][2], stored[0][7], up_weight, down_weight, (),
    )
    lower_grads = exchange_rows(share, nc)
    halves = frame_sum(keep, send)
    gmid, halves = attend_back(0, grad, halves, 3, (), ())
    lower = scattered(0)
    forward = frame_sum(tie(forward_keep, (gmid,)), tie(forward_send, (gmid,)))
    latents_out = out_stage(current, forward, living)


    half = nf // 2
    tables = [t for pair in tables for t in pair]
    firsts = [t for pair in firsts for t in pair]
    u = {}
    part, far_sums = media_back_stage(
        half, half, clips, patches, tables, firsts, wide_k, wide_v, ready[half:], (lower[0].sent, lower[1].sent)
    )
    for r in range(half):
        u[half + r] = [part[r]]
    for part_sum in upper:
        part_sum.step((part,))
    gate = tuple(part_sum.sent for part_sum in upper)
    latents_grad, lat_gain_grads[0] = last_stage(gmid, halves, latents.reshape(rows, width), latent_gain, gate)
    merged = lambda v: v[0] if len(v) == 1 else sum(x.astype(f32) for x in v).astype(bf16)

    def fold(bits, least):
        for bit in bits:
            for r in [r for r in u if r & bit and r >= least]:
                u[r ^ bit].append(swap(merged(u.pop(r)), "frame", bit))

    fold(bits_of(half), half)
    sent = merged(u.pop(half))
    lower_mine = tie(lower_grads, (far_sums,))
    arrived = swap(sent, "frame", half)
    part, near_sums = media_back_stage(
        0, half, clips, patches, tables, firsts, wide_k, wide_v, ready[:half], (sent, latents_grad, lower_mine)
    )
    for r in range(half):
        u[r] = [part[r]]
    fold(bits_of(half), 0)
    gate = (part,)
    ffn_parts = ffn_grad_stage(1, nc, rows, (early,), (early,), (1, 2), up_weight, down_weight, (), gate)
    gate = (ffn_parts[0],)
    for part_sum in upper + lower:
        part_sum.step(gate)
    lower_grads = spread_rows(lower_mine, (near_sums,), (ffn_parts[0],))
    up_grad, down_grad = ffn_grad_stage(
        0, nc, rows, (early,), lower_grads, (0, 0), up_weight, down_weight, ffn_parts,
        (lower[0].sent, lower[1].sent, upper[0].sent, upper[1].sent),
    )
    gate = (up_grad,)
    for part_sum in lower + upper:
        part_sum.step(gate)
    media_grad = media_last_stage(
        flat, stamps[0], u[0] + [tie(arrived, gate)], clips,
        (lower[0].sent, lower[1].sent, upper[0].pieces[-1], upper[1].pieces[-1]),
    )
    for part_sum in upper + lower:
        part_sum.step((media_grad,))
    for scatter in upper + lower:
        while scatter.arriving is not None:
            scatter.step(())
    sums = jnp.concatenate([near_sums, far_sums], axis=0)
    time_part = jnp.einsum("rct,rcd->td", onehot, sums[:, :, 0], precision=lax.Precision.HIGHEST)

    n_all = nc * nf
    narrow = jnp.concatenate([time_part] + media_gain_grads, axis=0)
    narrow = narrow.reshape(nf + 2, n_all, width // n_all).transpose(1, 0, 2).reshape(n_all, -1)
    broad = jnp.concatenate(lat_gain_grads + ffn_gain_grads, axis=0)
    broad = broad.reshape(4, nc, width // nc).transpose(1, 0, 2).reshape(nc, 1, -1)
    broad = jnp.broadcast_to(broad * (1.0 / nf), (nc, nf, broad.shape[2]))
    packed = tie(jnp.concatenate([narrow, broad.reshape(n_all, -1)], axis=1), (ffn_parts[0],))
    packed = jnp.sum(lax.all_to_all(packed, ("clip", "frame"), 0, 0, tiled=True), axis=0)
    edge = (nf + 2) * (width // n_all)
    narrow = packed[:edge].reshape(nf + 2, -1)
    broad = packed[edge:].reshape(4, -1)

    totals = [jnp.concatenate([part.total for part in pair], axis=0) for pair in (lower, upper)]
    pick = lambda n: jnp.stack([total[n] for total in totals])
    return (
        latents_out.reshape(latents.shape),
        media_grad.reshape(media.shape),
        latents_grad.reshape(latents.shape),
        narrow[:nf],
        narrow[nf:],
        broad[:2],
        broad[2:],
        pick(2),
        pick(0),
        pick(1),
        jnp.swapaxes(pick(3), 1, 2),
        up_grad,
        jnp.swapaxes(down_grad, 1, 2),
    )


def solution(mesh):
    return jax.shard_map(
        on_device,
        mesh=mesh,
        in_specs=(
            P("clip", "frame", None, None),
            P("clip", None),
            P(),
            P("clip", None, None),
            P(),
            P(),
            P(),
            P(),
            P(None, None, "frame"),
            P(None, None, "frame"),
            P(None, None, "frame"),
            P(None, "frame", None),
            P(None, None, "frame"),
            P(None, "frame", None),
            P("clip", None, None),
        ),
        out_specs=(
            P("clip", None, None),
            P("clip", "frame", None, None),
            P("clip", None, None),
            P(None, ("clip", "frame")),
            P(None, ("clip", "frame")),
            P(None, "clip"),
            P(None, "clip"),
            P(None, "clip", "frame"),
            P(None, "clip", "frame"),
            P(None, "clip", "frame"),
            P(None, "frame", "clip"),
            P(None, "clip", "frame"),
            P(None, "frame", "clip"),
        ),
        check_vma=False,
    )
```

```python
import functools

import jax
import jax.numpy as jnp
from jax import lax
from jax.experimental import pallas as pl
from jax.experimental.pallas import tpu as pltpu
from jax.sharding import PartitionSpec as P

HEAD_DIM = 96
SLOTS = 4
LAYERS = 2
EPSILON = 1e-05
SCALING = HEAD_DIM ** (-0.5)
MIB = 1 << 20
f32 = jnp.float32
bf16 = jnp.bfloat16
VMEM = pl.BlockSpec(memory_space=pltpu.VMEM)
ANY = pl.BlockSpec(memory_space=pl.ANY)
HBM = pl.BlockSpec(memory_space=pltpu.HBM)


def norm_plain(v):
    mean = jnp.mean(v, axis=-1, keepdims=True)
    centred = v - mean
    inverse = lax.rsqrt(jnp.mean(centred * centred, axis=-1, keepdims=True) + EPSILON)
    return centred * inverse, inverse


def norm_back(u, normed, inverse):
    return inverse * (
        u
        - jnp.mean(u, axis=-1, keepdims=True)
        - normed * jnp.mean(u * normed, axis=-1, keepdims=True)
    )


def dot(a, b):
    return jnp.dot(a, b, preferred_element_type=f32)


def dot_nt(a, b):
    return lax.dot_general(a, b, (((1,), (1,)), ((), ())), preferred_element_type=f32)


def dot_tn(a, b):
    return lax.dot_general(a, b, (((0,), (0,)), ((), ())), preferred_element_type=f32)


def gelu_parts(x):
    half = 0.5 + 0.5 * lax.erf(x * (0.5**0.5))
    return x * half, half + x * jnp.exp(-0.5 * x * x) * (0.5 / jnp.pi) ** 0.5


def skip(kernel, inputs, extra):
    return lambda *refs: kernel(*refs[:inputs], *refs[inputs + extra :])


def shape(dims, kind=bf16):
    return jax.ShapeDtypeStruct(tuple(dims), kind)


def far(dims, kind=bf16):
    return pltpu.HBM(tuple(dims), kind)


def settings(mib, micros):
    return dict(
        compiler_params=pltpu.CompilerParams(vmem_limit_bytes=mib * MIB),
        cost_estimate=pl.CostEstimate(flops=int(micros * 1.15e9), bytes_accessed=1000, transcendentals=0),
    )


def hbm(v):
    return pltpu.with_memory_space_constraint(v, pltpu.HBM)


def fixed(dims, maps=None):
    return pl.BlockSpec(tuple(dims), maps or (lambda *i: (0,) * len(dims)), pipeline_mode=pl.Buffered(1))


def spread(v, heads):
    head = lax.broadcasted_iota(jnp.int32, v.shape, 1) // HEAD_DIM
    return jnp.concatenate([jnp.where(head == h, v, jnp.zeros_like(v)) for h in range(heads)], axis=0)


def gathered(v, heads):
    rows = v.shape[0] // heads
    head = lax.broadcasted_iota(jnp.int32, (rows, v.shape[1]), 1) // HEAD_DIM
    total = v[:rows]
    for h in range(1, heads):
        total = jnp.where(head == h, v[h * rows : (h + 1) * rows], total)
    return total


def on_core(run):
    core = lax.rem(lax.axis_index("frame"), 2)
    for value in (0, 1):
        pl.when(core == value)(functools.partial(run, value))


def put_halves(part, keep, send):
    half = part.shape[0] // 2
    halves = (part[:half].astype(bf16), part[half:].astype(bf16))

    def run(core):
        keep[...] = halves[core]
        send[...] = halves[1 - core]

    on_core(run)


def take_halves(dest, base, mine, other):
    half = mine.shape[0]

    def run(core):
        ordered = (mine, other) if core == 0 else (other, mine)
        for n in range(2):
            rows = slice(n * half, (n + 1) * half)
            dest[rows] = base[rows] + ordered[n][...].astype(f32) if base is not None else ordered[n][...].astype(f32)

    on_core(run)


def tie(v, after):
    return pl.pallas_call(
        lambda *refs: None,
        in_specs=[ANY] * (1 + len(after)),
        out_specs=ANY,
        out_shape=shape(v.shape, v.dtype),
        input_output_aliases={0: 0},
        **settings(1, 1),
    )(v, *after)


class Fetch:
    def __init__(self, sems):
        self.sems, self.used = sems, 0

    def __call__(self, src, dst):
        copy = pltpu.make_async_copy(src, dst, self.sems.at[self.used])
        self.used += 1
        copy.start()
        return copy


def media_kernel(frame, stamp, wide_k, wide_v, plain_out, inverse_out, *outs):
    plain, inverse = norm_plain(frame[...].astype(f32) + stamp[0])
    inverse_out[...] = jnp.broadcast_to(inverse, inverse_out.shape)
    plain = plain.astype(bf16)
    plain_out[...] = plain
    for l in range(LAYERS):
        outs[2 * l][...] = dot(plain, wide_k[l]).astype(bf16)
        outs[2 * l + 1][...] = dot(plain, wide_v[l]).astype(bf16)


def media_stage(frame, stamp, wide_k, wide_v, clips):
    rows, width = frame.shape
    own = wide_k.shape[2]
    patches = rows // clips
    piece = lambda w: pl.BlockSpec((patches, w), lambda i: (i, 0))
    return pl.pallas_call(
        media_kernel,
        grid=(clips,),
        in_specs=[piece(width), pl.BlockSpec((1, 1, width), lambda i: (i, 0, 0)), VMEM, VMEM],
        out_specs=[piece(width), piece(128)] + [piece(own)] * 4,
        out_shape=[far((rows, width)), far((rows, 128), f32)] + [far((rows, own))] * 4,
        **settings(14, 5),
    )(frame, stamp, wide_k, wide_v)


def fetch_keys(fetch, groups, ks, clips):
    copies = [[] for _ in range(clips)]
    at = 0
    for ref in groups:
        patches = ref.shape[0] // clips
        for c in range(clips):
            copies[c].append(fetch(ref.at[pl.ds(c * patches, patches)], ks.at[c, pl.ds(at, patches)]))
        at += patches
    return copies, at


def attn_kernel(l, clips, nf, first, *refs):
    if first:
        base, gain, wq, wk, wv, wo = refs[:6]
        refs = refs[6:]
    else:
        base, mine, other, gain, wq, wk, wv, wo = refs[:8]
        refs = refs[8:]
    frame_keys, frame_values = refs[:nf], refs[nf : 2 * nf]
    keep, send, lat_n_out, heads_out, soft_out = refs[2 * nf : 2 * nf + 5]
    wqs, wks, wvs, wos, ks, vs, soft_s, lat_n_s, heads_s, sems = refs[-10:]
    fetch = Fetch(sems)
    waits = [fetch(wq.at[l], wqs), fetch(wk.at[l], wks), fetch(wv.at[l], wvs)]
    key_copies, media_keys = fetch_keys(fetch, frame_keys, ks, clips)
    value_copies, _ = fetch_keys(fetch, frame_values, vs, clips)
    wo_copy = fetch(wo.at[l], wos)
    stores = []
    if first:
        lat = base
    else:
        lat, lat_out = refs[2 * nf + 5 : 2 * nf + 7]
        take_halves(lat, base, mine, other)
        stores.append(fetch(lat, lat_out))
    plain, _ = norm_plain(lat[...])
    lat_n = (plain * gain[l : l + 1, :]).astype(bf16)
    lat_n_s[...] = lat_n
    stores.append(fetch(lat_n_s, lat_n_out))
    heads = wqs.shape[1] // HEAD_DIM
    rows = lat_n.shape[0] // clips
    for copy in waits:
        copy.wait()
    q = dot(lat_n, wqs[...]).astype(bf16)
    kl = dot(lat_n, wks[...]).astype(bf16)
    vl = dot(lat_n, wvs[...]).astype(bf16)
    heads_s[0] = q
    heads_s[1] = kl
    heads_s[2] = vl
    atts = []
    for c in range(clips):
        part = slice(c * rows, (c + 1) * rows)
        ks[c, media_keys:] = kl[part]
        vs[c, media_keys:] = vl[part]
        for copy in key_copies[c]:
            copy.wait()
        scores = dot_nt(spread(q[part], heads), ks[c]) * SCALING
        ex = jnp.exp(scores - jnp.max(scores, axis=-1, keepdims=True))
        soft = (ex / jnp.sum(ex, axis=-1, keepdims=True)).astype(bf16)
        soft_s[c] = soft
        stores.append(fetch(soft_s.at[c], soft_out.at[c]))
        for copy in value_copies[c]:
            copy.wait()
        atts.append(gathered(dot(soft, vs[c]), heads).astype(bf16))
    att = jnp.concatenate(atts, axis=0)
    heads_s[3] = att
    stores.append(fetch(heads_s, heads_out))
    wo_copy.wait()
    put_halves(dot(att, wos[...]), keep, send)
    for copy in stores:
        copy.wait()


def attn_stage(l, clips, base, halves, gain, wq, wk, wv, wo, keys, values, after):
    rows, width = base.shape
    own = wq.shape[2]
    heads = own // HEAD_DIM
    nkeys = sum(k.shape[0] // clips for k in keys) + rows // clips
    soft = (clips, heads * rows // clips, nkeys)
    first = halves is None
    smalls = [base] + ([] if first else list(halves)) + [gain]
    outs = [shape((rows // 2, width)), shape((rows // 2, width)), far((rows, width)), far((4, rows, own)), far(soft)]
    specs = [VMEM] * 2 + [HBM] * 3
    if not first:
        outs += [shape((rows, width), f32), far((rows, width), f32)]
        specs += [VMEM, HBM]
    return pl.pallas_call(
        skip(functools.partial(attn_kernel, l, clips, len(keys), first), len(smalls) + 4 + 2 * len(keys), len(after)),
        in_specs=[VMEM] * len(smalls) + [HBM] * (4 + 2 * len(keys)) + [ANY] * len(after),
        out_specs=specs,
        out_shape=outs,
        scratch_shapes=[pltpu.VMEM((width, own), bf16)] * 3
        + [pltpu.VMEM((own, width), bf16)]
        + [pltpu.VMEM((clips, nkeys, own), bf16)] * 2
        + [pltpu.VMEM(soft, bf16), pltpu.VMEM((rows, width), bf16), pltpu.VMEM((4, rows, own), bf16)]
        + [pltpu.SemaphoreType.DMA((7 + clips + 2 * clips * len(keys),))],
        **settings(20, 9),
    )(*smalls, wq, wk, wv, wo, *keys, *values, *after)


def quarter(dest, src):
    count = dest.shape[0]
    at = lax.rem(lax.axis_index("frame"), src.shape[0] // count)
    dest[...] = src[pl.ds(pl.multiple_of(at * count, count), count), :]


def ffn_kernel(l, step, top, *refs):
    base, mine, other, gain, up, down = refs[:6]
    if top:
        gh_in, keep, send, middle, rows_out, middle_out, keep_back, send_back = refs[6:14]
        ups, downs, ffn_s, sems, gh_s = refs[14:]
    else:
        keep, send, middle, rows_out, middle_out, slope_out = refs[6:12]
        ups, downs, ffn_s, sems, slope_s = refs[12:]
    fetch = Fetch(sems)
    hidden_all = ups.shape[1]
    blocks = [pl.ds(n * step, step) for n in range(hidden_all // step)]
    up_copies = [fetch(up.at[l, :, b], ups.at[:, b]) for b in blocks]
    gh_copy = fetch(gh_in, gh_s) if top else None
    down_copies = [fetch(down.at[l, b], downs.at[b]) for b in blocks]
    take_halves(middle, base, mine, other)
    stores = [fetch(middle, middle_out)]
    plain, _ = norm_plain(middle[...])
    ffn_in = (plain * gain[l : l + 1, :]).astype(bf16)
    ffn_s[...] = ffn_in
    quarter(rows_out, ffn_s)
    if top:
        gh_copy.wait()
    hiddens, gpres = [], []
    for n, b in enumerate(blocks):
        up_copies[n].wait()
        hidden, slope = gelu_parts(dot(ffn_in, ups[:, b]))
        if top:
            gpres.append((slope * gh_s[:, b]).astype(bf16))
        else:
            slope_s[:, b] = slope.astype(bf16)
        hiddens.append(hidden.astype(bf16))
    if top:
        total = None
        for n, b in enumerate(blocks):
            part = dot_nt(gpres[n], ups[:, b])
            total = part if total is None else total + part
        put_halves(total, keep_back, send_back)
    else:
        stores.append(fetch(slope_s, slope_out))
    total = None
    for n, b in enumerate(blocks):
        down_copies[n].wait()
        part = dot(hiddens[n], downs[b, :])
        total = part if total is None else total + part
    put_halves(total, keep, send)
    for copy in stores:
        copy.wait()


def ffn_stage(l, nf, base, halves, gain, up, down, gh, after):
    rows, width = base.shape
    hidden = up.shape[2]
    step = 256
    top = len(gh) == 1
    half = shape((rows // 2, width))
    return pl.pallas_call(
        skip(functools.partial(ffn_kernel, l, step, top), 6 + len(gh), len(after)),
        in_specs=[VMEM] * 4 + [HBM] * (2 + len(gh)) + [ANY] * len(after),
        out_specs=[VMEM] * 4 + [HBM] + ([VMEM] * 2 if top else [HBM]),
        out_shape=[half, half, shape((rows, width), f32), shape((rows // nf, width)), far((rows, width), f32)]
        + ([half, half] if top else [far((rows, hidden))]),
        scratch_shapes=[
            pltpu.VMEM((width, hidden), bf16),
            pltpu.VMEM((hidden, width), bf16),
            pltpu.VMEM((rows, width), bf16),
            pltpu.SemaphoreType.DMA((2 * hidden // step + 2,)),
            pltpu.VMEM((rows, hidden), f32 if top else bf16),
        ],
        **settings(16, 6),
    )(base, *halves, gain, up, down, *gh, *after)


def top_kernel(l, step, base, living, down, grad, rows_out, gh, downs, gy_s, sems):
    fetch = Fetch(sems)
    blocks = [pl.ds(n * step, step) for n in range(downs.shape[0] // step)]
    down_copies = [fetch(down.at[l, b], downs.at[b]) for b in blocks]
    now = base[...] * living[...]
    grad[...] = now
    gy = now.astype(bf16)
    gy_s[...] = gy
    quarter(rows_out, gy_s)
    for n, b in enumerate(blocks):
        down_copies[n].wait()
        gh[:, b] = dot_nt(gy, downs[b, :])


def top_stage(nf, base, living, down):
    rows, width = base.shape
    hidden = down.shape[1]
    step = 256
    return pl.pallas_call(
        functools.partial(top_kernel, LAYERS - 1, step),
        in_specs=[VMEM] * 2 + [HBM],
        out_specs=[VMEM] * 3,
        out_shape=[shape((rows, width), f32), shape((rows // nf, width)), shape((rows, hidden), f32)],
        scratch_shapes=[
            pltpu.VMEM((hidden, width), bf16),
            pltpu.VMEM((rows, width), bf16),
            pltpu.SemaphoreType.DMA((hidden // step,)),
        ],
        **settings(12, 4),
    )(base, living, down)


def ffn_back_kernel(
    l, step, base, mine, other, gain, lat_in, slope_in, up, down, keep, send, rows_out, gain_grad, grad_out,
    ups, downs, slope_s, gy_s, sems, work, lat, grad_s,
):
    fetch = Fetch(sems)
    blocks = [pl.ds(n * step, step) for n in range(ups.shape[1] // step)]
    lat_copy = fetch(lat_in, lat)
    down_copies = [fetch(down.at[l, b], downs.at[b]) for b in blocks]
    slope_copy = fetch(slope_in, slope_s)
    up_copies = [fetch(up.at[l, :, b], ups.at[:, b]) for b in blocks]
    take_halves(work, None, mine, other)
    lat_copy.wait()
    now = latent_back(base, work, lat, gain, l + 1, gain_grad)
    grad_s[...] = now
    grad_copy = fetch(grad_s, grad_out)
    gy = now.astype(bf16)
    gy_s[...] = gy
    quarter(rows_out, gy_s)
    slope_copy.wait()
    gpres = []
    for n, b in enumerate(blocks):
        down_copies[n].wait()
        gpres.append((slope_s[:, b].astype(f32) * dot_nt(gy, downs[b, :])).astype(bf16))
    total = None
    for n, b in enumerate(blocks):
        up_copies[n].wait()
        part = dot_nt(gpres[n], ups[:, b])
        total = part if total is None else total + part
    put_halves(total, keep, send)
    grad_copy.wait()


def latent_back(base, work, lat, gain, l, gain_grad):
    plain, inverse = norm_plain(lat[...])
    arrived = work[...]
    gain_grad[...] = jnp.sum(arrived * plain, axis=0, keepdims=True)
    return base[...] + norm_back(arrived * gain[l : l + 1, :], plain, inverse)


def ffn_back_stage(l, nf, base, halves, gain, lat, slope, up, down, after):
    rows, width = base.shape
    hidden = up.shape[2]
    step = 256
    half = shape((rows // 2, width))
    return pl.pallas_call(
        skip(functools.partial(ffn_back_kernel, l, step), 8, len(after)),
        in_specs=[VMEM] * 4 + [HBM] * 4 + [ANY] * len(after),
        out_specs=[VMEM] * 4 + [HBM],
        out_shape=[half, half, shape((rows // nf, width)), shape((1, width), f32), far((rows, width), f32)],
        scratch_shapes=[
            pltpu.VMEM((width, hidden), bf16),
            pltpu.VMEM((hidden, width), bf16),
            pltpu.VMEM((rows, hidden), bf16),
            pltpu.VMEM((rows, width), bf16),
            pltpu.SemaphoreType.DMA((2 * hidden // step + 3,)),
        ]
        + [pltpu.VMEM((rows, width), f32)] * 3,
        **settings(16, 6),
    )(base, *halves, gain, lat, slope, up, down, *after)


def attn_back_kernel(l, clips, nf, mine, other, gain, base_in, middle_in, heads_in, soft_in, wo, wq, wk, wv, *refs):
    frame_keys, frame_values = refs[:nf], refs[nf : 2 * nf]
    keep, send, gmid_out, gain_grad, gupd_out, grads_out, gscore_out = refs[2 * nf : 2 * nf + 7]
    wqs, wks, wvs, wos, ks, vs, work, middle, base, heads_s, grads_s, gupd_s, soft_s, score_s, sems = refs[2 * nf + 7 :]
    fetch = Fetch(sems)
    middle_copy, base_copy = fetch(middle_in, middle), fetch(base_in, base)
    wo_copy = fetch(wo.at[l], wos)
    heads_copy = fetch(heads_in, heads_s)
    value_copies, media_keys = fetch_keys(fetch, frame_values, vs, clips)
    soft_copies = [fetch(soft_in.at[c], soft_s.at[c]) for c in range(clips)]
    key_copies, _ = fetch_keys(fetch, frame_keys, ks, clips)
    waits = [fetch(wq.at[l], wqs), fetch(wk.at[l], wks), fetch(wv.at[l], wvs)]
    take_halves(work, None, mine, other)
    middle_copy.wait()
    base_copy.wait()
    gmid = latent_back(base, work, middle, gain, l, gain_grad)
    gmid_out[...] = gmid
    gupd = gmid.astype(bf16)
    gupd_s[...] = gupd
    stores = [fetch(gupd_s, gupd_out)]
    heads = wqs.shape[1] // HEAD_DIM
    rows = gupd.shape[0] // clips
    wo_copy.wait()
    gatt = dot_nt(gupd, wos[...]).astype(bf16)
    heads_copy.wait()
    gqs, gkls, gvls = [], [], []
    for c in range(clips):
        part = slice(c * rows, (c + 1) * rows)
        ks[c, media_keys:] = heads_s[1, part]
        vs[c, media_keys:] = heads_s[2, part]
        qs = spread(heads_s[0, part], heads)
        gs = spread(gatt[part], heads)
        for copy in value_copies[c]:
            copy.wait()
        gsoft = dot_nt(gs, vs[c])
        soft_copies[c].wait()
        soft = soft_s[c]
        soft32 = soft.astype(f32)
        delta = jnp.sum(soft32 * gsoft, axis=-1, keepdims=True)
        gscore = (soft32 * (gsoft - delta)).astype(bf16)
        score_s[c] = gscore
        stores.append(fetch(score_s.at[c], gscore_out.at[c]))
        for copy in key_copies[c]:
            copy.wait()
        gqs.append(gathered(dot(gscore, ks[c]), heads) * SCALING)
        gkls.append(dot_tn(gscore[:, media_keys:], qs) * SCALING)
        gvls.append(dot_tn(soft[:, media_keys:], gs))
    gq = jnp.concatenate(gqs, axis=0).astype(bf16)
    gkl = jnp.concatenate(gkls, axis=0).astype(bf16)
    gvl = jnp.concatenate(gvls, axis=0).astype(bf16)
    grads_s[0] = gatt
    grads_s[1] = gq
    grads_s[2] = gkl
    grads_s[3] = gvl
    stores.append(fetch(grads_s, grads_out))
    for copy in waits:
        copy.wait()
    put_halves(dot_nt(gq, wqs[...]) + dot_nt(gkl, wks[...]) + dot_nt(gvl, wvs[...]), keep, send)
    for copy in stores:
        copy.wait()


def attn_back_stage(l, clips, base, halves, gain, middle, heads_all, soft, wo, wq, wk, wv, keys, values, after):
    rows, width = base.shape
    own = wq.shape[2]
    outs = [
        shape((rows // 2, width)),
        shape((rows // 2, width)),
        shape((rows, width), f32),
        shape((1, width), f32),
        far((rows, width)),
        far((4, rows, own)),
        far(soft.shape),
    ]
    nkeys = soft.shape[2]
    return pl.pallas_call(
        skip(functools.partial(attn_back_kernel, l, clips, len(keys)), 11 + 2 * len(keys), len(after)),
        in_specs=[VMEM] * 3 + [HBM] * (8 + 2 * len(keys)) + [ANY] * len(after),
        out_specs=[VMEM] * 4 + [HBM] * 3,
        out_shape=outs,
        scratch_shapes=[pltpu.VMEM((width, own), bf16)] * 3
        + [pltpu.VMEM((own, width), bf16)]
        + [pltpu.VMEM((clips, nkeys, own), bf16)] * 2
        + [pltpu.VMEM((rows, width), f32)] * 3
        + [pltpu.VMEM((4, rows, own), bf16)] * 2
        + [pltpu.VMEM((rows, width), bf16)]
        + [pltpu.VMEM(soft.shape, bf16)] * 2
        + [pltpu.SemaphoreType.DMA((9 + 2 * clips + 2 * clips * len(keys),))],
        **settings(25, 7),
    )(*halves, gain, base, middle, heads_all, soft, wo, wq, wk, wv, *keys, *values, *after)


def last_kernel(l, base, mine, other, lat, gain, *refs):
    grad, gain_grad, work = refs[-3:]
    take_halves(work, None, mine, other)
    grad[...] = latent_back(base, work, lat, gain, l, gain_grad)


def last_stage(base, halves, lat, gain, after):
    rows, width = base.shape
    return pl.pallas_call(
        functools.partial(last_kernel, 0),
        in_specs=[VMEM] * 5 + [ANY] * len(after),
        out_specs=[VMEM] * 2,
        out_shape=[shape((rows, width), f32), shape((1, width), f32)],
        scratch_shapes=[pltpu.VMEM((rows, width), f32)],
        **settings(12, 2),
    )(base, *halves, lat, gain, *after)


def out_kernel(base, mine, other, living, dest):
    take_halves(dest, base, mine, other)
    dest[...] = dest[...] * living[...]


def out_stage(base, halves, living):
    return pl.pallas_call(
        out_kernel,
        in_specs=[VMEM] * 4,
        out_specs=VMEM,
        out_shape=shape(base.shape, f32),
        **settings(8, 1),
    )(base, *halves, living)


def proj_kernel(clips, cut, nf, lead, *refs):
    plains = refs[:nf]
    lat_n, gupd, wk, wv, gain, gscore, soft, heads_all, grads = refs[nf : nf + 9]
    media_gain, qs, gs = refs[-3:]
    outs = refs[nf + 9 : -3] if lead == 4 else refs[-5:-3]
    out, out_last = outs[-1] if lead == 4 else outs[0], outs[-1]
    _, total, own = heads_all.shape
    heads = own // HEAD_DIM
    rows = total // clips
    wide = heads * rows

    @pl.when(pl.program_id(0) == 0)
    def _():
        for c in range(clips):
            part = slice(c * rows, (c + 1) * rows)
            qs[c * wide : (c + 1) * wide] = (spread(heads_all[0, part], heads).astype(f32) * SCALING).astype(bf16)
            gs[c * wide : (c + 1) * wide] = spread(grads[0, part], heads)

    scale = gain[...]
    zs, ys = [], []
    for c in range(clips):
        z = y = None
        at = 0
        for plain in plains:
            patches = plain.shape[0] // clips
            block = plain[c * patches : (c + 1) * patches]
            part_z = dot(gscore[c, :, at : at + patches], block)
            part_y = dot(soft[c, :, at : at + patches], block)
            z = part_z if z is None else z + part_z
            y = part_y if y is None else y + part_y
            at += patches
        zs.append((z * scale).astype(bf16))
        ys.append((y * scale).astype(bf16))
    kg = dot_tn(jnp.concatenate(zs, axis=0), qs[...])
    vg = dot_tn(jnp.concatenate(ys, axis=0), gs[...])
    along = kg * wk[0].astype(f32) + vg * wv[0].astype(f32)
    along = jnp.broadcast_to(jnp.sum(along, axis=1, keepdims=True), (along.shape[0], 128))
    media_gain[...] = jnp.transpose(along)[:1] / scale
    lat_b = lat_n[...]
    kg = (kg + dot_tn(lat_b, grads[2])).astype(bf16)
    vg = (vg + dot_tn(lat_b, grads[3])).astype(bf16)
    qg = dot_tn(lat_b, grads[1]).astype(bf16)
    og = dot_tn(gupd[...], heads_all[3]).astype(bf16)
    for b in range(kg.shape[0] // cut):
        for n, grad in enumerate((kg, vg, qg, og)):
            dest = (out, n) if n < lead else (out_last, n - lead)
            dest[0][b, dest[1]] = grad[b * cut : (b + 1) * cut]


def proj_stage(l, lead, clips, nc, plains, lat_n, gupd, wk, wv, gain, gscore, soft, heads_all, grads, after):
    width = lat_n.shape[1]
    _, rows, own = heads_all.shape
    cut = width // nc
    block = 384
    per = block // cut
    heads = own // HEAD_DIM
    wide = heads * rows
    full = lambda v: fixed(v.shape)
    columns = lambda v: pl.BlockSpec(v.shape[:-1] + (block,), lambda i: (0,) * (v.ndim - 1) + (i,))
    weight = pl.BlockSpec((1, block, own), lambda i: (l, i, 0))
    return pl.pallas_call(
        functools.partial(proj_kernel, clips, cut, len(plains), lead),
        grid=(width // block,),
        in_specs=[columns(v) for v in plains]
        + [columns(lat_n), columns(gupd), weight, weight, columns(gain)]
        + [full(v) for v in (gscore, soft, heads_all, grads)]
        + [ANY] * len(after),
        out_specs=[pl.BlockSpec((per, n, cut, own), lambda i: (i, 0, 0, 0)) for n in (lead, 4 - lead) if n]
        + [pl.BlockSpec((1, block), lambda i: (0, i))],
        out_shape=[shape((nc, n, cut, own)) for n in (lead, 4 - lead) if n] + [shape((1, width), f32)],
        scratch_shapes=[pltpu.VMEM((wide, own), bf16)] * 2,
        **settings(22, 12),
    )(*plains, lat_n, gupd, wk, wv, gain, gscore, soft, heads_all, grads, *after)


def media_back_kernel(frames, *refs):
    count = 2 * LAYERS
    tables, firsts, weights = refs[:count], refs[count : 2 * count], refs[2 * count : 2 * count + 2]
    out, sums, stack = refs[-3:]
    norms = refs[2 * count + 2 : 2 * count + 2 + 2 * frames]

    @pl.when(pl.program_id(1) == 0)
    def _():
        own = weights[0].shape[2]
        heads = own // HEAD_DIM
        for n in range(count):
            l = n // 2
            v = firsts[n][0]
            if n % 2 == 0:
                v = (v.astype(f32) * SCALING).astype(bf16)
            across = dot_nt(spread(v, heads), weights[n % 2][l])
            rows = across.shape[0]
            stack[n * rows : (n + 1) * rows] = across.astype(bf16)

    left = jnp.concatenate([t[0] for t in tables], axis=0)
    u = dot_tn(left, stack[...])
    out[0] = u.astype(bf16)
    mean = jnp.mean(u, axis=-1, keepdims=True)
    for n in range(frames):

        @pl.when(pl.program_id(1) == n)
        def _():
            plain, inverse = norms[2 * n][...].astype(f32), norms[2 * n + 1][:, :1]
            along = jnp.mean(u * plain, axis=-1, keepdims=True)
            sums[0, 0] = jnp.sum(inverse * (u - mean - plain * along), axis=0, keepdims=True)


def media_back_stage(first_frame, frames, clips, patches, tables, firsts, wk, wv, ready, after):
    width = wk.shape[1]
    table = pl.BlockSpec((1, tables[0].shape[1], patches), lambda c, r: (c, 0, first_frame + r))
    _, rows, own = firsts[0].shape
    piece = pl.BlockSpec((1, rows // clips, own), lambda c, r: (0, c, 0))
    full = lambda v: fixed(v.shape)
    norms = [hbm(v) for made in ready for v in made[:2]]
    norm_piece = lambda v: pl.BlockSpec((patches, v.shape[1]), lambda c, r: (c, 0))
    return pl.pallas_call(
        functools.partial(media_back_kernel, frames),
        grid=(clips, frames),
        in_specs=[table] * 4 + [piece] * 4 + [full(wk), full(wv)] + [norm_piece(v) for v in norms] + [ANY] * len(after),
        out_specs=[
            pl.BlockSpec((1, patches, width), lambda c, r: (r, c, 0)),
            pl.BlockSpec((1, 1, 1, width), lambda c, r: (r, c, 0, 0)),
        ],
        out_shape=[shape((frames, clips * patches, width)), shape((frames, clips, 1, width), f32)],
        scratch_shapes=[pltpu.VMEM((4 * tables[0].shape[1], width), bf16)],
        **settings(28, 9),
    )(*tables, *firsts, wk, wv, *norms, *after)


def media_last_kernel(count, media, stamp, *refs):
    parts, out = refs[:count], refs[-1]
    plain, inverse = norm_plain(media[...].astype(f32) + stamp[0])
    u = parts[0][...].astype(f32)
    for part in parts[1:]:
        u = u + part[...].astype(f32)
    out[...] = norm_back(u, plain, inverse)


def media_last_stage(media, stamp, parts, clips, after):
    rows, width = media.shape
    step = 128
    per = rows // clips // step
    piece = pl.BlockSpec((step, width), lambda i: (i, 0))
    clip = pl.BlockSpec((1, 1, width), lambda i: (i // per, 0, 0))
    return pl.pallas_call(
        functools.partial(media_last_kernel, len(parts)),
        grid=(rows // step,),
        in_specs=[piece, clip] + [piece] * len(parts) + [ANY] * len(after),
        out_specs=piece,
        out_shape=shape((rows, width), f32),
        **settings(20, 5),
    )(media, stamp, *parts, *after)


def own_columns(dest, src, nc):
    cut = dest.shape[1]
    block = 384
    at = lax.axis_index("clip") * cut
    wide = src[:, :, pl.ds(pl.multiple_of(at // block * block, block), block)].reshape(-1, block)
    for n in range(block // cut):

        @pl.when(lax.rem(at, block) == n * cut)
        def _():
            dest[...] = wide[:, n * cut : (n + 1) * cut]


def fetch_rows(fetch, refs, at, dest, chunk):
    each, rows, _ = dest.shape
    copies = []
    if len(refs) > 1:
        count = rows // len(refs)
        for r, ref in enumerate(refs):
            place = pl.ds(pl.multiple_of((lax.axis_index("frame") ^ r) * count, count), count)
            copies.append(fetch(ref.at[pl.ds(chunk * each, each)], dest.at[:, place]))
    else:
        nf = lax.axis_size("frame")
        count = rows // nf
        for c in range(each):
            for f in range(nf):
                source = refs[0].at[(chunk * each + c) * nf + f, pl.ds(at * count, count)]
                copies.append(fetch(source, dest.at[c, pl.ds(f * count, count)]))
    return copies


def ffn_grad_kernel(counts, shares, nc, *refs):
    rows_refs, grads_refs = refs[: counts[0]], refs[counts[0] : sum(counts)]
    up, down = refs[sum(counts) : sum(counts) + 2]
    up_grad, down_grad, rows_all, grads_all, rows_own, grads_own, sems = refs[-7:]
    chunk = pl.program_id(1)
    flat = lambda ref: ref[...].reshape(-1, ref.shape[2])

    @pl.when(jnp.logical_or(pl.program_id(0) == 0, pl.num_programs(1) > 1))
    def _():
        fetch = Fetch(sems)
        copies = fetch_rows(fetch, rows_refs, shares[0], rows_all, chunk)
        copies += fetch_rows(fetch, grads_refs, shares[1], grads_all, chunk)
        for copy in copies:
            copy.wait()
        own_columns(rows_own, rows_all, nc)
        own_columns(grads_own, grads_all, nc)

    step = up.shape[2]
    width = min(step, 256)
    halves = [slice(n, n + width) for n in range(0, step, width)]
    pres = [dot(flat(rows_all), up[0, :, b]) for b in halves]
    ghs = [dot_nt(flat(grads_all), down[0, b, :]) for b in halves]
    for n, b in enumerate(halves):
        hidden, slope = gelu_parts(pres[n])
        gpre = (slope * ghs[n]).astype(bf16)
        up_part = dot_tn(rows_own[...], gpre)
        down_part = dot_tn(grads_own[...], hidden.astype(bf16))

        @pl.when(chunk == 0)
        def _():
            up_grad[0, :, b] = up_part
            down_grad[0, :, b] = down_part

        @pl.when(chunk > 0)
        def _():
            up_grad[0, :, b] += up_part
            down_grad[0, :, b] += down_part


def ffn_grad_stage(l, nc, count, rows, grads, shares, up, down, earlier, after):
    width = rows[0].shape[2]
    cut = width // nc
    hidden = up.shape[2]
    step = 512 if hidden % 512 == 0 else 256
    each = min(nc, 1024 // count)
    outs = [shape((LAYERS, cut, hidden), f32)] * 2
    arrays = [hbm(v) for v in list(rows) + list(grads)]
    known = len(arrays) + 2
    return pl.pallas_call(
        functools.partial(ffn_grad_kernel, (len(rows), len(grads)), shares, nc),
        grid=(hidden // step, nc // each),
        in_specs=[HBM] * len(arrays)
        + [
            pl.BlockSpec((1, width, step), lambda j, i: (l, 0, j)),
            pl.BlockSpec((1, step, width), lambda j, i: (l, j, 0)),
        ]
        + [ANY] * (len(earlier) + len(after)),
        out_specs=[
            pl.BlockSpec((1, cut, step), lambda j, i: (l, 0, j)),
            pl.BlockSpec((1, cut, step), lambda j, i: (l, 0, j)),
        ],
        out_shape=outs,
        input_output_aliases={known: 0, known + 1: 1} if earlier else {},
        scratch_shapes=[pltpu.VMEM((each, count, width), bf16)] * 2
        + [pltpu.VMEM((each * count, cut), bf16)] * 2
        + [pltpu.SemaphoreType.DMA((2 * each * lax.axis_size("frame"),))],
        **settings(40, 14),
    )(*arrays, up, down, *earlier, *after)


def swap(v, axis, bit):
    size = lax.axis_size(axis)
    return lax.ppermute(v, axis, [(i, i ^ bit) for i in range(size)])


def bits_of(size):
    out, bit = [], 1
    while bit < size:
        out.append(bit)
        bit *= 2
    return out


def add_kernel(mine, arrived, *refs):
    refs[-1][...] = (mine[...].astype(f32) + arrived[...].astype(f32)).astype(bf16)


def add_after(mine, arrived, after):
    return pl.pallas_call(
        add_kernel,
        in_specs=[VMEM] * 2 + [ANY] * len(after),
        out_specs=VMEM,
        out_shape=shape(mine.shape),
        **settings(4, 1),
    )(mine, arrived, *after)


def frame_sum(keep, send, fill=None):
    mine = (keep.astype(f32) + swap(send, "frame", 1).astype(f32)).astype(bf16)
    made = None
    for bit in bits_of(lax.axis_size("frame"))[1:]:
        arrived = swap(mine, "frame", bit)
        if fill is not None and made is None:
            made = fill((mine,))
            mine = add_after(mine, arrived, made)
        else:
            mine = (mine.astype(f32) + arrived.astype(f32)).astype(bf16)
    return (mine, swap(mine, "frame", 1)) if fill is None else ((mine, swap(mine, "frame", 1)), made)


class Scatter:
    def __init__(self, parts, bits, clip_here):
        self.pieces = [parts.reshape((2,) * len(bits) + parts.shape[1:])]
        self.bits, self.left, self.clip_here = list(bits), sorted(bits, reverse=True), clip_here

    def send(self):
        bit = self.bits.pop(0)
        axis = self.left.index(bit)
        self.left.remove(bit)
        mine = (self.clip_here // bit) % 2
        pick = lambda v, n: lax.dynamic_index_in_dim(v, n, axis, keepdims=False)
        self.sent = sum(pick(v, 1 - mine).astype(f32) for v in self.pieces).astype(bf16)
        self.pieces = [pick(v, mine) for v in self.pieces]
        self.arriving = swap(self.sent, "clip", bit)
        return self

    def step(self, after):
        if self.arriving is None:
            return
        self.pieces.append(tie(self.arriving, after) if after else self.arriving)
        self.arriving = None
        if self.bits:
            self.send()

    @property
    def total(self):
        return sum(v.astype(f32) for v in self.pieces)


def gather_rows(shares):
    return lax.all_gather(jnp.concatenate(shares, axis=0), ("clip", "frame"), axis=0)


def exchange_rows(share, nc):
    return lax.all_to_all(jnp.broadcast_to(share, (nc,) + share.shape), "clip", 0, 0, tiled=True)


def spread_rows(mine, first_gate, second_gate):
    pieces = {0: tie(mine, first_gate)}
    for bit in bits_of(lax.axis_size("frame"))[::-1]:
        for r in list(pieces):
            arrived = swap(pieces[r], "frame", bit)
            pieces[r | bit] = tie(arrived, second_gate) if bit > 1 else arrived
    return [pieces[r] for r in range(len(pieces))]


def on_device(
    media, frame_order, clip_counts, latents, time_embed, media_gain, latent_gain, ffn_gain,
    query_weight, key_weight, value_weight, out_weight, up_weight, down_weight, cotangent,
):
    clips, _, patches, width = media.shape
    lat_rows = latents.shape[1]
    nf = lax.axis_size("frame")
    nc = lax.axis_size("clip")
    frame_here = lax.axis_index("frame")
    clip_here = lax.axis_index("clip")
    rows = clips * lat_rows

    key_plain, value_plain = key_weight, value_weight
    query_weight, key_weight, value_weight, out_weight, up_weight, down_weight = (
        pltpu.with_memory_space_constraint(w, pltpu.HBM)
        for w in (query_weight, key_weight, value_weight, out_weight, up_weight, down_weight)
    )
    clip_ids = clip_here * clips + jnp.arange(clips, dtype=jnp.int32)
    owner_match = (clip_ids // SLOTS)[:, None] == jnp.arange(clip_counts.shape[0], dtype=jnp.int32)[None, :]
    owner_count = jnp.sum(jnp.where(owner_match, clip_counts[None, :], 0), axis=1)
    living = (clip_ids % SLOTS < owner_count).astype(f32)
    living = jnp.repeat(living, lat_rows)[:, None]

    flat = media.reshape(clips * patches, width)
    top = nf // 2
    frames = {0: flat}
    if top > 1:
        frames[top] = swap(flat, "frame", top)
    for bit in bits_of(top)[::-1]:
        for r in [r for r in frames if r < top]:
            frames[r | bit] = swap(frames[r], "frame", bit)
    times = jnp.arange(nf, dtype=jnp.int32)
    order = jnp.stack(
        [lax.dynamic_index_in_dim(frame_order, frame_here ^ r, 1, keepdims=False) for r in range(nf)]
    )
    onehot = (order[:, :, None] == times).astype(f32)
    stamps = jnp.sum(onehot[..., None] * time_embed, axis=2)[:, :, None, :]
    wide_k = (media_gain[:, :, None] * key_plain.astype(f32)).astype(bf16)
    wide_v = (media_gain[:, :, None] * value_plain.astype(f32)).astype(bf16)
    ready = [media_stage(frames[r], stamps[r], wide_k, wide_v, clips) for r in range(top)]
    last = LAYERS - 1
    grad, top_share, gh = top_stage(nf, cotangent.reshape(rows, width), living, down_weight)
    frames[top] = tie(frames[top], [made[0] for made in ready] + [gh])
    for bit in bits_of(top)[::-1]:
        for r in [r for r in frames if r >= top]:
            frames[r | bit] = swap(frames[r], "frame", bit)
    ready += [media_stage(frames[r], stamps[r], wide_k, wide_v, clips) for r in range(top, nf)]
    plains = [hbm(g[0]) for g in ready]

    stored, ffn_shares = [], []
    current, halves = latents.reshape(rows, width), None
    for l in range(LAYERS):
        keys = [hbm(g[2 + 2 * l]) for g in ready]
        values = [hbm(g[3 + 2 * l]) for g in ready]
        out = attn_stage(
            l, clips, current, halves, latent_gain, query_weight, key_weight, value_weight, out_weight, keys, values, ()
        )
        keep, send, lat_n, heads_all, soft = out[:5]
        lat, lat_far = (current, None) if halves is None else (out[5], hbm(out[6]))
        halves = frame_sum(keep, send)
        gh_here = (hbm(gh),) if l == last else ()
        out = ffn_stage(l, nf, lat, halves, ffn_gain, up_weight, down_weight, gh_here, ())
        keep, send, current, share, middle = out[:5]
        ffn_shares.append(share)
        if l < last:
            slope = out[5]
        else:
            slope, (keep_back, send_back) = middle, out[5:]
            early = gather_rows(ffn_shares + [top_share])
        halves = frame_sum(keep, send) if l < last else None
        stored.append((keys, values, lat_far, hbm(lat_n), hbm(heads_all), hbm(soft), hbm(middle), hbm(slope)))
    forward_keep, forward_send = keep, send
    lat_gain_grads, ffn_gain_grads, media_gain_grads = [None] * LAYERS, [None] * LAYERS, [None] * LAYERS
    projs, tables, firsts = [None] * LAYERS, [None] * LAYERS, [None] * LAYERS

    def attend_back(l, grad, halves, lead, before, between):
        keys, values, _, lat_n, heads_all, soft, middle, _ = stored[l]
        keep, send, gmid, ffn_gain_grads[l], gupd, grads, gscore = attn_back_stage(
            l, clips, hbm(grad), halves, ffn_gain, middle, heads_all, soft, out_weight, query_weight, key_weight,
            value_weight, keys, values, before,
        )
        gupd, grads, gscore = hbm(gupd), hbm(grads), hbm(gscore)
        tables[l], firsts[l] = (gscore, soft), (heads_all, grads)

        def projections(after):
            return proj_stage(
                l, lead, clips, nc, plains, lat_n, gupd, key_weight, value_weight, media_gain[l : l + 1], gscore, soft,
                heads_all, grads, after + between,
            )

        halves, (*projs[l], along) = frame_sum(keep, send, projections)
        media_gain_grads[l] = along
        return gmid, halves

    def scattered(l):
        bits = bits_of(nc)
        orders = (bits, bits[1:] + bits[:1])
        return [Scatter(v, order, clip_here).send() for v, order in zip(projs[l], orders)]

    back_halves = frame_sum(keep_back, send_back)
    gmid, halves = attend_back(1, grad, back_halves, 3, (), ())
    upper = scattered(1)
    keep, send, share, lat_gain_grads[1], grad = ffn_back_stage(
        0, nf, gmid, halves, latent_gain, stored[1][2], stored[0][7], up_weight, down_weight, (),
    )
    lower_grads = exchange_rows(share, nc)
    halves = frame_sum(keep, send)
    gmid, halves = attend_back(0, grad, halves, 3, (), ())
    lower = scattered(0)
    forward = frame_sum(tie(forward_keep, (gmid,)), tie(forward_send, (gmid,)))
    latents_out = out_stage(current, forward, living)


    half = nf // 2
    tables = [t for pair in tables for t in pair]
    firsts = [t for pair in firsts for t in pair]
    u = {}
    part, far_sums = media_back_stage(
        half, half, clips, patches, tables, firsts, wide_k, wide_v, ready[half:], (lower[0].sent, lower[1].sent)
    )
    for r in range(half):
        u[half + r] = [part[r]]
    for part_sum in upper:
        part_sum.step((part,))
    gate = tuple(part_sum.sent for part_sum in upper)
    latents_grad, lat_gain_grads[0] = last_stage(gmid, halves, latents.reshape(rows, width), latent_gain, gate)
    merged = lambda v: v[0] if len(v) == 1 else sum(x.astype(f32) for x in v).astype(bf16)

    def fold(bits, least):
        for bit in bits:
            for r in [r for r in u if r & bit and r >= least]:
                u[r ^ bit].append(swap(merged(u.pop(r)), "frame", bit))

    fold(bits_of(half), half)
    sent = merged(u.pop(half))
    lower_mine = tie(lower_grads, (far_sums,))
    arrived = swap(sent, "frame", half)
    part, near_sums = media_back_stage(
        0, half, clips, patches, tables, firsts, wide_k, wide_v, ready[:half], (sent, latents_grad, lower_mine)
    )
    for r in range(half):
        u[r] = [part[r]]
    fold(bits_of(half), 0)
    gate = (part,)
    ffn_parts = ffn_grad_stage(1, nc, rows, (early,), (early,), (1, 2), up_weight, down_weight, (), gate)
    gate = (ffn_parts[0],)
    for part_sum in upper + lower:
        part_sum.step(gate)
    lower_grads = spread_rows(lower_mine, (near_sums,), (ffn_parts[0],))
    up_grad, down_grad = ffn_grad_stage(
        0, nc, rows, (early,), lower_grads, (0, 0), up_weight, down_weight, ffn_parts,
        (lower[0].sent, lower[1].sent, upper[0].sent, upper[1].sent),
    )
    gate = (up_grad,)
    for part_sum in lower + upper:
        part_sum.step(gate)
    media_grad = media_last_stage(
        flat, stamps[0], u[0] + [tie(arrived, gate)], clips,
        (lower[0].sent, lower[1].sent),
    )
    for part_sum in upper + lower:
        part_sum.step((media_grad,))
    for scatter in upper + lower:
        while scatter.arriving is not None:
            scatter.step(())
    sums = jnp.concatenate([near_sums, far_sums], axis=0)
    time_part = jnp.einsum("rct,rcd->td", onehot, sums[:, :, 0], precision=lax.Precision.HIGHEST)

    n_all = nc * nf
    narrow = jnp.concatenate([time_part] + media_gain_grads, axis=0)
    narrow = narrow.reshape(nf + 2, n_all, width // n_all).transpose(1, 0, 2).reshape(n_all, -1)
    broad = jnp.concatenate(lat_gain_grads + ffn_gain_grads, axis=0)
    broad = broad.reshape(4, nc, width // nc).transpose(1, 0, 2).reshape(nc, 1, -1)
    broad = jnp.broadcast_to(broad * (1.0 / nf), (nc, nf, broad.shape[2]))
    packed = tie(jnp.concatenate([narrow, broad.reshape(n_all, -1)], axis=1), (ffn_parts[0],))
    packed = jnp.sum(lax.all_to_all(packed, ("clip", "frame"), 0, 0, tiled=True), axis=0)
    edge = (nf + 2) * (width // n_all)
    narrow = packed[:edge].reshape(nf + 2, -1)
    broad = packed[edge:].reshape(4, -1)

    totals = [jnp.concatenate([part.total for part in pair], axis=0) for pair in (lower, upper)]
    pick = lambda n: jnp.stack([total[n] for total in totals])
    return (
        latents_out.reshape(latents.shape),
        media_grad.reshape(media.shape),
        latents_grad.reshape(latents.shape),
        narrow[:nf],
        narrow[nf:],
        broad[:2],
        broad[2:],
        pick(2),
        pick(0),
        pick(1),
        jnp.swapaxes(pick(3), 1, 2),
        up_grad,
        jnp.swapaxes(down_grad, 1, 2),
    )


def solution(mesh):
    return jax.shard_map(
        on_device,
        mesh=mesh,
        in_specs=(
            P("clip", "frame", None, None),
            P("clip", None),
            P(),
            P("clip", None, None),
            P(),
            P(),
            P(),
            P(),
            P(None, None, "frame"),
            P(None, None, "frame"),
            P(None, None, "frame"),
            P(None, "frame", None),
            P(None, None, "frame"),
            P(None, "frame", None),
            P("clip", None, None),
        ),
        out_specs=(
            P("clip", None, None),
            P("clip", "frame", None, None),
            P("clip", None, None),
            P(None, ("clip", "frame")),
            P(None, ("clip", "frame")),
            P(None, "clip"),
            P(None, "clip"),
            P(None, "clip", "frame"),
            P(None, "clip", "frame"),
            P(None, "clip", "frame"),
            P(None, "frame", "clip"),
            P(None, "clip", "frame"),
            P(None, "frame", "clip"),
        ),
        check_vma=False,
    )
```
